32 devices in a mesh: dp: 8 (over z, y), chan: 4 (over x, core).
Axes of the slice: x: 2, y: 2, z: 4, core: 2. Of those that a mesh axis runs over, the one named last changes fastest.
Arguments:
- inputs: bfloat16 [262144, 256], P(('dp', 'chan')), may hold values from -6 to 6
- valid_mask: int32 [262144], P('dp'), may hold values from 0 to 1, as said below
- code_ids: int32 [262144], P(('dp', 'chan')), may hold values from 0 to 511
- cotangent: bfloat16 [262144, 256], P(('dp', 'chan')), may hold values from -6 to 6
- conv_weight: float32 [9, 256, 256], P(None, 'dp', 'chan'), may hold values from -0.125 to 0.125
- conv_first: float32 [9, 256, 256], P(None, 'dp', 'chan'), may hold values from -1024 to 1024
- conv_second: float32 [9, 256, 256], P(None, 'dp', 'chan'), may hold values from 26869.76 to 107479.04
- point_weight: float32 [256, 256], P('chan', 'dp'), may hold values from -0.375 to 0.375
- point_first: float32 [256, 256], P('chan', 'dp'), may hold values from -1024 to 1024
- point_second: float32 [256, 256], P('chan', 'dp'), may hold values from 26869.76 to 107479.04
- proj_weight: float32 [256, 64], P(('dp', 'chan')), may hold values from -0.375 to 0.375
- proj_first: float32 [256, 64], P(('dp', 'chan')), may hold values from -4096 to 4096
- proj_second: float32 [256, 64], P(('dp', 'chan')), may hold values from 568852.5 to 2275410
- code_book: float32 [512, 64], P(('dp', 'chan')), may hold values from -6 to 6
- code_first: float32 [512, 64], P(('dp', 'chan')), may hold values from -2560 to 2560
- code_second: float32 [512, 64], P(('dp', 'chan')), may hold values from 175636.48 to 705167.4
- dec_weight: float32 [256, 64], P(('dp', 'chan')), may hold values from -0.75 to 0.75
- dec_first: float32 [256, 64], P(('dp', 'chan')), may hold values from -2048 to 2048
- dec_second: float32 [256, 64], P(('dp', 'chan')), may hold values from 107479.04 to 429916.16
Outputs:
- output: bfloat16 [262144, 256], P(('dp', 'chan'))
- input_grad: bfloat16 [262144, 256], P(('dp', 'chan'))
- losses: float32 [2], replicated
- conv_new: float32 [9, 256, 256], P(None, 'dp', 'chan')
- conv_first_new: float32 [9, 256, 256], P(None, 'dp', 'chan')
- conv_second_new: float32 [9, 256, 256], P(None, 'dp', 'chan')
- conv_copy: bfloat16 [9, 256, 256], P(None, 'dp', 'chan')
- point_new: float32 [256, 256], P('chan', 'dp')
- point_first_new: float32 [256, 256], P('chan', 'dp')
- point_second_new: float32 [256, 256], P('chan', 'dp')
- point_copy: bfloat16 [256, 256], P('chan', 'dp')
- proj_new: float32 [256, 64], P(('dp', 'chan'))
- proj_first_new: float32 [256, 64], P(('dp', 'chan'))
- proj_second_new: float32 [256, 64], P(('dp', 'chan'))
- proj_copy: bfloat16 [256, 64], P(('dp', 'chan'))
- code_new: float32 [512, 64], P(('dp', 'chan'))
- code_first_new: float32 [512, 64], P(('dp', 'chan'))
- code_second_new: float32 [512, 64], P(('dp', 'chan'))
- code_copy: bfloat16 [512, 64], P(('dp', 'chan'))
- dec_new: float32 [256, 64], P(('dp', 'chan'))
- dec_first_new: float32 [256, 64], P(('dp', 'chan'))
- dec_second_new: float32 [256, 64], P(('dp', 'chan'))
- dec_copy: bfloat16 [256, 64], P(('dp', 'chan'))
The draws below stay inside these ranges and needn't reach their ends.
Inputs may be any that keep to these rules, and one draw needn't show every extreme that they name: The canvas of each index of dp holds 2 tiles of 128 x 128 pixels side by side (tile b covers columns b * 128 to (b + 1) * 128 - 1). In each index of dp one tile, drawn from the seed, holds one image in its top left corner that is 112 rows tall and between 16 and 112 columns wide. Every other tile holds one square image of side s in its top left corner or, where s < 64, four of side s at row and column offsets 0 and 64, with s between 16 and 112. valid_mask is 1 on the images' pixels.
All inputs are finite; a program needn't handle non-finite values.
Results may differ from the reference program's by a relative error of at most 0.0044.
The reference program's roundings to bfloat16 on the way count: a program that leaves them out, or rounds other values in their place, can miss the bound.
Values may be sent and summed in bfloat16 or wider, within the bound.
A program may use at most 256 MiB of HBM per device.

```python
import math
import jax
import jax.numpy as jnp
from jax import lax

C = 256
LAT = 64
K = 512
BAND = 128
BANDS = 2
STEP = 5
PIX_DEV = 32768
PIXELS = 262144
N_DP = 8


def draw_valid_mask(key, part):
    key = jax.random.fold_in(key, 11)
    side_key = jax.random.fold_in(key, 1)
    slot_key = jax.random.fold_in(key, 2)
    width_key = jax.random.fold_in(key, 3)
    tiles = N_DP * BANDS
    sides = jax.random.randint(side_key, (tiles,), BAND // 8, 7 * BAND // 8 + 1)
    tall_slot = jax.random.randint(slot_key, (N_DP,), 0, BANDS)
    widths = jax.random.randint(width_key, (tiles,), BAND // 8, 7 * BAND // 8 + 1)
    position = jnp.arange(tiles, dtype=jnp.int32)
    is_tall = position % BANDS == jnp.repeat(tall_slot, BANDS)
    half_band = BAND // 2
    row_index = jnp.arange(BAND, dtype=jnp.int32)[None, :, None]
    col_index = jnp.arange(BAND, dtype=jnp.int32)[None, None, :]
    side_cube = sides[:, None, None]
    grid_mask = (row_index % half_band < side_cube) & (col_index % half_band < side_cube)
    single_mask = (row_index < side_cube) & (col_index < side_cube)
    square_mask = jnp.where(side_cube < half_band, grid_mask, single_mask)
    tall_mask = (row_index < 7 * BAND // 8) & (col_index < widths[:, None, None])
    tile_mask = jnp.where(is_tall[:, None, None], tall_mask, square_mask)
    laid = tile_mask.reshape(N_DP, BANDS, BAND, BAND).transpose(0, 2, 1, 3)
    return laid.astype(jnp.int32).reshape(PIXELS)


def touch_ends(entries, rng, least, largest):
    shape = entries.shape
    index_at = [jax.random.randint(jax.random.fold_in(rng, axis), (), 0, shape[axis]) for axis in range(len(shape))]
    entries = entries.at[tuple(index_at)].set(least)
    longest = shape.index(max(shape))
    index_at[longest] = (index_at[longest] + 1) % shape[longest]
    return entries.at[tuple(index_at)].set(largest)


def block_levels(stream_key, extent, cuts, smallest, top_value):
    def one(axis_at, blocks):
        steps = jax.random.uniform(jax.random.fold_in(jax.random.fold_in(stream_key, 6), axis_at), (blocks,), jnp.float32, smallest / len(cuts), top_value / len(cuts))
        return jnp.repeat(jnp.exp(steps), extent[axis_at] // blocks).reshape((-1,) + (1,) * (len(extent) - axis_at - 1))

    loudness = one(*cuts[0])
    for cut in cuts[1:]:
        loudness = loudness * one(*cut)
    return loudness


def bell_draw(key, extent, deviation, limit, pieces=(), kind=jnp.bfloat16):
    drawn = deviation * jax.random.normal(key, extent, jnp.float32)
    if pieces:
        drawn = drawn * block_levels(key, extent, pieces, -0.22, 0.18)
    return jnp.clip(drawn, -limit, limit).astype(kind)


def setup_inputs(seed: int = 0) -> dict:
    keys = jax.random.split(jax.random.key(seed), 20)
    inputs = bell_draw(keys[0], (PIXELS, C), 1.0, 6.0, ((0, 32),))
    valid_mask = draw_valid_mask(jax.random.fold_in(keys[19], 71), 0)
    code_ids = touch_ends(jax.random.randint(keys[2], (PIXELS,), 0, K), jax.random.fold_in(keys[2], 1), 0, K - 1).astype(jnp.int32)
    cotangent = bell_draw(keys[3], (PIXELS, C), 1.0, 6.0, ((0, 32),))
    conv_weight = bell_draw(keys[4], (9, C, C), (9 * C) ** -0.5, 0.125, ((1, 8), (2, 4)), jnp.float32)
    conv_first = bell_draw(keys[5], (9, C, C), (0.5 * (0.41 * PIXELS) ** 0.5), 1024.0, ((1, 8), (2, 4)), jnp.float32)
    conv_second = jnp.clip(jnp.exp(math.log(107479.04) - 1.3862944 * jax.random.uniform(keys[6], (9, C, C), jnp.float32) ** block_levels(keys[6], (9, C, C), ((1, 8), (2, 4)), -0.2, 0.2)), 26869.76, 107479.04)
    point_weight = bell_draw(keys[7], (C, C), C ** -0.5, 0.375, ((0, 4), (1, 8)), jnp.float32)
    point_first = bell_draw(keys[8], (C, C), (0.5 * (0.41 * PIXELS) ** 0.5), 1024.0, ((0, 4), (1, 8)), jnp.float32)
    point_second = jnp.clip(jnp.exp(math.log(107479.04) - 1.3862944 * jax.random.uniform(keys[9], (C, C), jnp.float32) ** block_levels(keys[9], (C, C), ((0, 4), (1, 8)), -0.2, 0.2)), 26869.76, 107479.04)
    proj_weight = bell_draw(keys[10], (C, LAT), C ** -0.5, 0.375, ((0, 32),), jnp.float32)
    proj_first = bell_draw(keys[11], (C, LAT), (2.3 * (0.41 * PIXELS) ** 0.5), 4096.0, ((0, 32),), jnp.float32)
    proj_second = jnp.clip(jnp.exp(math.log(2275410) - 1.3862944 * jax.random.uniform(keys[12], (C, LAT), jnp.float32) ** block_levels(keys[12], (C, LAT), ((0, 32),), -0.2, 0.2)), 568852.5, 2275410)
    code_book = bell_draw(keys[13], (K, LAT), 1.0, 6.0, ((0, 32),), jnp.float32)
    code_first = bell_draw(keys[14], (K, LAT), (0.82 * PIXELS / K), 2560.0, ((0, 32),), jnp.float32)
    code_second = jnp.clip(jnp.exp(math.log(705167.4) - 1.39001876 * jax.random.uniform(keys[15], (K, LAT), jnp.float32) ** block_levels(keys[15], (K, LAT), ((0, 32),), -0.2, 0.2)), 175636.48, 705167.4)
    dec_weight = bell_draw(keys[16], (C, LAT), LAT ** -0.5, 0.75, ((0, 32),), jnp.float32)
    dec_first = bell_draw(keys[17], (C, LAT), ((0.41 * PIXELS) ** 0.5), 2048.0, ((0, 32),), jnp.float32)
    dec_second = jnp.clip(jnp.exp(math.log(429916.16) - 1.3862944 * jax.random.uniform(keys[18], (C, LAT), jnp.float32) ** block_levels(keys[18], (C, LAT), ((0, 32),), -0.2, 0.2)), 107479.04, 429916.16)
    return dict(inputs=inputs, valid_mask=valid_mask, code_ids=code_ids, cotangent=cotangent, conv_weight=conv_weight, conv_first=conv_first, conv_second=conv_second, point_weight=point_weight, point_first=point_first, point_second=point_second, proj_weight=proj_weight, proj_first=proj_first, proj_second=proj_second, code_book=code_book, code_first=code_first, code_second=code_second, dec_weight=dec_weight, dec_first=dec_first, dec_second=dec_second)


@jax.custom_vjp
def low(v):
    return lax.optimization_barrier(v.astype(jnp.bfloat16)).astype(jnp.float32)

@jax.custom_vjp
def low_back(v):
    return v

def low_keep(v):
    return (low(v), None)

def low_pass(kept, grad):
    return (grad,)

def back_keep(v):
    return (v, None)

def back_low(kept, grad):
    return (low(grad),)
low.defvjp(low_keep, low_pass)
low_back.defvjp(back_keep, back_low)
beta_first = 0.5
beta_second = 0.5
epsilon = 1e-08
decay_rate = 0.01

def row_stride():
    return BANDS * BAND

def tap_offsets():
    stride = row_stride()
    return [row_step * stride + col_step for row_step in (-1, 0, 1) for col_step in (-1, 0, 1)]

def network(inputs_f, conv_w, point_w, proj_w, book_w, dec_w, fixed_latent, fixed_chosen, mask_f, code_ids):
    highest = lax.Precision.HIGHEST
    conv_low = low(conv_w)
    point_low = low(point_w)
    proj_low = low(proj_w)
    book_low = low(book_w)
    dec_low = low(dec_w)
    margin = row_stride() + 1

    def canvas(item):
        image_in, mask_in, codes_in, latent_in, chosen_in = item
        weights_in = mask_in[:, None]
        activations = jnp.maximum(image_in, 0.0) * weights_in
        padded = jnp.pad(activations, ((margin, margin), (0, 0)))
        hidden = jnp.zeros((PIX_DEV, C), jnp.float32)
        for tap_index, offset in enumerate(tap_offsets()):
            begin = margin + offset
            hidden = hidden + jnp.dot(padded[begin:begin + PIX_DEV], conv_low[tap_index], precision=highest)
        middle = low(low_back(jnp.maximum(hidden, 0.0)))
        branch = low_back(jnp.dot(middle, point_low, precision=highest))
        summed = low(image_in + branch)
        latent = low_back(jnp.dot(summed, proj_low, precision=highest))
        chosen = jnp.take(book_low, codes_in, axis=0)
        decoded = low(latent - latent_in + chosen_in)
        output = jnp.dot(decoded, dec_low.T, precision=highest) * weights_in
        gap_book = latent_in - chosen
        gap_commit = latent - chosen_in
        book_loss = jnp.sum(weights_in * gap_book * gap_book)
        commit_loss = 0.25 * jnp.sum(weights_in * gap_commit * gap_commit)
        return (output, book_loss, commit_loss, latent, chosen)
    mapped = lax.map(jax.checkpoint(canvas), (inputs_f.reshape(N_DP, PIX_DEV, C), mask_f.reshape(N_DP, PIX_DEV), code_ids.reshape(N_DP, PIX_DEV), fixed_latent.reshape(N_DP, PIX_DEV, LAT), fixed_chosen.reshape(N_DP, PIX_DEV, LAT)))
    return (mapped[0].reshape(PIXELS, C), jnp.sum(mapped[1]), jnp.sum(mapped[2]), mapped[3].reshape(PIXELS, LAT), mapped[4].reshape(PIXELS, LAT))

def adamw(grad, weight, first, second, rate):
    first_new = beta_first * first + (1.0 - beta_first) * grad
    second_new = beta_second * second + (1.0 - beta_second) * grad * grad
    first_hat = first_new / (1.0 - beta_first ** STEP)
    second_hat = second_new / (1.0 - beta_second ** STEP)
    weight_new = weight - rate * (first_hat / (jnp.sqrt(second_hat) + epsilon) + decay_rate * weight)
    return (weight_new, first_new, second_new, weight_new.astype(jnp.bfloat16))

def reference(inputs, valid_mask, code_ids, cotangent, conv_weight, conv_first, conv_second, point_weight, point_first, point_second, proj_weight, proj_first, proj_second, code_book, code_first, code_second, dec_weight, dec_first, dec_second):
    inputs_f = inputs.astype(jnp.float32)
    mask_f = valid_mask.astype(jnp.float32)
    zero_latent = jnp.zeros((PIXELS, LAT), jnp.float32)
    first_pass = network(inputs_f, conv_weight, point_weight, proj_weight, code_book, dec_weight, zero_latent, zero_latent, mask_f, code_ids)
    fixed_latent = first_pass[3]
    fixed_chosen = first_pass[4]

    def objective(image_f, conv_w, point_w, proj_w, book_w, dec_w):
        return network(image_f, conv_w, point_w, proj_w, book_w, dec_w, fixed_latent, fixed_chosen, mask_f, code_ids)
    primal, pullback = jax.vjp(objective, inputs_f, conv_weight, point_weight, proj_weight, code_book, dec_weight)
    unit = jnp.ones((), jnp.float32)
    grads = pullback((cotangent.astype(jnp.float32), unit, unit, jnp.zeros_like(fixed_latent), jnp.zeros_like(fixed_chosen)))
    count = jnp.sum(mask_f)
    losses = jnp.stack([primal[1], primal[2]]) / (count * LAT)
    conv_out = adamw(grads[1], conv_weight, conv_first, conv_second, 0.01)
    point_out = adamw(grads[2], point_weight, point_first, point_second, 0.03)
    proj_out = adamw(grads[3], proj_weight, proj_first, proj_second, 0.03)
    code_out = adamw(grads[4], code_book, code_first, code_second, 0.5)
    dec_out = adamw(grads[5], dec_weight, dec_first, dec_second, 0.06)
    return (primal[0].astype(jnp.bfloat16), grads[0].astype(jnp.bfloat16), losses, conv_out[0], conv_out[1], conv_out[2], conv_out[3], point_out[0], point_out[1], point_out[2], point_out[3], proj_out[0], proj_out[1], proj_out[2], proj_out[3], code_out[0], code_out[1], code_out[2], code_out[3], dec_out[0], dec_out[1], dec_out[2], dec_out[3])
```

```python
import functools

import jax
import jax.numpy as jnp
from jax import lax
from jax.experimental import pallas as pl
from jax.experimental.pallas import tpu as pltpu
from jax.sharding import PartitionSpec as P

LAT = 64
BAND = 128
BANDS = 2
STEP = 5
SIDE = BAND
PITCH = BANDS * SIDE
CHUNK_ROWS = 4
CHUNK = CHUNK_ROWS * PITCH
MESH = pl.DeviceIdType.MESH
F32 = jnp.float32
BF16 = jnp.bfloat16

beta_first = 0.5
beta_second = 0.5
epsilon = 1e-08
decay_rate = 0.01


def adamw(grad, weight, first, second, rate):
    first_new = beta_first * first + (1.0 - beta_first) * grad
    second_new = beta_second * second + (1.0 - beta_second) * grad * grad
    first_hat = first_new / (1.0 - beta_first**STEP)
    second_hat = second_new / (1.0 - beta_second**STEP)
    weight_new = weight - rate * (
        first_hat / (jnp.sqrt(second_hat) + epsilon) + decay_rate * weight
    )
    return (weight_new, first_new, second_new, weight_new.astype(BF16))


def dot(a, b):
    return jnp.dot(a, b, preferred_element_type=F32)


def dot_rows(a, b):
    return lax.dot_general(a, b, (((0,), (0,)), ((), ())), preferred_element_type=F32)


def aligned(value, unit):
    return pl.multiple_of(value, unit)


def block_kernel(
    rows,
    x_hbm,
    cot_hbm,
    ids_ref,
    mask_ref,
    conv_ref,
    point_ref,
    proj_ref,
    book_ref,
    dec_ref,
    ub_hbm,
    ig_hbm,
    g_ref,
    q_ref,
    dz_ref,
    xv,
    xhalo,
    cotv,
    shifted,
    mask_rows,
    col_mask,
    u_rows,
    ub_rows,
    lg_rows,
    hgp,
    hgt,
    wsend,
    wpre,
    wb,
    pb,
    wfull,
    wback,
    point_t,
    point_n,
    qf,
    bookf,
    decz,
    projz,
    proj_t,
    book_t,
    dec_acc,
    proj_acc,
    point_acc,
    book_acc,
    loss_acc,
    gp,
    gs,
    rp0,
    rp1,
    rp2,
    rc0,
    rc1,
    rc2,
    fin,
    rx3,
    x_sem,
    cot_sem,
    out_sem,
    ub_sem,
    halo_s,
    halo_r,
    ag_s,
    ag_r,
    rs_s,
    rs_r,
):
    dp, chan = lax.axis_index("dp"), lax.axis_index("chan")
    core, xc = lax.rem(chan, 2), lax.div(chan, 2)
    yc, zc = lax.rem(dp, 2), lax.div(dp, 2)
    core_peer = (dp, chan + 1 - 2 * core)

    def xy_of(k):
        x_new = 1 - xc if k % 2 else xc
        y_new = 1 - yc if k // 2 else yc
        return x_new, y_new

    def xy_peer(k):
        x_new, y_new = xy_of(k)
        return (2 * zc + y_new, 2 * x_new + core)

    def z_of(k):
        if k == 1:
            return zc + 1 - 2 * lax.rem(zc, 2)
        if k == 2:
            return lax.rem(zc + 2, 4)
        return 3 - zc

    def z_peer(k):
        return (2 * z_of(k) + yc, chan)

    up_peer, down_peer = (dp, chan - 1), (dp, chan + 1)
    chunks = rows // CHUNK_ROWS
    pixels = rows * PITCH
    pending = []

    def send(src, dst, s_sem, r_sem, peer):
        copy = pltpu.make_async_remote_copy(
            src_ref=src, dst_ref=dst, send_sem=s_sem, recv_sem=r_sem, device_id=peer, device_id_type=MESH
        )
        copy.start()
        pending.append(copy)
        return copy

    def x_copy(k):
        part = pl.ds(k * CHUNK_ROWS, CHUNK_ROWS)
        return pltpu.make_async_copy(x_hbm.at[part, :, pl.ds(0, SIDE), :], xv.at[part], x_sem.at[k])

    def cot_copy(k):
        part = pl.ds(k * CHUNK_ROWS, CHUNK_ROWS)
        return pltpu.make_async_copy(cot_hbm.at[part, :, pl.ds(0, SIDE), :], cotv.at[part], cot_sem.at[k])

    for k in range(chunks):
        x_copy(k).start()
    for k in range(chunks):
        cot_copy(k).start()

    lane = lax.broadcasted_iota(jnp.int32, (1, 128), 1)
    high = lane >= LAT
    own_half = high.astype(jnp.int32) == core

    def wide(block):
        return jnp.where(own_half, jnp.concatenate([block, block], axis=-1), 0.0).astype(BF16)

    conv_wide = wide(conv_ref[...])
    point_wide = wide(point_ref[...].T)
    for half in range(2):
        part = slice(half * 16, half * 16 + 16)
        wsend[half, 0:9] = conv_wide[:, part]
        wsend[half, 9] = point_wide[part]

    barrier = pltpu.get_barrier_semaphore()
    partners = [core_peer, (dp, 3 - chan)]
    partners += [xy_peer(k) for k in (1, 2, 3)] + [z_peer(k) for k in (1, 2, 3)]
    for partner in partners:
        pl.semaphore_signal(barrier, inc=1, device_id=partner, device_id_type=MESH)
    pl.semaphore_wait(barrier, len(partners))

    pre = send(wsend.at[1 - core], wpre, ag_s.at[0, 0], ag_r.at[0, 0], core_peer)

    def halo_copies(up_src, up_dst, down_src, down_dst, at):
        up = pltpu.make_async_remote_copy(
            src_ref=up_src, dst_ref=up_dst, send_sem=halo_s.at[at], recv_sem=halo_r.at[at],
            device_id=up_peer, device_id_type=MESH,
        )
        down = pltpu.make_async_remote_copy(
            src_ref=down_src, dst_ref=down_dst, send_sem=halo_s.at[at + 1], recv_sem=halo_r.at[at + 1],
            device_id=down_peer, device_id_type=MESH,
        )
        return up, down

    def halo_start(copies):
        @pl.when(chan > 0)
        def _():
            copies[0].start()

        @pl.when(chan < 3)
        def _():
            copies[1].start()

    def halo_wait_send(copies):
        @pl.when(chan > 0)
        def _():
            copies[0].wait_send()

        @pl.when(chan < 3)
        def _():
            copies[1].wait_send()

    def halo_wait_recv(copies):
        @pl.when(chan < 3)
        def _():
            copies[0].wait_recv()

        @pl.when(chan > 0)
        def _():
            copies[1].wait_recv()

    cols = pl.ds(0, SIDE)
    x_halo = halo_copies(
        x_hbm.at[0, :, cols, :], xhalo.at[1], x_hbm.at[rows - 1, :, cols, :], xhalo.at[0], 0
    )
    halo_start(x_halo)

    @pl.when(chan == 0)
    def _():
        xhalo[0] = jnp.zeros(xhalo.shape[1:], BF16)

    @pl.when(chan == 3)
    def _():
        xhalo[1] = jnp.zeros(xhalo.shape[1:], BF16)

    def gather_buffer(p):
        return pb if p == 0 else wb.at[p - 1]

    def gather_z(p):
        buffer = gather_buffer(p)
        block = buffer.at[core, xc, yc, zc]
        return [send(block, block, ag_s.at[p, k], ag_r.at[p, k], z_peer(k)) for k in (1, 2, 3)]

    def gather_xy(p):
        block = gather_buffer(p).at[core, xc, yc]
        return [send(block, block, ag_s.at[p, 3 + k], ag_r.at[p, 3 + k], xy_peer(k)) for k in (1, 2, 3)]

    def gather_core(p):
        block = gather_buffer(p).at[core]
        return [send(block, block, ag_s.at[p, 7], ag_r.at[p, 7], core_peer)]

    def landed(copies):
        for copy in copies:
            copy.wait_recv()

    top = mask_ref[0:8, :].astype(F32).T
    for t in range(BANDS):
        col_mask[t] = jnp.broadcast_to(top[0:SIDE, t : t + 1], (SIDE, 128))
    step_in = lax.broadcasted_iota(jnp.int32, (SIDE, 128), 0)
    not_first = (step_in > 0).astype(F32)
    not_last = (step_in < SIDE - 1).astype(F32)

    def two(block):
        return jnp.concatenate([block, block], axis=1)

    def shift_row(block_of, row_flags, at, keep):
        for t in range(BANDS):
            valid = col_mask[t] * row_flags[t : t + 1, 0:1]
            base = aligned(at + t * SIDE, 16)
            act = jnp.maximum(block_of(t).astype(F32), 0.0) * two(valid)
            shifted[pl.ds(base, SIDE), 256:512] = act.astype(BF16)
            before = pltpu.roll(act, 1, 0) * two(not_first)
            shifted[pl.ds(base, SIDE), 0:256] = before.astype(BF16)
            after = pltpu.roll(act, SIDE - 1, 0) * two(not_last)
            shifted[pl.ds(base, SIDE), 512:768] = after.astype(BF16)
            if keep is not None:
                mask_rows[pl.ds(aligned(keep + t * SIDE, 16), SIDE), :] = valid.astype(BF16)

    def shift_chunk(k, carry):
        flags = mask_ref[pl.ds(aligned((chan * rows + k * CHUNK_ROWS) * BANDS, 8), 8), :].astype(F32)
        for r in range(CHUNK_ROWS):
            row = k * CHUNK_ROWS + r
            shift_row(
                lambda t: xv[row, t],
                flags[r * BANDS : (r + 1) * BANDS],
                (row + 1) * PITCH,
                row * PITCH,
            )
        return carry

    x_copy(0).wait()
    shift_chunk(0, 0)
    pre.wait_recv()
    joined = wsend[core] + wpre[...]
    for i in range(3):
        wb[i, core, xc, yc, zc] = joined[3 * i : 3 * i + 3]
    pb[core, xc, yc, zc, 0] = joined[9]
    quant = jnp.concatenate(
        [
            jnp.concatenate([dec_ref[...], proj_ref[...]], axis=1),
            jnp.concatenate([book_ref[0:8, :], book_ref[8:16, :]], axis=1),
        ],
        axis=0,
    )
    pb[core, xc, yc, zc, 1] = quant.astype(BF16)
    on_z = [gather_z(p) for p in range(4)]

    for k in range(1, chunks):
        x_copy(k).wait()
    lax.fori_loop(1, chunks, shift_chunk, 0)
    landed(on_z[0])
    on_xy = [gather_xy(0)]
    halo_wait_recv(x_halo)

    def halo_row(side, at, global_row, present):
        first = aligned(lax.div(jnp.maximum(global_row, 0), 4) * 8, 8)
        group = mask_ref[pl.ds(first, 8), :].astype(F32)
        inside = 2 * (3 if side == 0 else 0)
        flags = group[inside : inside + 2]
        scale = present.astype(F32)

        shift_row(lambda t: xhalo[side, t], flags * scale, at, None)

    halo_row(0, 0, chan * rows - 1, chan > 0)
    halo_row(1, (rows + 1) * PITCH, jnp.minimum(chan * rows + rows, 3 * rows), chan < 3)

    landed(on_z[1])
    on_xy.append(gather_xy(1))
    landed(on_z[2])
    on_xy.append(gather_xy(2))
    landed(on_z[3])
    on_xy.append(gather_xy(3))

    dec_acc[...] = jnp.zeros_like(dec_acc)
    proj_acc[...] = jnp.zeros_like(proj_acc)
    point_acc[...] = jnp.zeros_like(point_acc)
    book_acc[...] = jnp.zeros_like(book_acc)
    loss_acc[...] = jnp.zeros_like(loss_acc)

    landed(on_xy[0])
    on_core = [gather_core(0)]
    landed(on_core[0])

    blocks = [(h, x, y, z) for z in range(4) for y in range(2) for x in range(2) for h in range(2)]
    for h, x, y, z in blocks:
        point_t[z * 64 + y * 32 + h * 16 : z * 64 + y * 32 + h * 16 + 16, x * 128 : x * 128 + 128] = pb[h, x, y, z, 0]
        owner = (2 * z + y) * 4 + 2 * x + h
        small = pb[h, x, y, z, 1].astype(F32)
        qf[owner * 8 : owner * 8 + 8, :] = small[0:8]
        bookf[owner * 16 : owner * 16 + 8, :] = pltpu.roll(small[8:16], LAT, 1)
        bookf[owner * 16 + 8 : owner * 16 + 16, :] = small[8:16]
    point_n[...] = point_t[...].T
    small = qf[...]
    decz[...] = jnp.where(high, 0.0, small).astype(BF16)
    projz[...] = jnp.where(high, small, 0.0).astype(BF16)
    dz_ref[...] = jnp.where(high, pltpu.roll(small, LAT, 1), 0.0).astype(BF16)
    proj_t[...] = jnp.where(high, 0.0, pltpu.roll(small, LAT, 1)).astype(BF16).T
    book_t[...] = jnp.where(high, bookf[...], 0.0).astype(BF16).T

    def onehot_t(k):
        entries = lax.broadcasted_iota(jnp.int32, (book_t.shape[1], CHUNK), 0)
        return (entries == ids_ref[k]).astype(F32).astype(BF16)

    def chunk_of(ref, k):
        return ref[pl.ds(aligned(k * CHUNK, 16), CHUNK), :]

    def pixels_of(ref, k):
        return ref[pl.ds(k * CHUNK_ROWS, CHUNK_ROWS)].reshape(CHUNK, 256)

    def decoder_chunk(k, carry):
        valid = chunk_of(mask_rows, k).astype(F32)
        kept = (pixels_of(cotv, k).astype(F32) * two(valid)).astype(BF16)
        chosen = dot(book_t[...], onehot_t(k)).T
        both = chosen + dot(kept, decz[...])
        u_rows[pl.ds(aligned(k * CHUNK, 16), CHUNK), :] = both
        both_low = both.astype(BF16)
        ub_rows[pl.ds(aligned(k * CHUNK, 16), CHUNK), :] = both_low
        dec_acc[...] += dot_rows(kept, both_low)
        return carry

    for k in range(chunks):
        cot_copy(k).wait()
    lax.fori_loop(0, 2, decoder_chunk, 0)
    landed(on_xy[1])
    on_core.append(gather_core(1))
    lax.fori_loop(2, 4, decoder_chunk, 0)
    landed(on_xy[2])
    on_core.append(gather_core(2))
    lax.fori_loop(4, 6, decoder_chunk, 0)
    landed(on_xy[3])
    on_core.append(gather_core(3))
    lax.fori_loop(6, chunks, decoder_chunk, 0)
    ub_copy = pltpu.make_async_copy(ub_rows, ub_hbm, ub_sem)
    ub_copy.start()

    for i in range(3):
        landed(on_core[1 + i])
        for h, x, y, z in blocks:
            for j in range(3):
                first = j * 256 + z * 64 + y * 32 + h * 16
                wfull[i, first : first + 16, x * 128 : x * 128 + 128] = wb[i, h, x, y, z, j]
        for j in range(3):
            wback[i, :, j * 256 : j * 256 + 256] = wfull[i, j * 256 : j * 256 + 256, :].T

    def forward_chunk(k, carry):
        hidden = None
        for i in range(3):
            window = shifted[pl.ds(aligned((k * CHUNK_ROWS + i) * PITCH, 16), CHUNK), :]
            term = dot(window, wfull[i])
            hidden = term if hidden is None else hidden + term
        middle = jnp.maximum(hidden, 0.0).astype(BF16)
        branch = dot(middle, point_n[...])
        summed = (pixels_of(xv, k).astype(F32) + branch).astype(BF16)
        valid = chunk_of(mask_rows, k).astype(F32)
        gap = chunk_of(u_rows, k) - dot(summed, projz[...])
        weighted = gap * valid
        loss_acc[...] += jnp.sum((weighted * gap).reshape(CHUNK // 8, 8, 128), axis=0)
        latent_grad = (gap - 0.5 * pltpu.roll(weighted, LAT, 1)).astype(BF16)
        lg_rows[pl.ds(aligned(k * CHUNK, 16), CHUNK), :] = latent_grad
        term = 2.0 * weighted
        coarse = term.astype(BF16).astype(F32)
        fine = pltpu.roll(term - coarse, LAT, 1)
        parts = jnp.where(high, coarse, fine).astype(BF16)
        book_acc[...] += dot(onehot_t(k), parts)
        proj_acc[...] += dot_rows(summed, latent_grad)
        resid_low = dot(latent_grad, proj_t[...]).astype(BF16)
        point_acc[...] += dot_rows(resid_low, middle)
        back = dot(resid_low, point_t[...])
        hidden_grad = jnp.where(hidden > 0.0, back, 0.0).astype(BF16)
        hgp[pl.ds(aligned((k * CHUNK_ROWS + 1) * PITCH, 16), CHUNK), :] = hidden_grad
        hgt[:, pl.ds(aligned(k * CHUNK, 128), CHUNK)] = hidden_grad.T
        return carry

    lax.fori_loop(0, chunks, forward_chunk, 0)

    zero_row = jnp.zeros((PITCH, 256), BF16)

    @pl.when(chan == 0)
    def _():
        hgp[0:PITCH, :] = zero_row

    @pl.when(chan == 3)
    def _():
        hgp[(rows + 1) * PITCH : (rows + 2) * PITCH, :] = zero_row

    def grad_row(r):
        return hgp.at[pl.ds(r * PITCH, PITCH), :]

    hg_halo = halo_copies(grad_row(1), grad_row(rows + 1), grad_row(rows), grad_row(0), 2)
    halo_start(hg_halo)

    def reduce_buffers(p):
        if p == 0:
            return gp, rp0, rp1, rp2
        return gs.at[p - 1], rc0.at[p - 1], rc1.at[p - 1], rc2.at[p - 1]

    def reduce_core(p):
        buffer, first, _, _ = reduce_buffers(p)
        return [send(buffer.at[1 - core], first, rs_s.at[p, 0], rs_r.at[p, 0], core_peer)]

    def reduce_xy(p, copies):
        landed(copies)
        buffer, first, second, _ = reduce_buffers(p)
        buffer[core] = buffer[core] + first[...]
        out = []
        for k in (1, 2, 3):
            x_new, y_new = xy_of(k)
            out.append(
                send(buffer.at[core, x_new, y_new], second.at[k - 1], rs_s.at[p, k], rs_r.at[p, k], xy_peer(k))
            )
        return out

    def reduce_z(p, copies):
        landed(copies)
        buffer, _, second, third = reduce_buffers(p)
        buffer[core, xc, yc] = (buffer[core, xc, yc] + second[0]) + (second[1] + second[2])
        return [
            send(buffer.at[core, xc, yc, z_of(k)], third.at[k - 1], rs_s.at[p, 3 + k], rs_r.at[p, 3 + k], z_peer(k))
            for k in (1, 2, 3)
        ]

    def reduce_end(p, copies):
        landed(copies)
        buffer, _, _, third = reduce_buffers(p)
        total = (buffer[core, xc, yc, zc] + third[0]) + (third[1] + third[2])
        if p == 0:
            q_ref[...] = total[16:40]
            fin[9] = total[0:16]
        else:
            for j in range(3):
                fin[3 * (p - 1) + j] = total[j * 16 : j * 16 + 16]

    counts = mask_ref[pl.ds(aligned(chan * rows * BANDS, 8), rows * BANDS), :].astype(F32)
    counts = jnp.sum(counts.reshape(rows * BANDS // 8, 8, 128), axis=0)
    tallies = jnp.where(high, loss_acc[...], counts + pltpu.roll(counts, LAT, 1))
    heads = jnp.where(high, dec_acc[...], proj_acc[...])
    book_sum = book_acc[...] + pltpu.roll(book_acc[...], LAT, 1)
    for h, x, y, z in blocks:
        first = z * 64 + y * 32 + h * 16
        owner = (2 * z + y) * 4 + 2 * x + h
        gp[h, x, y, z, 0:16] = point_acc[first : first + 16, x * 128 : x * 128 + 128]
        gp[h, x, y, z, 16:24] = heads[owner * 8 : owner * 8 + 8]
        gp[h, x, y, z, 24:32] = jnp.where(
            high, book_sum[owner * 16 + 8 : owner * 16 + 16], book_sum[owner * 16 : owner * 16 + 8]
        )
        gp[h, x, y, z, 32:40] = tallies
    stage = [reduce_core(0), None, None, None]

    def conv_grad(i):
        product = dot(hgt[...], shifted[i * PITCH : i * PITCH + pixels, :])
        for j in range(3):
            turned = product[:, j * 256 : j * 256 + 256].T
            for h, x, y, z in blocks:
                first = z * 64 + y * 32 + h * 16
                gs[i, h, x, y, z, j * 16 : j * 16 + 16] = turned[first : first + 16, x * 128 : x * 128 + 128]

    conv_grad(0)
    stage[1] = reduce_core(1)
    stage[0] = reduce_xy(0, stage[0])
    conv_grad(1)
    stage[2] = reduce_core(2)
    stage[1] = reduce_xy(1, stage[1])
    conv_grad(2)
    stage[3] = reduce_core(3)
    stage[2] = reduce_xy(2, stage[2])
    stage[0] = reduce_z(0, stage[0])
    halo_wait_recv(hg_halo)

    edge_first = two(not_first)[None]
    edge_last = two(not_last)[None]

    def out_copy(k):
        part = pl.ds(k * CHUNK_ROWS, CHUNK_ROWS)
        return pltpu.make_async_copy(cotv.at[part], ig_hbm.at[part], out_sem.at[k])

    def back_chunk(k, carry):
        total = None
        for i in range(3):
            window = hgp[pl.ds(aligned((k * CHUNK_ROWS + 2 - i) * PITCH, 16), CHUNK), :]
            term = dot(window, wback[i])
            total = term if total is None else total + term
        segments = CHUNK // SIDE
        before = pltpu.roll(total[:, 512:768], 1, 0).reshape(segments, SIDE, 256) * edge_first
        after = pltpu.roll(total[:, 0:256], CHUNK - 1, 0).reshape(segments, SIDE, 256) * edge_last
        back_grad = total[:, 256:512] + (before + after).reshape(CHUNK, 256)
        slope = shifted[pl.ds(aligned((k * CHUNK_ROWS + 1) * PITCH, 16), CHUNK), 256:512].astype(F32) > 0.0
        resid = dot(chunk_of(lg_rows, k), proj_t[...])
        grad = (resid + jnp.where(slope, back_grad, 0.0)).astype(BF16)
        cotv[pl.ds(k * CHUNK_ROWS, CHUNK_ROWS)] = grad.reshape(CHUNK_ROWS, BANDS, SIDE, 256)
        return carry

    def back_chunks(first, last):
        lax.fori_loop(first, last, back_chunk, 0)
        for k in range(first, last):
            out_copy(k).start()

    back_chunks(0, 1)
    stage[3] = reduce_xy(3, stage[3])
    back_chunks(1, 3)
    stage[1] = reduce_z(1, stage[1])
    reduce_end(0, stage[0])
    back_chunks(3, 5)
    stage[2] = reduce_z(2, stage[2])
    reduce_end(1, stage[1])
    back_chunks(5, chunks)
    stage[3] = reduce_z(3, stage[3])
    reduce_end(2, stage[2])
    reduce_end(3, stage[3])
    last = send(fin, rx3, rs_s.at[0, 7], rs_r.at[0, 7], core_peer)
    last.wait_recv()
    mine, other = fin[...], rx3[...]
    is_first = core == 0
    lower = jnp.where(is_first, mine, other)
    upper = jnp.where(is_first, other, mine)
    whole = jnp.concatenate([lower, upper], axis=1)
    g_ref[...] = jnp.where(is_first, whole[..., 0:LAT], whole[..., LAT:])

    for k in range(chunks):
        out_copy(k).wait()
    ub_copy.wait()
    halo_wait_send(x_halo)
    halo_wait_send(hg_halo)
    for copy in pending:
        copy.wait_send()


def finish_kernel(
    ig_ref, ub_ref, mask_ref, dec_ref, g_ref, q_ref,
    conv_w, conv_m, conv_v, point_w, point_m, point_v, proj_w, proj_m, proj_v,
    code_w, code_m, code_v, dec_w, dec_m, dec_v,
    out_ref, grad_ref, loss_ref, *updates,
):
    step = pl.program_id(0)
    steps_rows = out_ref.shape[0]
    chan = lax.axis_index("chan")
    first = (chan * pl.num_programs(0) + step) * steps_rows * BANDS
    flags = mask_ref[pl.ds(aligned(first, 8), steps_rows * BANDS), :].astype(F32)
    top = mask_ref[0:8, :].astype(F32).T
    decoded = lax.dot_general(
        ub_ref[...], dec_ref[...], (((1,), (1,)), ((), ())), preferred_element_type=F32
    )
    decoded = decoded.reshape(steps_rows, BANDS, SIDE, 256)
    for r in range(steps_rows):
        for t in range(BANDS):
            at = r * BANDS + t
            valid = top[0:SIDE, t : t + 1] * flags[at : at + 1, 0:1]
            out_ref[r, t, 0:SIDE, :] = (decoded[r, t] * valid).astype(BF16)
            grad_ref[r, t, 0:SIDE, :] = ig_ref[r, t]

    @pl.when(step == 0)
    def _():
        q = q_ref[...]
        heads, book = q[0:8], q[8:16]
        high = lax.broadcasted_iota(jnp.int32, (8, 128), 1) >= LAT
        gap = jnp.sum(jnp.where(high, q[16:24], 0.0))
        count = jnp.sum(jnp.where(high, 0.0, q[16:24]))
        ratio = jnp.full((8, 128), gap, F32) / jnp.full((8, 128), count * LAT, F32)
        row = lax.broadcasted_iota(jnp.int32, (8, 128), 0)
        loss_ref[...] = jnp.where(row == 0, ratio, 0.25 * ratio)
        sets = (
            (g_ref[0:9], conv_w, conv_m, conv_v, 0.01),
            (g_ref[9].T, point_w, point_m, point_v, 0.03),
            (heads[:, 0:LAT], proj_w, proj_m, proj_v, 0.03),
            (jnp.concatenate([book[:, 0:LAT], book[:, LAT:]], axis=0), code_w, code_m, code_v, 0.5),
            (heads[:, LAT:], dec_w, dec_m, dec_v, 0.06),
        )
        for n, (grad, weight, moment, square, rate) in enumerate(sets):
            results = adamw(grad, weight[...], moment[...], square[...], rate)
            for m in range(4):
                updates[4 * n + m][...] = results[m]


def vmem():
    return pl.BlockSpec(memory_space=pltpu.VMEM)


def anywhere():
    return pl.BlockSpec(memory_space=pl.ANY)


def on_device(
    inputs, valid_mask, code_ids, cotangent,
    conv_weight, conv_first, conv_second, point_weight, point_first, point_second,
    proj_weight, proj_first, proj_second, code_book, code_first, code_second,
    dec_weight, dec_first, dec_second,
):
    channels = inputs.shape[1]
    rows = inputs.shape[0] // (BANDS * BAND)
    chunks = rows // CHUNK_ROWS
    pixels = rows * PITCH
    padded = pixels + 2 * PITCH
    entries = 32 * code_book.shape[0]
    canvas = (rows, BANDS, BAND, channels)
    mask = valid_mask.reshape(-1, BAND)
    ids = code_ids.reshape(rows * BANDS, BAND)[:, :SIDE].reshape(chunks, 1, CHUNK)
    packed = (rows, BANDS, SIDE, channels)
    dma = pltpu.SemaphoreType.DMA
    ub, ig, grads, quant, decoder = pl.pallas_call(
        functools.partial(block_kernel, rows),
        out_shape=(
            jax.ShapeDtypeStruct((pixels, 128), BF16),
            jax.ShapeDtypeStruct(packed, BF16),
            jax.ShapeDtypeStruct((10, 32, LAT), F32),
            jax.ShapeDtypeStruct((24, 128), F32),
            jax.ShapeDtypeStruct((channels, 128), BF16),
        ),
        in_specs=[anywhere()] * 2 + [vmem()] * 7,
        out_specs=(anywhere(), anywhere(), vmem(), vmem(), vmem()),
        scratch_shapes=[
            pltpu.VMEM(packed, BF16),
            pltpu.VMEM((2, BANDS, SIDE, channels), BF16),
            pltpu.VMEM(packed, BF16),
            pltpu.VMEM((padded, 3 * channels), BF16),
            pltpu.VMEM((pixels, 128), BF16),
            pltpu.VMEM((BANDS, SIDE, 128), F32),
            pltpu.VMEM((pixels, 128), F32),
            pltpu.VMEM((pixels, 128), BF16),
            pltpu.VMEM((pixels, 128), BF16),
            pltpu.VMEM((padded, channels), BF16),
            pltpu.VMEM((channels, pixels), BF16),
            pltpu.VMEM((2, 10, 16, 128), BF16),
            pltpu.VMEM((10, 16, 128), BF16),
            pltpu.VMEM((3, 2, 2, 2, 4, 3, 16, 128), BF16),
            pltpu.VMEM((2, 2, 2, 4, 2, 16, 128), BF16),
            pltpu.VMEM((3, 3 * channels, channels), BF16),
            pltpu.VMEM((3, channels, 3 * channels), BF16),
            pltpu.VMEM((channels, channels), BF16),
            pltpu.VMEM((channels, channels), BF16),
            pltpu.VMEM((channels, 128), F32),
            pltpu.VMEM((entries, 128), F32),
            pltpu.VMEM((channels, 128), BF16),
            pltpu.VMEM((channels, 128), BF16),
            pltpu.VMEM((128, channels), BF16),
            pltpu.VMEM((128, entries), BF16),
            pltpu.VMEM((channels, 128), F32),
            pltpu.VMEM((channels, 128), F32),
            pltpu.VMEM((channels, channels), F32),
            pltpu.VMEM((entries, 128), F32),
            pltpu.VMEM((8, 128), F32),
            pltpu.VMEM((2, 2, 2, 4, 40, 128), F32),
            pltpu.VMEM((3, 2, 2, 2, 4, 48, 128), F32),
            pltpu.VMEM((2, 2, 4, 40, 128), F32),
            pltpu.VMEM((3, 4, 40, 128), F32),
            pltpu.VMEM((3, 40, 128), F32),
            pltpu.VMEM((3, 2, 2, 4, 48, 128), F32),
            pltpu.VMEM((3, 3, 4, 48, 128), F32),
            pltpu.VMEM((3, 3, 48, 128), F32),
            pltpu.VMEM((10, 16, 128), F32),
            pltpu.VMEM((10, 16, 128), F32),
            dma((chunks,)),
            dma((chunks,)),
            dma((chunks,)),
            dma(()),
            dma((4,)),
            dma((4,)),
            dma((4, 8)),
            dma((4, 8)),
            dma((4, 8)),
            dma((4, 8)),
        ],
        compiler_params=pltpu.CompilerParams(
            collective_id=0, has_side_effects=True, vmem_limit_bytes=60 * 2**20
        ),
        name="block",
    )(
        inputs.reshape(canvas), cotangent.reshape(canvas), ids, mask,
        conv_weight, point_weight, proj_weight, code_book, dec_weight,
    )

    states = (
        conv_weight, conv_first, conv_second, point_weight, point_first, point_second,
        proj_weight, proj_first, proj_second, code_book, code_first, code_second,
        dec_weight, dec_first, dec_second,
    )
    tiles = pl.BlockSpec((CHUNK_ROWS, BANDS, BAND, channels), lambda n: (n, 0, 0, 0))

    def whole(shape):
        return pl.BlockSpec(shape, lambda n: (0,) * len(shape))

    updates, specs = [], []
    for n in range(5):
        shape = states[3 * n].shape
        for kind in (F32, F32, F32, BF16):
            updates.append(jax.ShapeDtypeStruct(shape, kind))
            specs.append(whole(shape))
    results = pl.pallas_call(
        finish_kernel,
        grid=(chunks,),
        out_shape=(
            jax.ShapeDtypeStruct(canvas, BF16),
            jax.ShapeDtypeStruct(canvas, BF16),
            jax.ShapeDtypeStruct((8, 128), F32),
            *updates,
        ),
        in_specs=[
            pl.BlockSpec((CHUNK_ROWS, BANDS, SIDE, channels), lambda n: (n, 0, 0, 0)),
            pl.BlockSpec((CHUNK, 128), lambda n: (n, 0)),
            whole(mask.shape),
            whole(decoder.shape),
            whole(grads.shape),
            whole(quant.shape),
            *[whole(s.shape) for s in states],
        ],
        out_specs=(tiles, tiles, whole((8, 128)), *specs),
        compiler_params=pltpu.CompilerParams(vmem_limit_bytes=40 * 2**20),
        name="finish",
    )(ig, ub, mask, decoder, grads, quant, *states)
    output, input_grad, ratio = results[:3]
    return (
        output.reshape(inputs.shape),
        input_grad.reshape(inputs.shape),
        ratio[0:2, 0],
        *results[3:],
    )


def row_stride():
    return BANDS * BAND


def tap_offsets():
    stride = row_stride()
    return [row_step * stride + col_step for row_step in (-1, 0, 1) for col_step in (-1, 0, 1)]


def conv_forward(padded, weights, row_count):
    margin = row_stride() + 1
    summed_terms = None
    for tap_index, offset in enumerate(tap_offsets()):
        begin = margin + offset
        window = lax.slice_in_dim(padded, begin, begin + row_count, axis=0)
        product = jnp.dot(window, weights[tap_index], preferred_element_type=jnp.float32)
        summed_terms = product if summed_terms is None else summed_terms + product
    return summed_terms


def conv_weight_grad(padded, grads, row_count):
    margin = row_stride() + 1
    products = []
    for offset in tap_offsets():
        begin = margin + offset
        window = lax.slice_in_dim(padded, begin, begin + row_count, axis=0)
        products.append(
            lax.dot_general(
                window, grads, (((0,), (0,)), ((), ())), preferred_element_type=jnp.float32
            )
        )
    return jnp.stack(products)


def conv_input_grad(padded_grads, weights, row_count):
    margin = row_stride() + 1
    summed_terms = None
    for tap_index, offset in enumerate(tap_offsets()):
        begin = margin - offset
        window = lax.slice_in_dim(padded_grads, begin, begin + row_count, axis=0)
        product = lax.dot_general(
            window, weights[tap_index], (((1,), (1,)), ((), ())), preferred_element_type=jnp.float32
        )
        summed_terms = product if summed_terms is None else summed_terms + product
    return summed_terms


def bottleneck(latent, mask_rows, code_rows, cotangent, codebook, decoder):
    weight_rows = mask_rows.astype(jnp.float32)[:, None]
    entries = jnp.arange(codebook.shape[0], dtype=jnp.int32)
    onehot = (code_rows[:, None] == entries[None, :]).astype(jnp.bfloat16)
    chosen = jnp.dot(onehot, codebook, preferred_element_type=jnp.float32)
    gap_rows = latent - chosen
    loss_part = jnp.sum(weight_rows * gap_rows * gap_rows)
    count_part = jnp.sum(weight_rows)
    decoded = chosen.astype(jnp.bfloat16)
    decoded_out = lax.dot_general(
        decoded, decoder, (((1,), (1,)), ((), ())), preferred_element_type=jnp.float32
    )
    output = (decoded_out * weight_rows).astype(jnp.bfloat16)
    kept_rows = cotangent * mask_rows.astype(jnp.bfloat16)[:, None]
    decoded_grad = jnp.dot(kept_rows, decoder, preferred_element_type=jnp.float32)
    latent_grad = (decoded_grad + 0.5 * weight_rows * gap_rows).astype(jnp.bfloat16)
    decoder_grad = lax.dot_general(
        kept_rows, decoded, (((0,), (0,)), ((), ())), preferred_element_type=jnp.float32
    )
    book_term = -2.0 * weight_rows * gap_rows
    high_part = book_term.astype(jnp.bfloat16)
    rest_term = book_term - high_part.astype(jnp.float32)
    middle_part = rest_term.astype(jnp.bfloat16)
    low_part = (rest_term - middle_part.astype(jnp.float32)).astype(jnp.bfloat16)
    stacked = jnp.concatenate([high_part, middle_part, low_part], axis=1)
    book_parts = lax.dot_general(
        onehot, stacked, (((0,), (0,)), ((), ())), preferred_element_type=jnp.float32
    )
    width = book_term.shape[1]
    book_grad = book_parts[:, :width] + (
        book_parts[:, width : 2 * width] + book_parts[:, 2 * width :]
    )
    return (output, latent_grad, decoder_grad, book_grad, loss_part, count_part)


def general(
    inputs,
    valid_mask,
    code_ids,
    cotangent,
    conv_weight,
    conv_first,
    conv_second,
    point_weight,
    point_first,
    point_second,
    proj_weight,
    proj_first,
    proj_second,
    code_book,
    code_first,
    code_second,
    dec_weight,
    dec_first,
    dec_second,
):
    chan_count = lax.axis_size("chan")
    chan_index = lax.axis_index("chan")
    rows_quarter = inputs.shape[0]
    rows_all = valid_mask.shape[0]
    channels = inputs.shape[1]
    chan_width = channels // chan_count
    margin = row_stride() + 1
    conv_low, point_low = (
        lax.all_gather(conv_weight.astype(jnp.bfloat16), "dp", axis=1, tiled=True),
        lax.all_gather(point_weight.astype(jnp.bfloat16), "dp", axis=1, tiled=True),
    )
    proj_full, book_full, dec_full = (
        lax.all_gather(proj_weight.astype(jnp.bfloat16), ("dp", "chan"), axis=0, tiled=True),
        lax.all_gather(code_book.astype(jnp.bfloat16), ("dp", "chan"), axis=0, tiled=True),
        lax.all_gather(dec_weight.astype(jnp.bfloat16), ("dp", "chan"), axis=0, tiled=True),
    )
    mask_rows = lax.dynamic_slice_in_dim(valid_mask, chan_index * rows_quarter, rows_quarter)
    first_column = chan_index * chan_width
    gathered = lax.all_gather(inputs, "chan", axis=0, tiled=True)
    valid_all = (valid_mask > 0)[:, None]
    activations = jnp.where(valid_all, jnp.maximum(gathered, 0), 0)
    padded = jnp.pad(activations, ((margin, margin), (0, 0)))
    hidden = conv_forward(padded, conv_low, rows_all)
    middle = jnp.maximum(hidden, 0.0).astype(jnp.bfloat16)
    partial_branch = jnp.dot(middle, point_low, preferred_element_type=jnp.float32)
    branch = lax.psum_scatter(partial_branch, "chan", scatter_dimension=1, tiled=True)
    own_inputs = lax.dynamic_slice_in_dim(gathered, first_column, chan_width, 1).astype(jnp.float32)
    summed = (own_inputs + branch).astype(jnp.bfloat16)
    proj_rows = lax.dynamic_slice_in_dim(proj_full, first_column, chan_width, 0)
    window = summed
    latent = lax.psum_scatter(
        jnp.dot(window, proj_rows, preferred_element_type=jnp.float32),
        "chan",
        scatter_dimension=0,
        tiled=True,
    )
    output, latent_grad, decoder_grad, book_grad, loss_part, count_part = bottleneck(
        latent, mask_rows, code_ids, cotangent, book_full, dec_full
    )
    grads_all = lax.all_gather(latent_grad, "chan", axis=0, tiled=True)
    proj_part = lax.dot_general(
        summed, grads_all, (((0,), (0,)), ((), ())), preferred_element_type=jnp.float32
    )
    proj_grad = lax.dynamic_update_slice_in_dim(
        jnp.zeros((channels, proj_part.shape[1]), jnp.float32), proj_part, first_column, 0
    )
    resid = lax.dot_general(
        grads_all, proj_rows, (((1,), (1,)), ((), ())), preferred_element_type=jnp.float32
    )
    resid_all = lax.all_gather(resid.astype(jnp.bfloat16), "chan", axis=1, tiled=True)
    point_grad = lax.dot_general(
        middle, resid_all, (((0,), (0,)), ((), ())), preferred_element_type=jnp.float32
    )
    hidden_back = lax.dot_general(
        resid_all, point_low, (((1,), (1,)), ((), ())), preferred_element_type=jnp.float32
    )
    hidden_grad = jnp.where(hidden > 0.0, hidden_back.astype(jnp.bfloat16), 0)
    conv_grad = conv_weight_grad(padded, hidden_grad, rows_all)
    grad_padded = jnp.pad(hidden_grad, ((margin, margin), (0, 0)))
    slopes = jnp.logical_and(gathered > 0, valid_all)
    window = grad_padded
    back_grad = conv_input_grad(window, conv_low, rows_quarter * lax.axis_size("chan"))
    back_grad = jnp.where(slopes, back_grad, 0.0)
    own_back = lax.dynamic_slice_in_dim(back_grad, first_column, chan_width, 1)
    input_grad = lax.psum_scatter(
        lax.dynamic_update_slice_in_dim(back_grad, own_back + resid, first_column, 1),
        "chan",
        scatter_dimension=0,
        tiled=True,
    ).astype(jnp.bfloat16)
    conv_reduced, point_reduced = (
        lax.psum_scatter(conv_grad, "dp", scatter_dimension=1, tiled=True),
        lax.psum_scatter(point_grad, "dp", scatter_dimension=1, tiled=True),
    )
    proj_reduced, book_reduced, dec_reduced = (
        lax.psum_scatter(proj_grad, ("dp", "chan"), scatter_dimension=0, tiled=True),
        lax.psum_scatter(book_grad, ("dp", "chan"), scatter_dimension=0, tiled=True),
        lax.psum_scatter(decoder_grad, ("dp", "chan"), scatter_dimension=0, tiled=True),
    )
    loss_total, count_total = lax.psum((loss_part, count_part), ("dp", "chan"))
    losses = jnp.stack([loss_total, 0.25 * loss_total]) / (count_total * LAT)
    conv_out = adamw(conv_reduced, conv_weight, conv_first, conv_second, 0.01)
    point_out = adamw(point_reduced, point_weight, point_first, point_second, 0.03)
    proj_out = adamw(proj_reduced, proj_weight, proj_first, proj_second, 0.03)
    code_out = adamw(book_reduced, code_book, code_first, code_second, 0.5)
    dec_out = adamw(dec_reduced, dec_weight, dec_first, dec_second, 0.06)
    return (
        output,
        input_grad,
        losses,
        conv_out[0],
        conv_out[1],
        conv_out[2],
        conv_out[3],
        point_out[0],
        point_out[1],
        point_out[2],
        point_out[3],
        proj_out[0],
        proj_out[1],
        proj_out[2],
        proj_out[3],
        code_out[0],
        code_out[1],
        code_out[2],
        code_out[3],
        dec_out[0],
        dec_out[1],
        dec_out[2],
        dec_out[3],
    )


def solution(mesh):
    pixel = P(("dp", "chan"), None)
    conv, point = P(None, "dp", "chan"), P("chan", "dp")
    in_specs = (pixel, P("dp"), P(("dp", "chan")), pixel)
    in_specs += (conv,) * 3 + (point,) * 3 + (pixel,) * 9
    out_specs = (pixel, pixel, P()) + (conv,) * 4 + (point,) * 4 + (pixel,) * 12
    fits = mesh.shape["dp"] == 8 and mesh.shape["chan"] == 4
    body = on_device if fits else general
    return jax.shard_map(body, mesh=mesh, in_specs=in_specs, out_specs=out_specs, check_vma=False)
```

```python
import functools

import jax
import jax.numpy as jnp
from jax import lax
from jax.experimental import pallas as pl
from jax.experimental.pallas import tpu as pltpu
from jax.sharding import PartitionSpec as P

LAT = 64
BAND = 128
BANDS = 2
STEP = 5
PITCH = BANDS * BAND
CHUNK_ROWS = 8
CHUNK = CHUNK_ROWS * PITCH
MESH = pl.DeviceIdType.MESH
F32 = jnp.float32
BF16 = jnp.bfloat16

beta_first = 0.5
beta_second = 0.5
epsilon = 1e-08
decay_rate = 0.01


def adamw(grad, weight, first, second, rate):
    first_new = beta_first * first + (1.0 - beta_first) * grad
    second_new = beta_second * second + (1.0 - beta_second) * grad * grad
    first_hat = first_new / (1.0 - beta_first**STEP)
    second_hat = second_new / (1.0 - beta_second**STEP)
    weight_new = weight - rate * (
        first_hat / (jnp.sqrt(second_hat) + epsilon) + decay_rate * weight
    )
    return (weight_new, first_new, second_new, weight_new.astype(BF16))


def dot(a, b):
    return jnp.dot(a, b, preferred_element_type=F32)


def dot_rows(a, b):
    return lax.dot_general(a, b, (((0,), (0,)), ((), ())), preferred_element_type=F32)


def aligned(value, unit):
    return pl.multiple_of(value, unit)


def block_kernel(
    rows,
    x_hbm,
    cot_hbm,
    ids_ref,
    mask_ref,
    conv_ref,
    point_ref,
    proj_ref,
    book_ref,
    dec_ref,
    ub_hbm,
    ig_hbm,
    g_ref,
    q_ref,
    dz_ref,
    xv,
    xhalo,
    cotv,
    shifted,
    col_mask,
    u_rows,
    lg_rows,
    hgp,
    hgt,
    wsend,
    wpre,
    wb,
    pb,
    wfull,
    wback,
    point_t,
    point_n,
    qf,
    bookf,
    decz,
    projz,
    proj_t,
    book_t,
    dec_acc,
    proj_acc,
    point_acc,
    book_acc,
    loss_acc,
    gp,
    gs,
    rp0,
    rp1,
    rp2,
    rc0,
    rc1,
    rc2,
    fin,
    rx3,
    x_sem,
    cot_sem,
    out_sem,
    ub_sem,
    halo_s,
    halo_r,
    ag_s,
    ag_r,
    rs_s,
    rs_r,
):
    dp, chan = lax.axis_index("dp"), lax.axis_index("chan")
    core, xc = lax.rem(chan, 2), lax.div(chan, 2)
    yc, zc = lax.rem(dp, 2), lax.div(dp, 2)
    core_peer = (dp, chan + 1 - 2 * core)
    other_core = 1 - core
    xy_of = [(1 - xc if k % 2 else xc, 1 - yc if k // 2 else yc) for k in range(4)]
    xy_peer = [(2 * zc + y, 2 * x + core) for x, y in xy_of]
    z_of = [zc, zc + 1 - 2 * lax.rem(zc, 2), lax.rem(zc + 2, 4), 3 - zc]
    z_peer = [(2 * z + yc, chan) for z in z_of]
    up_peer, down_peer = (dp, chan - 1), (dp, chan + 1)
    chunks = rows // CHUNK_ROWS
    pixels = rows * PITCH
    def remote(src, dst, s_sem, r_sem, peer):
        return pltpu.make_async_remote_copy(
            src_ref=src, dst_ref=dst, send_sem=s_sem, recv_sem=r_sem, device_id=peer, device_id_type=MESH
        )

    def start(copies):
        for copy in copies:
            copy.start()

    def landed(copies):
        for copy in copies:
            copy.wait_recv()

    def sent(copies):
        for copy in copies:
            copy.wait_send()

    def part(k):
        return pl.ds(k * CHUNK, CHUNK)

    def x_copy(k):
        return pltpu.make_async_copy(x_hbm.at[part(k)], xv.at[part(k)], x_sem.at[k])

    def cot_copy(k):
        return pltpu.make_async_copy(cot_hbm.at[part(k)], cotv.at[part(k)], cot_sem.at[k])

    for k in range(chunks):
        x_copy(k).start()
    for k in range(chunks):
        cot_copy(k).start()

    lane = lax.broadcasted_iota(jnp.int32, (1, 128), 1)
    high = lane >= LAT
    own_half = high.astype(jnp.int32) == core

    def wide(block):
        return jnp.where(own_half, jnp.concatenate([block, block], axis=-1), 0.0).astype(BF16)

    conv_wide = wide(conv_ref[...])
    point_wide = wide(point_ref[...])
    for half in range(2):
        sixteen = slice(half * 16, half * 16 + 16)
        wsend[half, 0:9] = conv_wide[:, sixteen]
        wsend[half, 9] = point_wide[sixteen]

    barrier = pltpu.get_barrier_semaphore()
    partners = [core_peer, (dp, 3 - chan)]
    partners += xy_peer[1:] + z_peer[1:]
    for partner in partners:
        pl.semaphore_signal(barrier, inc=1, device_id=partner, device_id_type=MESH)
    pl.semaphore_wait(barrier, len(partners))

    pre = remote(wsend.at[other_core], wpre, ag_s.at[0, 0], ag_r.at[0, 0], core_peer)
    pre.start()

    def halo_copies(up_src, up_dst, down_src, down_dst, at):
        up = remote(up_src, up_dst, halo_s.at[at], halo_r.at[at], up_peer)
        down = remote(down_src, down_dst, halo_s.at[at + 1], halo_r.at[at + 1], down_peer)
        return up, down

    def halo_start(copies):
        @pl.when(chan > 0)
        def _():
            copies[0].start()

        @pl.when(chan < 3)
        def _():
            copies[1].start()

    def halo_wait_send(copies):
        @pl.when(chan > 0)
        def _():
            copies[0].wait_send()

        @pl.when(chan < 3)
        def _():
            copies[1].wait_send()

    def halo_wait_recv(copies):
        @pl.when(chan < 3)
        def _():
            copies[0].wait_recv()

        @pl.when(chan > 0)
        def _():
            copies[1].wait_recv()

    last_row = pl.ds((rows - 1) * PITCH, PITCH)
    x_halo = halo_copies(x_hbm.at[pl.ds(0, PITCH)], xhalo.at[1], x_hbm.at[last_row], xhalo.at[0], 0)
    halo_start(x_halo)

    @pl.when(chan == 0)
    def _():
        xhalo[0] = jnp.zeros(xhalo.shape[1:], BF16)

    @pl.when(chan == 3)
    def _():
        xhalo[1] = jnp.zeros(xhalo.shape[1:], BF16)

    def gather_buffer(p):
        return pb if isinstance(p, int) and p == 0 else wb.at[p - 1]

    def gather_z(p):
        block = gather_buffer(p).at[core, xc, yc, zc]
        return [remote(block, block, ag_s.at[p, k], ag_r.at[p, k], z_peer[k]) for k in (1, 2, 3)]

    def gather_xy(p):
        block = gather_buffer(p).at[core, xc, yc]
        return [remote(block, block, ag_s.at[p, 3 + k], ag_r.at[p, 3 + k], xy_peer[k]) for k in (1, 2, 3)]

    def gather_core(p):
        block = gather_buffer(p).at[core]
        return [remote(block, block, ag_s.at[p, 7], ag_r.at[p, 7], core_peer)]

    top = mask_ref[0:8, :].astype(F32).T
    for t in range(BANDS):
        col_mask[t] = jnp.broadcast_to(top[:, t : t + 1], (BAND, 128))

    def two(block):
        return jnp.concatenate([block, block], axis=1)

    def tile_mask(flags, n):
        return col_mask[n % BANDS] * flags[n : n + 1, 0:1]

    def row_flags(first_row, row_count):
        first = aligned(first_row * BANDS, 8)
        return mask_ref[pl.ds(first, row_count * BANDS), :].astype(F32)

    def shift_tile(block, valid, at):
        base = aligned(at, 16)
        act = jnp.maximum(block.astype(F32), 0.0) * two(valid)
        shifted[pl.ds(base, BAND), 256:512] = act.astype(BF16)
        before = pltpu.roll(act, 1, 0)
        shifted[pl.ds(base, BAND), 0:256] = before.astype(BF16)
        after = pltpu.roll(act, BAND - 1, 0)
        shifted[pl.ds(base, BAND), 512:768] = after.astype(BF16)

    def shift_rows(k, carry):
        flags = row_flags(chan * rows + k * 4, 4)
        for n in range(4 * BANDS):
            at = k * 4 * PITCH + n * BAND
            shift_tile(xv[pl.ds(aligned(at, 16), BAND), :], tile_mask(flags, n), at + PITCH)
        return carry

    x_copy(0).wait()
    lax.fori_loop(0, 2, shift_rows, 0)
    pre.wait_recv()
    joined = wsend[core] + wpre[...]
    for i in range(3):
        wb[i, core, xc, yc, zc] = joined[3 * i : 3 * i + 3]
    pb[core, xc, yc, zc, 0] = joined[9]
    quant = jnp.concatenate(
        [
            jnp.concatenate([dec_ref[...], proj_ref[...]], axis=1),
            jnp.concatenate([book_ref[0:8, :], book_ref[8:16, :]], axis=1),
        ],
        axis=0,
    )
    pb[core, xc, yc, zc, 1] = quant.astype(BF16)
    for p in range(4):
        start(gather_z(p))

    for k in range(1, chunks):
        x_copy(k).wait()
    lax.fori_loop(2, rows // 4, shift_rows, 0)
    landed(gather_z(0))
    start(gather_xy(0))
    halo_wait_recv(x_halo)

    def halo_row(side, at, global_row, present):
        group = row_flags(lax.div(jnp.maximum(global_row, 0), 4) * 4, 4)
        inside = 2 * (3 if side == 0 else 0)
        flags = group[inside : inside + 2] * present.astype(F32)
        for t in range(BANDS):
            shift_tile(xhalo[side, t * BAND : (t + 1) * BAND], tile_mask(flags, t), at + t * BAND)

    halo_row(0, 0, chan * rows - 1, chan > 0)
    halo_row(1, (rows + 1) * PITCH, jnp.minimum(chan * rows + rows, 3 * rows), chan < 3)

    landed(gather_z(1))
    start(gather_xy(1))
    landed(gather_z(2))
    start(gather_xy(2))
    landed(gather_z(3))
    start(gather_xy(3))

    point_acc[...] = jnp.zeros_like(point_acc)
    book_acc[...] = jnp.zeros_like(book_acc)
    loss_acc[...] = jnp.zeros_like(loss_acc)

    landed(gather_xy(0))
    start(gather_core(0))
    landed(gather_core(0))

    blocks = [(h, x, y, z) for z in range(4) for y in range(2) for x in range(2) for h in range(2)]
    for h, x, y, z in blocks:
        point_t[z * 64 + y * 32 + h * 16 : z * 64 + y * 32 + h * 16 + 16, x * 128 : x * 128 + 128] = pb[h, x, y, z, 0]
        owner = (2 * z + y) * 4 + 2 * x + h
        small = pb[h, x, y, z, 1].astype(F32)
        qf[owner * 8 : owner * 8 + 8, :] = small[0:8]
        bookf[owner * 16 : owner * 16 + 8, :] = pltpu.roll(small[8:16], LAT, 1)
        bookf[owner * 16 + 8 : owner * 16 + 16, :] = small[8:16]
    point_n[...] = point_t[...].T
    small = qf[...]
    decz[...] = jnp.where(high, 0.0, small).astype(BF16)
    projz[...] = jnp.where(high, small, 0.0).astype(BF16)
    dz_ref[...] = jnp.where(high, pltpu.roll(small, LAT, 1), 0.0).astype(BF16)
    proj_t[...] = jnp.where(high, 0.0, pltpu.roll(small, LAT, 1)).astype(BF16).T
    book_t[...] = jnp.where(high, bookf[...], 0.0).astype(BF16).T

    def onehot_t(k):
        entries = lax.broadcasted_iota(jnp.int32, (book_t.shape[1], CHUNK), 0)
        return (entries == ids_ref[k]).astype(F32).astype(BF16)

    def rows_of(k):
        return pl.ds(aligned(k * CHUNK, CHUNK), CHUNK)

    def valid_of(k):
        flags = row_flags(chan * rows + k * CHUNK_ROWS, CHUNK_ROWS)
        return jnp.concatenate([tile_mask(flags, n) for n in range(CHUNK_ROWS * BANDS)], axis=0)

    def decoder_chunk(k):
        kept = (cotv[rows_of(k), :].astype(F32) * two(valid_of(k))).astype(BF16)
        cotv[rows_of(k), :] = kept
        chosen = dot(book_t[...], onehot_t(k)).T
        both = chosen + dot(kept, decz[...])
        u_rows[rows_of(k), :] = both
        lg_rows[rows_of(k), :] = both.astype(BF16)

    def decoder_step(k, carry):
        cot_copy(k).wait()
        decoder_chunk(k)

        @pl.when(k < 3)
        def _():
            landed(gather_xy(k + 1))
            start(gather_core(k + 1))

        return carry

    lax.fori_loop(0, chunks, decoder_step, 0)
    ub_copy = pltpu.make_async_copy(lg_rows, ub_hbm, ub_sem)
    ub_copy.start()
    dec_acc[...] = dot_rows(lg_rows[...], cotv[...]).T

    for i in range(3):
        landed(gather_core(1 + i))
        for h, x, y, z in blocks:
            for j in range(3):
                first = j * 256 + z * 64 + y * 32 + h * 16
                wfull[i, first : first + 16, x * 128 : x * 128 + 128] = wb[i, h, x, y, z, j]
        for j in range(3):
            wback[i, :, j * 256 : j * 256 + 256] = wfull[i, j * 256 : j * 256 + 256, :].T

    def middle_chunk(k, carry):
        hidden = None
        for i in range(3):
            window = shifted[pl.ds(aligned((k * CHUNK_ROWS + i) * PITCH, PITCH), CHUNK), :]
            term = dot(window, wfull[i])
            hidden = term if hidden is None else hidden + term
        cotv[rows_of(k), :] = jnp.maximum(hidden, 0.0).astype(BF16)
        return carry

    def latent_chunk(k, carry):
        middle = cotv[rows_of(k), :]
        branch = dot(middle, point_n[...])
        summed = (xv[rows_of(k), :].astype(F32) + branch).astype(BF16)
        xv[rows_of(k), :] = summed
        valid = valid_of(k)
        gap = u_rows[rows_of(k), :] - dot(summed, projz[...])
        weighted = gap * valid
        loss_acc[...] += jnp.sum((weighted * gap).reshape(CHUNK // 8, 8, 128), axis=0)
        latent_grad = (gap - 0.5 * pltpu.roll(weighted, LAT, 1)).astype(BF16)
        lg_rows[rows_of(k), :] = latent_grad
        term = 2.0 * weighted
        coarse = term.astype(BF16).astype(F32)
        u_rows[rows_of(k), :] = jnp.where(high, coarse, pltpu.roll(term - coarse, LAT, 1))
        resid_low = dot(latent_grad, proj_t[...]).astype(BF16)
        point_acc[...] += dot_rows(resid_low, middle)
        back = dot(resid_low, point_t[...])
        hidden_grad = jnp.where(middle.astype(F32) > 0.0, back, 0.0).astype(BF16)
        hgp[pl.ds(aligned((k * CHUNK_ROWS + 1) * PITCH, PITCH), CHUNK), :] = hidden_grad
        hgt[:, pl.ds(aligned(k * CHUNK, CHUNK), CHUNK)] = hidden_grad.T
        return carry

    def book_chunk(k, carry):
        book_acc[...] += dot(onehot_t(k), u_rows[rows_of(k), :].astype(BF16))
        return carry

    lax.fori_loop(0, chunks, middle_chunk, 0)
    ub_copy.wait()
    lax.fori_loop(0, chunks, latent_chunk, 0)

    zero_row = jnp.zeros((PITCH, 256), BF16)

    @pl.when(chan == 0)
    def _():
        hgp[0:PITCH, :] = zero_row

    @pl.when(chan == 3)
    def _():
        hgp[(rows + 1) * PITCH : (rows + 2) * PITCH, :] = zero_row

    def grad_row(r):
        return hgp.at[pl.ds(r * PITCH, PITCH), :]

    hg_halo = halo_copies(grad_row(1), grad_row(rows + 1), grad_row(rows), grad_row(0), 2)
    halo_start(hg_halo)

    def reduce_buffers(p):
        if isinstance(p, int) and p == 0:
            return gp, rp0, rp1, rp2
        return gs.at[p - 1], rc0.at[p - 1], rc1.at[p - 1], rc2.at[p - 1]

    def reduce_core(p):
        buffer, first, _, _ = reduce_buffers(p)
        return [remote(buffer.at[other_core], first, rs_s.at[p, 0], rs_r.at[p, 0], core_peer)]

    def reduce_xy(p):
        buffer, _, second, _ = reduce_buffers(p)
        return [
            remote(buffer.at[core, *xy_of[k]], second.at[k - 1], rs_s.at[p, k], rs_r.at[p, k], xy_peer[k])
            for k in (1, 2, 3)
        ]

    def reduce_z(p):
        buffer, _, _, third = reduce_buffers(p)
        return [
            remote(
                buffer.at[core, xc, yc, z_of[k]], third.at[k - 1], rs_s.at[p, 3 + k], rs_r.at[p, 3 + k], z_peer[k]
            )
            for k in (1, 2, 3)
        ]

    def core_to_xy(p):
        landed(reduce_core(p))
        buffer, first, _, _ = reduce_buffers(p)
        buffer[core] = buffer[core] + first[...]
        start(reduce_xy(p))

    def xy_to_z(p):
        landed(reduce_xy(p))
        buffer, _, second, _ = reduce_buffers(p)
        buffer[core, xc, yc] = (buffer[core, xc, yc] + second[0]) + (second[1] + second[2])
        start(reduce_z(p))

    def reduce_end(p):
        landed(reduce_z(p))
        buffer, _, _, third = reduce_buffers(p)
        total = (buffer[core, xc, yc, zc] + third[0]) + (third[1] + third[2])
        if p == 0:
            q_ref[...] = total[16:40]
            fin[9] = total[0:16]
        else:
            for j in range(3):
                fin[3 * (p - 1) + j] = total[j * 16 : j * 16 + 16]

    def conv_grad(i):
        window = shifted[pl.ds(aligned(i * PITCH, PITCH), pixels), :]
        product = dot(hgt[...], window)
        for j in range(3):
            turned = product[:, j * 256 : j * 256 + 256].T
            for h, x, y, z in blocks:
                first = z * 64 + y * 32 + h * 16
                gs[i, h, x, y, z, j * 16 : j * 16 + 16] = turned[first : first + 16, x * 128 : x * 128 + 128]

    def pack_small():
        counts = mask_ref[pl.ds(aligned(chan * rows * BANDS, 8), rows * BANDS), :].astype(F32)
        counts = jnp.sum(counts.reshape(rows * BANDS // 8, 8, 128), axis=0)
        tallies = jnp.where(high, loss_acc[...], counts + pltpu.roll(counts, LAT, 1))
        heads = jnp.where(high, dec_acc[...], proj_acc[...])
        book_sum = book_acc[...] + pltpu.roll(book_acc[...], LAT, 1)
        for h, x, y, z in blocks:
            first = z * 64 + y * 32 + h * 16
            owner = (2 * z + y) * 4 + 2 * x + h
            gp[h, x, y, z, 0:16] = point_acc[first : first + 16, x * 128 : x * 128 + 128]
            gp[h, x, y, z, 16:24] = heads[owner * 8 : owner * 8 + 8]
            gp[h, x, y, z, 24:32] = jnp.where(
                high, book_sum[owner * 16 + 8 : owner * 16 + 16], book_sum[owner * 16 : owner * 16 + 8]
            )
            gp[h, x, y, z, 32:40] = tallies

    def grad_step(i, carry):
        conv_grad(i)
        start(reduce_core(i + 1))

        @pl.when(i == 0)
        def _():
            lax.fori_loop(0, chunks, book_chunk, 0)
            core_to_xy(1)

        @pl.when(i == 1)
        def _():
            proj_acc[...] = proj_sum()
            pack_small()
            start(reduce_core(0))
            core_to_xy(2)

        @pl.when(i == 2)
        def _():
            core_to_xy(0)
            xy_to_z(1)

        return carry

    def proj_sum():
        return dot_rows(lg_rows[...], xv[...]).T

    lax.fori_loop(0, 3, grad_step, 0)
    halo_wait_recv(hg_halo)

    def out_copy(k):
        return pltpu.make_async_copy(cotv.at[part(k)], ig_hbm.at[part(k)], out_sem.at[k])

    def back_chunk(k):
        back_grad = None
        for j in (1, 0, 2):
            total = None
            for i in range(3):
                window = hgp[pl.ds(aligned((k * CHUNK_ROWS + 2 - i) * PITCH, PITCH), CHUNK), :]
                term = dot(window, wback[i, :, j * 256 : j * 256 + 256])
                total = term if total is None else total + term
            if j != 1:
                total = pltpu.roll(total, CHUNK - 1 if j == 0 else 1, 0)
            back_grad = total if back_grad is None else back_grad + total
        centre = pl.ds(aligned((k * CHUNK_ROWS + 1) * PITCH, PITCH), CHUNK)
        slope = shifted[centre, 256:512].astype(F32) > 0.0
        resid = dot(lg_rows[rows_of(k), :], proj_t[...])
        cotv[rows_of(k), :] = (resid + jnp.where(slope, back_grad, 0.0)).astype(BF16)

    def back_step(k, carry):
        back_chunk(k)
        out_copy(k).start()

        @pl.when(k == 0)
        def _():
            core_to_xy(3)
            xy_to_z(2)
            reduce_end(1)

        @pl.when(k == 1)
        def _():
            xy_to_z(0)

        @pl.when(k == 2)
        def _():
            reduce_end(2)
            xy_to_z(3)

        return carry

    lax.fori_loop(0, chunks, back_step, 0)
    reduce_end(0)
    reduce_end(3)
    last = remote(fin, rx3, rs_s.at[0, 7], rs_r.at[0, 7], core_peer)
    last.start()
    last.wait_recv()
    mine, other = fin[...], rx3[...]
    is_first = core == 0
    lower = jnp.where(is_first, mine, other)
    upper = jnp.where(is_first, other, mine)
    whole = jnp.concatenate([lower, upper], axis=1)
    g_ref[...] = jnp.where(is_first, whole[..., 0:LAT], whole[..., LAT:])

    for k in range(chunks):
        out_copy(k).wait()
    halo_wait_send(x_halo)
    halo_wait_send(hg_halo)
    sent([pre, last])
    for p in range(4):
        sent(gather_z(p) + gather_xy(p) + gather_core(p))
        sent(reduce_core(p) + reduce_xy(p) + reduce_z(p))


def finish_kernel(
    ig_ref, ub_ref, mask_ref, dec_ref, g_ref, q_ref,
    conv_w, conv_m, conv_v, point_w, point_m, point_v, proj_w, proj_m, proj_v,
    code_w, code_m, code_v, dec_w, dec_m, dec_v,
    out_ref, grad_ref, loss_ref, *updates,
):
    step = pl.program_id(0)
    tiles = out_ref.shape[0] // BAND
    chan = lax.axis_index("chan")
    first = (chan * pl.num_programs(0) + step) * tiles
    flags = mask_ref[pl.ds(aligned(first, 8), tiles), :].astype(F32)
    top = mask_ref[0:8, :].astype(F32).T
    columns = [jnp.broadcast_to(top[:, t : t + 1], (BAND, 256)) for t in range(BANDS)]
    decoded = lax.dot_general(
        ub_ref[...], dec_ref[...], (((1,), (1,)), ((), ())), preferred_element_type=F32
    )
    for n in range(tiles):
        part = slice(n * BAND, (n + 1) * BAND)
        valid = columns[n % BANDS] * flags[n : n + 1, 0:1]
        out_ref[part, :] = (decoded[part] * valid).astype(BF16)
    grad_ref[...] = ig_ref[...]

    @pl.when(step == 0)
    def _():
        q = q_ref[...]
        heads, book = q[0:8], q[8:16]
        high = lax.broadcasted_iota(jnp.int32, (8, 128), 1) >= LAT
        gap = jnp.sum(jnp.where(high, q[16:24], 0.0))
        count = jnp.sum(jnp.where(high, 0.0, q[16:24]))
        ratio = jnp.full((8, 128), gap, F32) / jnp.full((8, 128), count * LAT, F32)
        loss_ref[0] = ratio[0, 0]
        loss_ref[1] = 0.25 * ratio[0, 0]
        sets = (
            (g_ref[0:9], conv_w, conv_m, conv_v, 0.01),
            (g_ref[9], point_w, point_m, point_v, 0.03),
            (heads[:, 0:LAT], proj_w, proj_m, proj_v, 0.03),
            (jnp.concatenate([book[:, 0:LAT], book[:, LAT:]], axis=0), code_w, code_m, code_v, 0.5),
            (heads[:, LAT:], dec_w, dec_m, dec_v, 0.06),
        )
        for n, (grad, weight, moment, square, rate) in enumerate(sets):
            results = adamw(grad, weight[...], moment[...], square[...], rate)
            for m in range(4):
                updates[4 * n + m][...] = results[m]


def vmem():
    return pl.BlockSpec(memory_space=pltpu.VMEM)


def anywhere():
    return pl.BlockSpec(memory_space=pl.ANY)


def on_device(
    inputs, valid_mask, code_ids, cotangent,
    conv_weight, conv_first, conv_second, point_weight, point_first, point_second,
    proj_weight, proj_first, proj_second, code_book, code_first, code_second,
    dec_weight, dec_first, dec_second,
):
    channels = inputs.shape[1]
    rows = inputs.shape[0] // PITCH
    chunks = rows // CHUNK_ROWS
    pixels = rows * PITCH
    padded = pixels + 2 * PITCH
    entries = 32 * code_book.shape[0]
    mask = valid_mask.reshape(-1, BAND)
    ids = code_ids.reshape(chunks, 1, CHUNK)
    point_weight, point_first, point_second = point_weight.T, point_first.T, point_second.T
    dma = pltpu.SemaphoreType.DMA
    ub, ig, grads, quant, decoder = pl.pallas_call(
        functools.partial(block_kernel, rows),
        out_shape=(
            jax.ShapeDtypeStruct((pixels, 128), BF16),
            jax.ShapeDtypeStruct((pixels, channels), BF16),
            jax.ShapeDtypeStruct((10, 32, LAT), F32),
            jax.ShapeDtypeStruct((24, 128), F32),
            jax.ShapeDtypeStruct((channels, 128), BF16),
        ),
        in_specs=[anywhere()] * 2 + [vmem()] * 7,
        out_specs=(anywhere(), anywhere(), vmem(), vmem(), vmem()),
        scratch_shapes=[
            pltpu.VMEM((pixels, channels), BF16),
            pltpu.VMEM((2, PITCH, channels), BF16),
            pltpu.VMEM((pixels, channels), BF16),
            pltpu.VMEM((padded, 3 * channels), BF16),
            pltpu.VMEM((BANDS, BAND, 128), F32),
            pltpu.VMEM((pixels, 128), F32),
            pltpu.VMEM((pixels, 128), BF16),
            pltpu.VMEM((padded, channels), BF16),
            pltpu.VMEM((channels, pixels), BF16),
            pltpu.VMEM((2, 10, 16, 128), BF16),
            pltpu.VMEM((10, 16, 128), BF16),
            pltpu.VMEM((3, 2, 2, 2, 4, 3, 16, 128), BF16),
            pltpu.VMEM((2, 2, 2, 4, 2, 16, 128), BF16),
            pltpu.VMEM((3, 3 * channels, channels), BF16),
            pltpu.VMEM((3, channels, 3 * channels), BF16),
            pltpu.VMEM((channels, channels), BF16),
            pltpu.VMEM((channels, channels), BF16),
            pltpu.VMEM((channels, 128), F32),
            pltpu.VMEM((entries, 128), F32),
            pltpu.VMEM((channels, 128), BF16),
            pltpu.VMEM((channels, 128), BF16),
            pltpu.VMEM((128, channels), BF16),
            pltpu.VMEM((128, entries), BF16),
            pltpu.VMEM((channels, 128), F32),
            pltpu.VMEM((channels, 128), F32),
            pltpu.VMEM((channels, channels), F32),
            pltpu.VMEM((entries, 128), F32),
            pltpu.VMEM((8, 128), F32),
            pltpu.VMEM((2, 2, 2, 4, 40, 128), F32),
            pltpu.VMEM((3, 2, 2, 2, 4, 48, 128), F32),
            pltpu.VMEM((2, 2, 4, 40, 128), F32),
            pltpu.VMEM((3, 4, 40, 128), F32),
            pltpu.VMEM((3, 40, 128), F32),
            pltpu.VMEM((3, 2, 2, 4, 48, 128), F32),
            pltpu.VMEM((3, 3, 4, 48, 128), F32),
            pltpu.VMEM((3, 3, 48, 128), F32),
            pltpu.VMEM((10, 16, 128), F32),
            pltpu.VMEM((10, 16, 128), F32),
            dma((chunks,)),
            dma((chunks,)),
            dma((chunks,)),
            dma(()),
            dma((4,)),
            dma((4,)),
            dma((4, 8)),
            dma((4, 8)),
            dma((4, 8)),
            dma((4, 8)),
        ],
        compiler_params=pltpu.CompilerParams(
            collective_id=0, has_side_effects=True, vmem_limit_bytes=62 * 2**20
        ),
        name="block",
    )(
        inputs, cotangent, ids, mask,
        conv_weight, point_weight, proj_weight, code_book, dec_weight,
    )

    states = (
        conv_weight, conv_first, conv_second, point_weight, point_first, point_second,
        proj_weight, proj_first, proj_second, code_book, code_first, code_second,
        dec_weight, dec_first, dec_second,
    )
    tiles = pl.BlockSpec((CHUNK, channels), lambda n: (n, 0))

    def whole(shape):
        return pl.BlockSpec(shape, lambda n: (0,) * len(shape))

    updates, specs = [], []
    for n in range(5):
        shape = states[3 * n].shape
        for kind in (F32, F32, F32, BF16):
            updates.append(jax.ShapeDtypeStruct(shape, kind))
            specs.append(whole(shape))
    results = pl.pallas_call(
        finish_kernel,
        grid=(chunks,),
        out_shape=(
            jax.ShapeDtypeStruct(inputs.shape, BF16),
            jax.ShapeDtypeStruct(inputs.shape, BF16),
            jax.ShapeDtypeStruct((2,), F32),
            *updates,
        ),
        in_specs=[
            tiles,
            pl.BlockSpec((CHUNK, 128), lambda n: (n, 0)),
            whole(mask.shape),
            whole(decoder.shape),
            whole(grads.shape),
            whole(quant.shape),
            *[whole(s.shape) for s in states],
        ],
        out_specs=(tiles, tiles, pl.BlockSpec(memory_space=pltpu.SMEM), *specs),
        compiler_params=pltpu.CompilerParams(vmem_limit_bytes=62 * 2**20),
        name="finish",
    )(ig, ub, mask, decoder, grads, quant, *states)
    point_new = tuple(block.T for block in results[7:11])
    return (*results[:7], *point_new, *results[11:])


def row_stride():
    return BANDS * BAND


def tap_offsets():
    stride = row_stride()
    return [row_step * stride + col_step for row_step in (-1, 0, 1) for col_step in (-1, 0, 1)]


def conv_forward(padded, weights, row_count):
    margin = row_stride() + 1
    summed_terms = None
    for tap_index, offset in enumerate(tap_offsets()):
        begin = margin + offset
        window = lax.slice_in_dim(padded, begin, begin + row_count, axis=0)
        product = jnp.dot(window, weights[tap_index], preferred_element_type=jnp.float32)
        summed_terms = product if summed_terms is None else summed_terms + product
    return summed_terms


def conv_weight_grad(padded, grads, row_count):
    margin = row_stride() + 1
    products = []
    for offset in tap_offsets():
        begin = margin + offset
        window = lax.slice_in_dim(padded, begin, begin + row_count, axis=0)
        products.append(
            lax.dot_general(
                window, grads, (((0,), (0,)), ((), ())), preferred_element_type=jnp.float32
            )
        )
    return jnp.stack(products)


def conv_input_grad(padded_grads, weights, row_count):
    margin = row_stride() + 1
    summed_terms = None
    for tap_index, offset in enumerate(tap_offsets()):
        begin = margin - offset
        window = lax.slice_in_dim(padded_grads, begin, begin + row_count, axis=0)
        product = lax.dot_general(
            window, weights[tap_index], (((1,), (1,)), ((), ())), preferred_element_type=jnp.float32
        )
        summed_terms = product if summed_terms is None else summed_terms + product
    return summed_terms


def bottleneck(latent, mask_rows, code_rows, cotangent, codebook, decoder):
    weight_rows = mask_rows.astype(jnp.float32)[:, None]
    entries = jnp.arange(codebook.shape[0], dtype=jnp.int32)
    onehot = (code_rows[:, None] == entries[None, :]).astype(jnp.bfloat16)
    chosen = jnp.dot(onehot, codebook, preferred_element_type=jnp.float32)
    gap_rows = latent - chosen
    loss_part = jnp.sum(weight_rows * gap_rows * gap_rows)
    count_part = jnp.sum(weight_rows)
    decoded = chosen.astype(jnp.bfloat16)
    decoded_out = lax.dot_general(
        decoded, decoder, (((1,), (1,)), ((), ())), preferred_element_type=jnp.float32
    )
    output = (decoded_out * weight_rows).astype(jnp.bfloat16)
    kept_rows = cotangent * mask_rows.astype(jnp.bfloat16)[:, None]
    decoded_grad = jnp.dot(kept_rows, decoder, preferred_element_type=jnp.float32)
    latent_grad = (decoded_grad + 0.5 * weight_rows * gap_rows).astype(jnp.bfloat16)
    decoder_grad = lax.dot_general(
        kept_rows, decoded, (((0,), (0,)), ((), ())), preferred_element_type=jnp.float32
    )
    book_term = -2.0 * weight_rows * gap_rows
    high_part = book_term.astype(jnp.bfloat16)
    rest_term = book_term - high_part.astype(jnp.float32)
    middle_part = rest_term.astype(jnp.bfloat16)
    low_part = (rest_term - middle_part.astype(jnp.float32)).astype(jnp.bfloat16)
    stacked = jnp.concatenate([high_part, middle_part, low_part], axis=1)
    book_parts = lax.dot_general(
        onehot, stacked, (((0,), (0,)), ((), ())), preferred_element_type=jnp.float32
    )
    width = book_term.shape[1]
    book_grad = book_parts[:, :width] + (
        book_parts[:, width : 2 * width] + book_parts[:, 2 * width :]
    )
    return (output, latent_grad, decoder_grad, book_grad, loss_part, count_part)


def general(
    inputs,
    valid_mask,
    code_ids,
    cotangent,
    conv_weight,
    conv_first,
    conv_second,
    point_weight,
    point_first,
    point_second,
    proj_weight,
    proj_first,
    proj_second,
    code_book,
    code_first,
    code_second,
    dec_weight,
    dec_first,
    dec_second,
):
    chan_count = lax.axis_size("chan")
    chan_index = lax.axis_index("chan")
    rows_quarter = inputs.shape[0]
    rows_all = valid_mask.shape[0]
    channels = inputs.shape[1]
    chan_width = channels // chan_count
    margin = row_stride() + 1
    conv_low, point_low = (
        lax.all_gather(conv_weight.astype(jnp.bfloat16), "dp", axis=1, tiled=True),
        lax.all_gather(point_weight.astype(jnp.bfloat16), "dp", axis=1, tiled=True),
    )
    proj_full, book_full, dec_full = (
        lax.all_gather(proj_weight.astype(jnp.bfloat16), ("dp", "chan"), axis=0, tiled=True),
        lax.all_gather(code_book.astype(jnp.bfloat16), ("dp", "chan"), axis=0, tiled=True),
        lax.all_gather(dec_weight.astype(jnp.bfloat16), ("dp", "chan"), axis=0, tiled=True),
    )
    mask_rows = lax.dynamic_slice_in_dim(valid_mask, chan_index * rows_quarter, rows_quarter)
    first_column = chan_index * chan_width
    gathered = lax.all_gather(inputs, "chan", axis=0, tiled=True)
    valid_all = (valid_mask > 0)[:, None]
    activations = jnp.where(valid_all, jnp.maximum(gathered, 0), 0)
    padded = jnp.pad(activations, ((margin, margin), (0, 0)))
    hidden = conv_forward(padded, conv_low, rows_all)
    middle = jnp.maximum(hidden, 0.0).astype(jnp.bfloat16)
    partial_branch = jnp.dot(middle, point_low, preferred_element_type=jnp.float32)
    branch = lax.psum_scatter(partial_branch, "chan", scatter_dimension=1, tiled=True)
    own_inputs = lax.dynamic_slice_in_dim(gathered, first_column, chan_width, 1).astype(jnp.float32)
    summed = (own_inputs + branch).astype(jnp.bfloat16)
    proj_rows = lax.dynamic_slice_in_dim(proj_full, first_column, chan_width, 0)
    window = summed
    latent = lax.psum_scatter(
        jnp.dot(window, proj_rows, preferred_element_type=jnp.float32),
        "chan",
        scatter_dimension=0,
        tiled=True,
    )
    output, latent_grad, decoder_grad, book_grad, loss_part, count_part = bottleneck(
        latent, mask_rows, code_ids, cotangent, book_full, dec_full
    )
    grads_all = lax.all_gather(latent_grad, "chan", axis=0, tiled=True)
    proj_part = lax.dot_general(
        summed, grads_all, (((0,), (0,)), ((), ())), preferred_element_type=jnp.float32
    )
    proj_grad = lax.dynamic_update_slice_in_dim(
        jnp.zeros((channels, proj_part.shape[1]), jnp.float32), proj_part, first_column, 0
    )
    resid = lax.dot_general(
        grads_all, proj_rows, (((1,), (1,)), ((), ())), preferred_element_type=jnp.float32
    )
    resid_all = lax.all_gather(resid.astype(jnp.bfloat16), "chan", axis=1, tiled=True)
    point_grad = lax.dot_general(
        middle, resid_all, (((0,), (0,)), ((), ())), preferred_element_type=jnp.float32
    )
    hidden_back = lax.dot_general(
        resid_all, point_low, (((1,), (1,)), ((), ())), preferred_element_type=jnp.float32
    )
    hidden_grad = jnp.where(hidden > 0.0, hidden_back.astype(jnp.bfloat16), 0)
    conv_grad = conv_weight_grad(padded, hidden_grad, rows_all)
    grad_padded = jnp.pad(hidden_grad, ((margin, margin), (0, 0)))
    slopes = jnp.logical_and(gathered > 0, valid_all)
    window = grad_padded
    back_grad = conv_input_grad(window, conv_low, rows_quarter * lax.axis_size("chan"))
    back_grad = jnp.where(slopes, back_grad, 0.0)
    own_back = lax.dynamic_slice_in_dim(back_grad, first_column, chan_width, 1)
    input_grad = lax.psum_scatter(
        lax.dynamic_update_slice_in_dim(back_grad, own_back + resid, first_column, 1),
        "chan",
        scatter_dimension=0,
        tiled=True,
    ).astype(jnp.bfloat16)
    conv_reduced, point_reduced = (
        lax.psum_scatter(conv_grad, "dp", scatter_dimension=1, tiled=True),
        lax.psum_scatter(point_grad, "dp", scatter_dimension=1, tiled=True),
    )
    proj_reduced, book_reduced, dec_reduced = (
        lax.psum_scatter(proj_grad, ("dp", "chan"), scatter_dimension=0, tiled=True),
        lax.psum_scatter(book_grad, ("dp", "chan"), scatter_dimension=0, tiled=True),
        lax.psum_scatter(decoder_grad, ("dp", "chan"), scatter_dimension=0, tiled=True),
    )
    loss_total, count_total = lax.psum((loss_part, count_part), ("dp", "chan"))
    losses = jnp.stack([loss_total, 0.25 * loss_total]) / (count_total * LAT)
    conv_out = adamw(conv_reduced, conv_weight, conv_first, conv_second, 0.01)
    point_out = adamw(point_reduced, point_weight, point_first, point_second, 0.03)
    proj_out = adamw(proj_reduced, proj_weight, proj_first, proj_second, 0.03)
    code_out = adamw(book_reduced, code_book, code_first, code_second, 0.5)
    dec_out = adamw(dec_reduced, dec_weight, dec_first, dec_second, 0.06)
    return (
        output,
        input_grad,
        losses,
        conv_out[0],
        conv_out[1],
        conv_out[2],
        conv_out[3],
        point_out[0],
        point_out[1],
        point_out[2],
        point_out[3],
        proj_out[0],
        proj_out[1],
        proj_out[2],
        proj_out[3],
        code_out[0],
        code_out[1],
        code_out[2],
        code_out[3],
        dec_out[0],
        dec_out[1],
        dec_out[2],
        dec_out[3],
    )


def solution(mesh):
    pixel = P(("dp", "chan"), None)
    conv, point = P(None, "dp", "chan"), P("chan", "dp")
    in_specs = (pixel, P("dp"), P(("dp", "chan")), pixel)
    in_specs += (conv,) * 3 + (point,) * 3 + (pixel,) * 9
    out_specs = (pixel, pixel, P()) + (conv,) * 4 + (point,) * 4 + (pixel,) * 12
    fits = mesh.shape["dp"] == 8 and mesh.shape["chan"] == 4
    body = on_device if fits else general
    return jax.shard_map(body, mesh=mesh, in_specs=in_specs, out_specs=out_specs, check_vma=False)
```

```python
import functools

import jax
import jax.numpy as jnp
from jax import lax
from jax.experimental import pallas as pl
from jax.experimental.pallas import tpu as pltpu
from jax.sharding import PartitionSpec as P

LAT = 64
BAND = 128
BANDS = 2
STEP = 5
PITCH = BANDS * BAND
CHUNK_ROWS = 8
CHUNK = CHUNK_ROWS * PITCH
BACK_ROWS = 4
BACK = BACK_ROWS * PITCH
MESH = pl.DeviceIdType.MESH
F32 = jnp.float32
BF16 = jnp.bfloat16

beta_first = 0.5
beta_second = 0.5
epsilon = 1e-08
decay_rate = 0.01


def adamw(grad, weight, first, second, rate):
    first_new = beta_first * first + (1.0 - beta_first) * grad
    second_new = beta_second * second + (1.0 - beta_second) * grad * grad
    first_hat = first_new / (1.0 - beta_first**STEP)
    second_hat = second_new / (1.0 - beta_second**STEP)
    weight_new = weight - rate * (
        first_hat / (jnp.sqrt(second_hat) + epsilon) + decay_rate * weight
    )
    return (weight_new, first_new, second_new, weight_new.astype(BF16))


def dot(a, b):
    return jnp.dot(a, b, preferred_element_type=F32)


def dot_rows(a, b):
    return lax.dot_general(a, b, (((0,), (0,)), ((), ())), preferred_element_type=F32)


def aligned(value, unit):
    return pl.multiple_of(value, unit)


def block_kernel(
    rows,
    x_hbm,
    cot_hbm,
    ids_hbm,
    mask_hbm,
    conv_hbm,
    point_hbm,
    proj_hbm,
    book_hbm,
    dec_hbm,
    ub_hbm,
    ig_hbm,
    g_ref,
    q_ref,
    dz_ref,
    ids_ref,
    mask_ref,
    conv_ref,
    point_ref,
    proj_ref,
    book_ref,
    dec_ref,
    xv,
    xhalo,
    cotv,
    shifted,
    col_mask,
    u_rows,
    lg_rows,
    hgp,
    hgt,
    wb,
    pb,
    qb,
    hidden_rows,
    wfull,
    wback,
    point_t,
    point_n,
    qf,
    bookf,
    decz,
    projz,
    proj_t,
    book_t,
    dec_acc,
    proj_acc,
    point_acc,
    book_acc,
    loss_acc,
    gp,
    gb,
    gs,
    rp0,
    rp1,
    rp2,
    rb0,
    rb1,
    rb2,
    rc0,
    rc1,
    rc2,
    small_sem,
    x_sem,
    cot_sem,
    out_sem,
    ub_sem,
    halo_s,
    halo_r,
    ag_s,
    ag_r,
    rs_s,
    rs_r,
):
    dp, chan = lax.axis_index("dp"), lax.axis_index("chan")
    core, xc = lax.rem(chan, 2), lax.div(chan, 2)
    yc, zc = lax.rem(dp, 2), lax.div(dp, 2)
    core_peer = (dp, chan + 1 - 2 * core)
    other_core = 1 - core
    xy_of = [(1 - xc if k % 2 else xc, 1 - yc if k // 2 else yc) for k in range(4)]
    xy_peer = [(2 * zc + y, 2 * x + core) for x, y in xy_of]
    z_of = [zc, zc + 1 - 2 * lax.rem(zc, 2), lax.rem(zc + 2, 4), 3 - zc]
    z_peer = [(2 * z + yc, chan) for z in z_of]
    up_peer, down_peer = (dp, chan - 1), (dp, chan + 1)
    chunks = rows // CHUNK_ROWS
    pixels = rows * PITCH
    def remote(src, dst, s_sem, r_sem, peer):
        return pltpu.make_async_remote_copy(
            src_ref=src, dst_ref=dst, send_sem=s_sem, recv_sem=r_sem, device_id=peer, device_id_type=MESH
        )

    def start(copies):
        for copy in copies:
            copy.start()

    def landed(copies):
        for copy in copies:
            copy.wait_recv()

    def sent(copies):
        for copy in copies:
            copy.wait_send()

    barrier = pltpu.get_barrier_semaphore()
    partners = [core_peer, (dp, 3 - chan)]
    partners += xy_peer[1:] + z_peer[1:]
    for partner in partners:
        pl.semaphore_signal(barrier, inc=1, device_id=partner, device_id_type=MESH)

    smalls = [
        pltpu.make_async_copy(src, dst, small_sem.at[n])
        for n, (src, dst) in enumerate(
            (
                (conv_hbm, conv_ref),
                (point_hbm, point_ref),
                (proj_hbm, proj_ref),
                (book_hbm, book_ref),
                (dec_hbm, dec_ref),
                (mask_hbm, mask_ref),
                (ids_hbm, ids_ref),
            )
        )
    ]
    for copy in smalls:
        copy.start()

    def part(k):
        return pl.ds(k * CHUNK, CHUNK)

    def x_copy(k):
        return pltpu.make_async_copy(x_hbm.at[part(k)], xv.at[part(k)], x_sem.at[k])

    def cot_copy(k):
        return pltpu.make_async_copy(cot_hbm.at[part(k)], cotv.at[part(k)], cot_sem.at[k])

    for k in range(chunks):
        x_copy(k).start()
    for k in range(chunks):
        cot_copy(k).start()

    lane = lax.broadcasted_iota(jnp.int32, (1, 128), 1)
    high = lane >= LAT

    def packed(block):
        return jnp.concatenate([block[..., 0:16, :], block[..., 16:32, :]], axis=-1).astype(BF16)

    for copy in smalls[0:5]:
        copy.wait()
    conv_own = packed(conv_ref[...])
    for i in range(3):
        wb[i, core, xc, yc, zc] = conv_own[3 * i : 3 * i + 3]
    pb[core, xc, yc, zc] = packed(point_ref[...])
    quant = jnp.concatenate(
        [
            jnp.concatenate([dec_ref[...], proj_ref[...]], axis=1),
            jnp.concatenate([book_ref[0:8, :], book_ref[8:16, :]], axis=1),
        ],
        axis=0,
    )
    qb[core, xc, yc, zc] = quant.astype(BF16)

    pl.semaphore_wait(barrier, len(partners))


    def halo_copies(up_src, up_dst, down_src, down_dst, at):
        up = remote(up_src, up_dst, halo_s.at[at], halo_r.at[at], up_peer)
        down = remote(down_src, down_dst, halo_s.at[at + 1], halo_r.at[at + 1], down_peer)
        return up, down

    def halo_start(copies):
        @pl.when(chan > 0)
        def _():
            copies[0].start()

        @pl.when(chan < 3)
        def _():
            copies[1].start()

    def halo_wait_send(copies):
        @pl.when(chan > 0)
        def _():
            copies[0].wait_send()

        @pl.when(chan < 3)
        def _():
            copies[1].wait_send()

    def halo_wait_recv(copies):
        @pl.when(chan < 3)
        def _():
            copies[0].wait_recv()

        @pl.when(chan > 0)
        def _():
            copies[1].wait_recv()

    last_row = pl.ds((rows - 1) * PITCH, PITCH)
    x_halo = halo_copies(x_hbm.at[pl.ds(0, PITCH)], xhalo.at[1], x_hbm.at[last_row], xhalo.at[0], 0)
    @pl.when(chan == 0)
    def _():
        xhalo[0] = jnp.zeros(xhalo.shape[1:], BF16)

    @pl.when(chan == 3)
    def _():
        xhalo[1] = jnp.zeros(xhalo.shape[1:], BF16)

    def gather_buffer(p):
        if isinstance(p, int) and p in (0, 4):
            return qb if p == 0 else pb
        return wb.at[p - 1]

    def gather_z(p):
        block = gather_buffer(p).at[core, xc, yc, zc]
        return [remote(block, block, ag_s.at[p, k], ag_r.at[p, k], z_peer[k]) for k in (1, 2, 3)]

    def gather_xy(p):
        block = gather_buffer(p).at[core, xc, yc]
        return [remote(block, block, ag_s.at[p, 3 + k], ag_r.at[p, 3 + k], xy_peer[k]) for k in (1, 2, 3)]

    def gather_core(p):
        block = gather_buffer(p).at[core]
        return [remote(block, block, ag_s.at[p, 7], ag_r.at[p, 7], core_peer)]

    for p in (0, 1, 2, 3, 4):
        start(gather_z(p))
    halo_start(x_halo)

    for copy in smalls[5:]:
        copy.wait()

    top = mask_ref[0:8, :].astype(F32).T
    for t in range(BANDS):
        col_mask[t] = jnp.broadcast_to(top[:, t : t + 1], (BAND, 128))

    def two(block):
        return jnp.concatenate([block, block], axis=1)

    def tile_mask(flags, n):
        return col_mask[n % BANDS] * flags[n : n + 1, 0:1]

    def row_flags(first_row, row_count):
        first = aligned(first_row * BANDS, 8)
        return mask_ref[pl.ds(first, row_count * BANDS), :].astype(F32)

    def shift_tile(block, valid, at):
        base = aligned(at, 16)
        act = jnp.maximum(block.astype(F32), 0.0) * two(valid)
        shifted[pl.ds(base, BAND), 256:512] = act.astype(BF16)
        before = pltpu.roll(act, 1, 0)
        shifted[pl.ds(base, BAND), 0:256] = before.astype(BF16)
        after = pltpu.roll(act, BAND - 1, 0)
        shifted[pl.ds(base, BAND), 512:768] = after.astype(BF16)

    def shift_rows(k, carry):
        flags = row_flags(chan * rows + k * 4, 4)
        for n in range(4 * BANDS):
            at = k * 4 * PITCH + n * BAND
            shift_tile(xv[pl.ds(aligned(at, 16), BAND), :], tile_mask(flags, n), at + PITCH)
        return carry

    x_copy(0).wait()
    lax.fori_loop(0, 2, shift_rows, 0)
    for k in range(1, chunks):
        x_copy(k).wait()
    lax.fori_loop(2, 5, shift_rows, 0)
    landed(gather_z(0))
    start(gather_xy(0))
    lax.fori_loop(5, rows // 4, shift_rows, 0)
    landed(gather_z(1))
    start(gather_xy(1))
    halo_wait_recv(x_halo)

    def halo_row(side, at, global_row, present):
        group = row_flags(lax.div(jnp.maximum(global_row, 0), 4) * 4, 4)
        inside = 2 * (3 if side == 0 else 0)
        flags = group[inside : inside + 2] * present.astype(F32)
        for t in range(BANDS):
            shift_tile(xhalo[side, t * BAND : (t + 1) * BAND], tile_mask(flags, t), at + t * BAND)

    halo_row(0, 0, chan * rows - 1, chan > 0)
    halo_row(1, (rows + 1) * PITCH, jnp.minimum(chan * rows + rows, 3 * rows), chan < 3)

    for p in (2, 3, 4):
        landed(gather_z(p))
        start(gather_xy(p))
    landed(gather_xy(0))
    start(gather_core(0))

    point_acc[...] = jnp.zeros_like(point_acc)
    book_acc[...] = jnp.zeros_like(book_acc)
    loss_acc[...] = jnp.zeros_like(loss_acc)
    landed(gather_core(0))

    squares = [(x, y, z) for z in range(4) for y in range(2) for x in range(2)]
    blocks = [(h, x, y, z) for x, y, z in squares for h in range(2)]

    def natural(first, second):
        lower = jnp.concatenate([first[:, 0:LAT], second[:, 0:LAT]], axis=1)
        upper = jnp.concatenate([first[:, LAT:], second[:, LAT:]], axis=1)
        return jnp.concatenate([lower, upper], axis=0)

    def by_core(tile):
        lower, upper = tile[0:16], tile[16:32]
        return jnp.where(high, pltpu.roll(upper, LAT, 1), lower), jnp.where(high, upper, pltpu.roll(lower, LAT, 1))

    for h, x, y, z in blocks:
        owner = (2 * z + y) * 4 + 2 * x + h
        small = qb[h, x, y, z].astype(F32)
        qf[owner * 8 : owner * 8 + 8, :] = small[0:8]
        bookf[owner * 16 : owner * 16 + 8, :] = pltpu.roll(small[8:16], LAT, 1)
        bookf[owner * 16 + 8 : owner * 16 + 16, :] = small[8:16]
    small = qf[...]
    decz[...] = jnp.where(high, 0.0, small).astype(BF16)
    projz[...] = jnp.where(high, small, 0.0).astype(BF16)
    dz_ref[...] = jnp.where(high, pltpu.roll(small, LAT, 1), 0.0).astype(BF16)
    proj_t[...] = jnp.where(high, 0.0, pltpu.roll(small, LAT, 1)).astype(BF16).T
    book_t[...] = jnp.where(high, bookf[...], 0.0).astype(BF16).T

    def onehot_t(k):
        entries = lax.broadcasted_iota(jnp.int32, (book_t.shape[1], CHUNK), 0)
        return (entries == ids_ref[k]).astype(F32).astype(BF16)

    def rows_of(k):
        return pl.ds(aligned(k * CHUNK, CHUNK), CHUNK)

    def valid_of(k):
        flags = row_flags(chan * rows + k * CHUNK_ROWS, CHUNK_ROWS)
        return jnp.concatenate([tile_mask(flags, n) for n in range(CHUNK_ROWS * BANDS)], axis=0)

    def decoder_chunk(k):
        kept = (cotv[rows_of(k), :].astype(F32) * two(valid_of(k))).astype(BF16)
        cotv[rows_of(k), :] = kept
        chosen = dot(book_t[...], onehot_t(k)).T
        both = chosen + dot(kept, decz[...])
        u_rows[rows_of(k), :] = both
        lg_rows[rows_of(k), :] = both.astype(BF16)

    def decoder_step(k, carry):
        cot_copy(k).wait()
        decoder_chunk(k)

        @pl.when(k == 2)
        def _():
            landed(gather_xy(1))
            start(gather_core(1))

        return carry

    lax.fori_loop(0, chunks, decoder_step, 0)
    ub_copy = pltpu.make_async_copy(lg_rows, ub_hbm, ub_sem)
    ub_copy.start()
    dec_acc[...] = dot_rows(lg_rows[...], cotv[...]).T

    def unpack_taps(i):
        landed(gather_core(1 + i))
        for x, y, z in squares:
            for j in range(3):
                first = j * 256 + z * 64 + y * 32
                wfull[i, first : first + 32, x * 128 : x * 128 + 128] = natural(wb[i, 0, x, y, z, j], wb[i, 1, x, y, z, j])
        for j in range(3):
            wback[i, :, j * 256 : j * 256 + 256] = wfull[i, j * 256 : j * 256 + 256, :].T

    def taps(k, i):
        window = shifted[pl.ds(aligned((k * CHUNK_ROWS + i) * PITCH, PITCH), CHUNK), :]
        return dot(window, wfull[i])

    def hidden_chunk(k, carry):
        hidden_rows[rows_of(k), :] = taps(k, 0)

        @pl.when(k == 0)
        def _():
            landed(gather_xy(2))
            start(gather_core(2))

        @pl.when(k == 1)
        def _():
            landed(gather_xy(3))
            start(gather_core(3))

        return carry

    def middle_chunk(k, carry):
        hidden = hidden_rows[rows_of(k), :] + (taps(k, 1) + taps(k, 2))
        cotv[rows_of(k), :] = jnp.maximum(hidden, 0.0).astype(BF16)

        @pl.when(k == 0)
        def _():
            landed(gather_xy(4))
            start(gather_core(4))

        return carry

    def whole_chunk(k, carry):
        hidden = taps(k, 0) + (taps(k, 1) + taps(k, 2))
        cotv[rows_of(k), :] = jnp.maximum(hidden, 0.0).astype(BF16)
        return carry

    def latent_chunk(k, carry):
        middle = cotv[rows_of(k), :]
        branch = dot(middle, point_n[...])
        summed = (xv[rows_of(k), :].astype(F32) + branch).astype(BF16)
        xv[rows_of(k), :] = summed
        valid = valid_of(k)
        gap = u_rows[rows_of(k), :] - dot(summed, projz[...])
        weighted = gap * valid
        loss_acc[...] += jnp.sum((weighted * gap).reshape(CHUNK // 8, 8, 128), axis=0)
        latent_grad = (gap - 0.5 * pltpu.roll(weighted, LAT, 1)).astype(BF16)
        lg_rows[rows_of(k), :] = latent_grad
        term = 2.0 * weighted
        coarse = term.astype(BF16).astype(F32)
        u_rows[rows_of(k), :] = jnp.where(high, coarse, pltpu.roll(term - coarse, LAT, 1))
        resid_low = dot(latent_grad, proj_t[...]).astype(BF16)
        point_acc[...] += dot_rows(resid_low, middle)
        back = dot(resid_low, point_t[...])
        hidden_grad = jnp.where(middle.astype(F32) > 0.0, back, 0.0).astype(BF16)
        hgp[pl.ds(aligned((k * CHUNK_ROWS + 1) * PITCH, PITCH), CHUNK), :] = hidden_grad
        hgt[:, pl.ds(aligned(k * CHUNK, CHUNK), CHUNK)] = hidden_grad.T
        return carry

    def book_chunk(k, carry):
        book_acc[...] += dot(onehot_t(k), u_rows[rows_of(k), :].astype(BF16))
        return carry

    unpack_taps(0)
    lax.fori_loop(0, chunks // 2, hidden_chunk, 0)
    unpack_taps(1)
    unpack_taps(2)
    lax.fori_loop(0, chunks // 2, middle_chunk, 0)
    lax.fori_loop(chunks // 2, chunks, whole_chunk, 0)
    landed(gather_core(4))
    for x, y, z in squares:
        first = z * 64 + y * 32
        point_t[first : first + 32, x * 128 : x * 128 + 128] = natural(pb[0, x, y, z], pb[1, x, y, z])
    point_n[...] = point_t[...].T
    ub_copy.wait()
    lax.fori_loop(0, chunks, latent_chunk, 0)

    zero_row = jnp.zeros((PITCH, 256), BF16)

    @pl.when(chan == 0)
    def _():
        hgp[0:PITCH, :] = zero_row

    @pl.when(chan == 3)
    def _():
        hgp[(rows + 1) * PITCH : (rows + 2) * PITCH, :] = zero_row

    def grad_row(r):
        return hgp.at[pl.ds(r * PITCH, PITCH), :]

    hg_halo = halo_copies(grad_row(1), grad_row(rows + 1), grad_row(rows), grad_row(0), 2)
    halo_start(hg_halo)

    def reduce_buffers(p):
        if isinstance(p, int) and p == 0:
            return gp, rp0, rp1, rp2
        if isinstance(p, int) and p == 4:
            return gb, rb0, rb1, rb2
        return gs.at[p - 1], rc0.at[p - 1], rc1.at[p - 1], rc2.at[p - 1]

    def reduce_core(p):
        buffer, first, _, _ = reduce_buffers(p)
        return [remote(buffer.at[other_core], first, rs_s.at[p, 0], rs_r.at[p, 0], core_peer)]

    def reduce_xy(p):
        buffer, _, second, _ = reduce_buffers(p)
        return [
            remote(buffer.at[core, *xy_of[k]], second.at[k - 1], rs_s.at[p, k], rs_r.at[p, k], xy_peer[k])
            for k in (1, 2, 3)
        ]

    def reduce_z(p):
        buffer, _, _, third = reduce_buffers(p)
        return [
            remote(
                buffer.at[core, xc, yc, z_of[k]], third.at[k - 1], rs_s.at[p, 3 + k], rs_r.at[p, 3 + k], z_peer[k]
            )
            for k in (1, 2, 3)
        ]

    def core_to_xy(p):
        landed(reduce_core(p))
        buffer, first, _, _ = reduce_buffers(p)
        buffer[core] = buffer[core] + first[...]
        start(reduce_xy(p))

    def xy_to_z(p):
        landed(reduce_xy(p))
        buffer, _, second, _ = reduce_buffers(p)
        buffer[core, xc, yc] = (buffer[core, xc, yc] + second[0]) + (second[1] + second[2])
        start(reduce_z(p))

    def reduce_end(p):
        landed(reduce_z(p))
        buffer, _, _, third = reduce_buffers(p)
        total = (buffer[core, xc, yc, zc] + third[0]) + (third[1] + third[2])
        if p == 0:
            q_ref[0:8] = total[16:24]
            q_ref[16:24] = total[24:32]
            g_ref[9] = total[0:16]
        elif p == 4:
            q_ref[8:16] = total
        else:
            for j in range(3):
                g_ref[3 * (p - 1) + j] = total[j * 16 : j * 16 + 16]

    def conv_grad(i):
        window = shifted[pl.ds(aligned(i * PITCH, PITCH), pixels), :]
        product = dot(hgt[...], window)
        for j in range(3):
            turned = product[:, j * 256 : j * 256 + 256].T
            for x, y, z in squares:
                first = z * 64 + y * 32
                halves = by_core(turned[first : first + 32, x * 128 : x * 128 + 128])
                for h in range(2):
                    gs[i, h, x, y, z, j * 16 : j * 16 + 16] = halves[h]

    def pack_small():
        counts = mask_ref[pl.ds(aligned(chan * rows * BANDS, 8), rows * BANDS), :].astype(F32)
        counts = jnp.sum(counts.reshape(rows * BANDS // 8, 8, 128), axis=0)
        tallies = jnp.where(high, loss_acc[...], counts + pltpu.roll(counts, LAT, 1))
        heads = jnp.where(high, dec_acc[...], proj_acc[...])
        for x, y, z in squares:
            first = z * 64 + y * 32
            halves = by_core(point_acc[first : first + 32, x * 128 : x * 128 + 128])
            for h in range(2):
                gp[h, x, y, z, 0:16] = halves[h]
        for h, x, y, z in blocks:
            owner = (2 * z + y) * 4 + 2 * x + h
            gp[h, x, y, z, 16:24] = heads[owner * 8 : owner * 8 + 8]
            gp[h, x, y, z, 24:32] = tallies

    def pack_book():
        book_sum = book_acc[...] + pltpu.roll(book_acc[...], LAT, 1)
        for h, x, y, z in blocks:
            first = ((2 * z + y) * 4 + 2 * x + h) * 16
            gb[h, x, y, z] = jnp.where(high, book_sum[first + 8 : first + 16], book_sum[first : first + 8])

    def grad_step(i, carry):
        conv_grad(i)
        start(reduce_core(i + 1))

        @pl.when(i == 0)
        def _():
            core_to_xy(0)

        @pl.when(i < 2)
        def _():
            lax.fori_loop(2 * i, 2 * i + 2, book_chunk, 0)
            core_to_xy(i + 1)

        return carry

    proj_acc[...] = dot_rows(lg_rows[...], xv[...]).T
    pack_small()
    start(reduce_core(0))
    lax.fori_loop(0, 3, grad_step, 0)
    pack_book()
    start(reduce_core(4))
    xy_to_z(0)
    xy_to_z(1)
    halo_wait_recv(hg_halo)

    def back_rows(k):
        return pl.ds(aligned(k * BACK, BACK), BACK)

    def out_copy(k):
        return pltpu.make_async_copy(cotv.at[back_rows(k)], ig_hbm.at[back_rows(k)], out_sem.at[k])

    def back_chunk(k):
        back_grad = None
        for j in (1, 0, 2):
            total = None
            for i in range(3):
                window = hgp[pl.ds(aligned((k * BACK_ROWS + 2 - i) * PITCH, PITCH), BACK), :]
                term = dot(window, wback[i, :, j * 256 : j * 256 + 256])
                total = term if total is None else total + term
            if j != 1:
                total = pltpu.roll(total, BACK - 1 if j == 0 else 1, 0)
            back_grad = total if back_grad is None else back_grad + total
        centre = pl.ds(aligned((k * BACK_ROWS + 1) * PITCH, PITCH), BACK)
        slope = shifted[centre, 256:512].astype(F32) > 0.0
        resid = dot(lg_rows[back_rows(k), :], proj_t[...])
        grad = resid + jnp.where(slope, back_grad, 0.0)
        cotv[back_rows(k), :] = grad.astype(BF16)

    steps = {
        0: [(core_to_xy, 3), (core_to_xy, 4)],
        1: [(reduce_end, 0)],
        2: [(xy_to_z, 2), (reduce_end, 1)],
        5: [(xy_to_z, 3), (xy_to_z, 4)],
        6: [(reduce_end, 2)],
    }

    def back_step(k, carry):
        back_chunk(k)
        out_copy(k).start()
        for at, todo in steps.items():

            @pl.when(k == at)
            def _():
                for act, p in todo:
                    act(p)

        return carry

    lax.fori_loop(0, rows // BACK_ROWS, back_step, 0)
    reduce_end(4)
    reduce_end(3)

    for k in range(rows // BACK_ROWS):
        out_copy(k).wait()
    halo_wait_send(x_halo)
    halo_wait_send(hg_halo)
    for p in range(5):
        sent(gather_z(p) + gather_xy(p) + gather_core(p))
        sent(reduce_core(p) + reduce_xy(p) + reduce_z(p))


def finish_kernel(tile, ig_hbm, ub_hbm, *refs):
    smalls, (out_hbm, grad_hbm, loss_ref), updates = refs[0:19], refs[19:22], refs[22:42]
    ub_rows, out_rows, ig_rows = refs[42:45]
    held, results = refs[45:64], refs[64:79]
    ub_sem, out_sem, ig_sem, grad_sem, in_sem, end_sem = refs[79:]
    tiles = ub_rows.shape[0] // tile

    def part(k):
        return pl.ds(k * tile, tile)

    def ub_copy(k):
        return pltpu.make_async_copy(ub_hbm.at[part(k)], ub_rows.at[part(k)], ub_sem.at[k])

    def ig_copy(k):
        return pltpu.make_async_copy(ig_hbm.at[part(k)], ig_rows.at[part(k)], ig_sem.at[k])

    def grad_copy(k):
        return pltpu.make_async_copy(ig_rows.at[part(k)], grad_hbm.at[part(k)], grad_sem.at[k])

    def out_copy(k):
        return pltpu.make_async_copy(out_rows.at[part(k)], out_hbm.at[part(k)], out_sem.at[k])

    arrive = [pltpu.make_async_copy(src, dst, in_sem.at[n]) for n, (src, dst) in enumerate(zip(smalls, held))]
    wide_updates = [ref for n, ref in enumerate(updates) if n % 4 < 3]
    leave = [pltpu.make_async_copy(src, dst, end_sem.at[n]) for n, (src, dst) in enumerate(zip(results, wide_updates))]
    for n in range(2):
        arrive[n].start()
    for k in range(tiles):
        ub_copy(k).start()
    for copy in arrive[2:]:
        copy.start()
    for k in range(tiles):
        ig_copy(k).start()
    mask_ref, dec_ref, g_ref, q_ref = held[0:4]
    arrive[0].wait()
    arrive[1].wait()
    chan = lax.axis_index("chan")
    top = mask_ref[0:8, :].astype(F32).T
    columns = [jnp.broadcast_to(top[:, t : t + 1], (BAND, 256)) for t in range(BANDS)]
    inner = tile // BAND

    def out_tile(k, carry):
        ub_copy(k).wait()
        here = pl.ds(aligned(k * tile, tile), tile)
        first = aligned((chan * tiles + k) * inner, 8)
        flags = mask_ref[pl.ds(first, inner), :].astype(F32)
        decoded = lax.dot_general(
            ub_rows[here, :], dec_ref[...], (((1,), (1,)), ((), ())), preferred_element_type=F32
        )
        valid = jnp.concatenate([columns[n % BANDS] * flags[n : n + 1, 0:1] for n in range(inner)], axis=0)
        out_rows[here, :] = (decoded * valid).astype(BF16)
        out_copy(k).start()
        ig_copy(k).wait()
        grad_copy(k).start()
        return carry

    lax.fori_loop(0, tiles, out_tile, 0)
    for copy in arrive[2:]:
        copy.wait()
    q = q_ref[...]
    heads, book = q[0:8], q[8:16]
    high = lax.broadcasted_iota(jnp.int32, (8, 128), 1) >= LAT
    gap = jnp.sum(jnp.where(high, q[16:24], 0.0))
    count = jnp.sum(jnp.where(high, 0.0, q[16:24]))
    ratio = jnp.full((8, 128), gap, F32) / jnp.full((8, 128), count * LAT, F32)
    loss_ref[0] = ratio[0, 0]
    loss_ref[1] = 0.25 * ratio[0, 0]
    blocks = jnp.concatenate([g_ref[..., 0:LAT], g_ref[..., LAT:]], axis=1)
    grads = (
        blocks[0:9],
        blocks[9],
        heads[:, 0:LAT],
        jnp.concatenate([book[:, 0:LAT], book[:, LAT:]], axis=0),
        heads[:, LAT:],
    )
    for n, rate in enumerate((0.01, 0.03, 0.03, 0.5, 0.06)):
        weight, moment, square = (ref[...] for ref in held[4 + 3 * n : 7 + 3 * n])
        *values, low = adamw(grads[n], weight, moment, square, rate)
        updates[4 * n + 3][...] = low
        for m, value in enumerate(values):
            results[3 * n + m][...] = value
            leave[3 * n + m].start()
    for copy in leave:
        copy.wait()
    for k in range(tiles):
        grad_copy(k).wait()
        out_copy(k).wait()


def vmem():
    return pl.BlockSpec(memory_space=pltpu.VMEM)


def anywhere():
    return pl.BlockSpec(memory_space=pl.ANY)


def on_device(
    inputs, valid_mask, code_ids, cotangent,
    conv_weight, conv_first, conv_second, point_weight, point_first, point_second,
    proj_weight, proj_first, proj_second, code_book, code_first, code_second,
    dec_weight, dec_first, dec_second,
):
    channels = inputs.shape[1]
    rows = inputs.shape[0] // PITCH
    chunks = rows // CHUNK_ROWS
    pixels = rows * PITCH
    padded = pixels + 2 * PITCH
    entries = 32 * code_book.shape[0]
    mask = valid_mask.reshape(-1, BAND)
    ids = code_ids.reshape(chunks, 1, CHUNK)
    point_weight, point_first, point_second = point_weight.T, point_first.T, point_second.T
    dma = pltpu.SemaphoreType.DMA
    ub, ig, grads, quant, decoder = pl.pallas_call(
        functools.partial(block_kernel, rows),
        out_shape=(
            jax.ShapeDtypeStruct((pixels, 128), BF16),
            jax.ShapeDtypeStruct((pixels, channels), BF16),
            jax.ShapeDtypeStruct((10, 16, 128), F32),
            jax.ShapeDtypeStruct((24, 128), F32),
            jax.ShapeDtypeStruct((channels, 128), BF16),
        ),
        in_specs=[anywhere()] * 9,
        out_specs=(anywhere(), anywhere(), vmem(), vmem(), vmem()),
        scratch_shapes=[
            pltpu.VMEM(ids.shape, jnp.int32),
            pltpu.VMEM(mask.shape, jnp.int32),
            *[pltpu.VMEM(block.shape, F32) for block in (conv_weight, point_weight, proj_weight, code_book, dec_weight)],
            pltpu.VMEM((pixels, channels), BF16),
            pltpu.VMEM((2, PITCH, channels), BF16),
            pltpu.VMEM((pixels, channels), BF16),
            pltpu.VMEM((padded, 3 * channels), BF16),
            pltpu.VMEM((BANDS, BAND, 128), F32),
            pltpu.VMEM((pixels, 128), F32),
            pltpu.VMEM((pixels, 128), BF16),
            pltpu.VMEM((padded, channels), BF16),
            pltpu.VMEM((channels, pixels), BF16),
            pltpu.VMEM((3, 2, 2, 2, 4, 3, 16, 128), BF16),
            pltpu.VMEM((2, 2, 2, 4, 16, 128), BF16),
            pltpu.VMEM((2, 2, 2, 4, 16, 128), BF16),
            pltpu.VMEM((pixels // 2, channels), F32),
            pltpu.VMEM((3, 3 * channels, channels), BF16),
            pltpu.VMEM((3, channels, 3 * channels), BF16),
            pltpu.VMEM((channels, channels), BF16),
            pltpu.VMEM((channels, channels), BF16),
            pltpu.VMEM((channels, 128), F32),
            pltpu.VMEM((entries, 128), F32),
            pltpu.VMEM((channels, 128), BF16),
            pltpu.VMEM((channels, 128), BF16),
            pltpu.VMEM((128, channels), BF16),
            pltpu.VMEM((128, entries), BF16),
            pltpu.VMEM((channels, 128), F32),
            pltpu.VMEM((channels, 128), F32),
            pltpu.VMEM((channels, channels), F32),
            pltpu.VMEM((entries, 128), F32),
            pltpu.VMEM((8, 128), F32),
            pltpu.VMEM((2, 2, 2, 4, 32, 128), F32),
            pltpu.VMEM((2, 2, 2, 4, 8, 128), F32),
            pltpu.VMEM((3, 2, 2, 2, 4, 48, 128), F32),
            pltpu.VMEM((2, 2, 4, 32, 128), F32),
            pltpu.VMEM((3, 4, 32, 128), F32),
            pltpu.VMEM((3, 32, 128), F32),
            pltpu.VMEM((2, 2, 4, 8, 128), F32),
            pltpu.VMEM((3, 4, 8, 128), F32),
            pltpu.VMEM((3, 8, 128), F32),
            pltpu.VMEM((3, 2, 2, 4, 48, 128), F32),
            pltpu.VMEM((3, 3, 4, 48, 128), F32),
            pltpu.VMEM((3, 3, 48, 128), F32),
            dma((7,)),
            dma((chunks,)),
            dma((chunks,)),
            dma((rows // BACK_ROWS,)),
            dma(()),
            dma((4,)),
            dma((4,)),
            dma((5, 8)),
            dma((5, 8)),
            dma((5, 8)),
            dma((5, 8)),
        ],
        compiler_params=pltpu.CompilerParams(
            collective_id=0, has_side_effects=True, vmem_limit_bytes=62 * 2**20
        ),
        name="block",
    )(
        inputs, cotangent, ids, mask,
        conv_weight, point_weight, proj_weight, code_book, dec_weight,
    )

    states = (
        conv_weight, conv_first, conv_second, point_weight, point_first, point_second,
        proj_weight, proj_first, proj_second, code_book, code_first, code_second,
        dec_weight, dec_first, dec_second,
    )
    updates = []
    for n in range(5):
        shape = states[3 * n].shape
        updates += [jax.ShapeDtypeStruct(shape, kind) for kind in (F32, F32, F32, BF16)]
    smalls = (mask, decoder, grads, quant, *states)
    tile = CHUNK
    tiles = pixels // tile
    results = pl.pallas_call(
        functools.partial(finish_kernel, tile),
        out_shape=(
            jax.ShapeDtypeStruct(inputs.shape, BF16),
            jax.ShapeDtypeStruct(inputs.shape, BF16),
            jax.ShapeDtypeStruct((2,), F32),
            *updates,
        ),
        in_specs=[anywhere()] * (2 + len(smalls)),
        out_specs=(anywhere(), anywhere(), pl.BlockSpec(memory_space=pltpu.SMEM), *[anywhere() if n % 4 < 3 else vmem() for n in range(20)]),
        scratch_shapes=[
            pltpu.VMEM((pixels, 128), BF16),
            pltpu.VMEM((pixels, channels), BF16),
            pltpu.VMEM((pixels, channels), BF16),
            *[pltpu.VMEM(block.shape, block.dtype) for block in smalls],
            *[pltpu.VMEM(block.shape, F32) for n, block in enumerate(updates) if n % 4 < 3],
            dma((tiles,)),
            dma((tiles,)),
            dma((tiles,)),
            dma((tiles,)),
            dma((len(smalls),)),
            dma((15,)),
        ],
        compiler_params=pltpu.CompilerParams(vmem_limit_bytes=61 * 2**20),
        name="finish",
    )(ig, ub, *smalls)
    point_new = tuple(block.T for block in results[7:11])
    return (*results[:7], *point_new, *results[11:])


def row_stride():
    return BANDS * BAND


def tap_offsets():
    stride = row_stride()
    return [row_step * stride + col_step for row_step in (-1, 0, 1) for col_step in (-1, 0, 1)]


def conv_forward(padded, weights, row_count):
    margin = row_stride() + 1
    summed_terms = None
    for tap_index, offset in enumerate(tap_offsets()):
        begin = margin + offset
        window = lax.slice_in_dim(padded, begin, begin + row_count, axis=0)
        product = jnp.dot(window, weights[tap_index], preferred_element_type=jnp.float32)
        summed_terms = product if summed_terms is None else summed_terms + product
    return summed_terms


def conv_weight_grad(padded, grads, row_count):
    margin = row_stride() + 1
    products = []
    for offset in tap_offsets():
        begin = margin + offset
        window = lax.slice_in_dim(padded, begin, begin + row_count, axis=0)
        products.append(
            lax.dot_general(
                window, grads, (((0,), (0,)), ((), ())), preferred_element_type=jnp.float32
            )
        )
    return jnp.stack(products)


def conv_input_grad(padded_grads, weights, row_count):
    margin = row_stride() + 1
    summed_terms = None
    for tap_index, offset in enumerate(tap_offsets()):
        begin = margin - offset
        window = lax.slice_in_dim(padded_grads, begin, begin + row_count, axis=0)
        product = lax.dot_general(
            window, weights[tap_index], (((1,), (1,)), ((), ())), preferred_element_type=jnp.float32
        )
        summed_terms = product if summed_terms is None else summed_terms + product
    return summed_terms


def bottleneck(latent, mask_rows, code_rows, cotangent, codebook, decoder):
    weight_rows = mask_rows.astype(jnp.float32)[:, None]
    entries = jnp.arange(codebook.shape[0], dtype=jnp.int32)
    onehot = (code_rows[:, None] == entries[None, :]).astype(jnp.bfloat16)
    chosen = jnp.dot(onehot, codebook, preferred_element_type=jnp.float32)
    gap_rows = latent - chosen
    loss_part = jnp.sum(weight_rows * gap_rows * gap_rows)
    count_part = jnp.sum(weight_rows)
    decoded = chosen.astype(jnp.bfloat16)
    decoded_out = lax.dot_general(
        decoded, decoder, (((1,), (1,)), ((), ())), preferred_element_type=jnp.float32
    )
    output = (decoded_out * weight_rows).astype(jnp.bfloat16)
    kept_rows = cotangent * mask_rows.astype(jnp.bfloat16)[:, None]
    decoded_grad = jnp.dot(kept_rows, decoder, preferred_element_type=jnp.float32)
    latent_grad = (decoded_grad + 0.5 * weight_rows * gap_rows).astype(jnp.bfloat16)
    decoder_grad = lax.dot_general(
        kept_rows, decoded, (((0,), (0,)), ((), ())), preferred_element_type=jnp.float32
    )
    book_term = -2.0 * weight_rows * gap_rows
    high_part = book_term.astype(jnp.bfloat16)
    rest_term = book_term - high_part.astype(jnp.float32)
    middle_part = rest_term.astype(jnp.bfloat16)
    low_part = (rest_term - middle_part.astype(jnp.float32)).astype(jnp.bfloat16)
    stacked = jnp.concatenate([high_part, middle_part, low_part], axis=1)
    book_parts = lax.dot_general(
        onehot, stacked, (((0,), (0,)), ((), ())), preferred_element_type=jnp.float32
    )
    width = book_term.shape[1]
    book_grad = book_parts[:, :width] + (
        book_parts[:, width : 2 * width] + book_parts[:, 2 * width :]
    )
    return (output, latent_grad, decoder_grad, book_grad, loss_part, count_part)


def general(
    inputs,
    valid_mask,
    code_ids,
    cotangent,
    conv_weight,
    conv_first,
    conv_second,
    point_weight,
    point_first,
    point_second,
    proj_weight,
    proj_first,
    proj_second,
    code_book,
    code_first,
    code_second,
    dec_weight,
    dec_first,
    dec_second,
):
    chan_count = lax.axis_size("chan")
    chan_index = lax.axis_index("chan")
    rows_quarter = inputs.shape[0]
    rows_all = valid_mask.shape[0]
    channels = inputs.shape[1]
    chan_width = channels // chan_count
    margin = row_stride() + 1
    conv_low, point_low = (
        lax.all_gather(conv_weight.astype(jnp.bfloat16), "dp", axis=1, tiled=True),
        lax.all_gather(point_weight.astype(jnp.bfloat16), "dp", axis=1, tiled=True),
    )
    proj_full, book_full, dec_full = (
        lax.all_gather(proj_weight.astype(jnp.bfloat16), ("dp", "chan"), axis=0, tiled=True),
        lax.all_gather(code_book.astype(jnp.bfloat16), ("dp", "chan"), axis=0, tiled=True),
        lax.all_gather(dec_weight.astype(jnp.bfloat16), ("dp", "chan"), axis=0, tiled=True),
    )
    mask_rows = lax.dynamic_slice_in_dim(valid_mask, chan_index * rows_quarter, rows_quarter)
    first_column = chan_index * chan_width
    gathered = lax.all_gather(inputs, "chan", axis=0, tiled=True)
    valid_all = (valid_mask > 0)[:, None]
    activations = jnp.where(valid_all, jnp.maximum(gathered, 0), 0)
    padded = jnp.pad(activations, ((margin, margin), (0, 0)))
    hidden = conv_forward(padded, conv_low, rows_all)
    middle = jnp.maximum(hidden, 0.0).astype(jnp.bfloat16)
    partial_branch = jnp.dot(middle, point_low, preferred_element_type=jnp.float32)
    branch = lax.psum_scatter(partial_branch, "chan", scatter_dimension=1, tiled=True)
    own_inputs = lax.dynamic_slice_in_dim(gathered, first_column, chan_width, 1).astype(jnp.float32)
    summed = (own_inputs + branch).astype(jnp.bfloat16)
    proj_rows = lax.dynamic_slice_in_dim(proj_full, first_column, chan_width, 0)
    window = summed
    latent = lax.psum_scatter(
        jnp.dot(window, proj_rows, preferred_element_type=jnp.float32),
        "chan",
        scatter_dimension=0,
        tiled=True,
    )
    output, latent_grad, decoder_grad, book_grad, loss_part, count_part = bottleneck(
        latent, mask_rows, code_ids, cotangent, book_full, dec_full
    )
    grads_all = lax.all_gather(latent_grad, "chan", axis=0, tiled=True)
    proj_part = lax.dot_general(
        summed, grads_all, (((0,), (0,)), ((), ())), preferred_element_type=jnp.float32
    )
    proj_grad = lax.dynamic_update_slice_in_dim(
        jnp.zeros((channels, proj_part.shape[1]), jnp.float32), proj_part, first_column, 0
    )
    resid = lax.dot_general(
        grads_all, proj_rows, (((1,), (1,)), ((), ())), preferred_element_type=jnp.float32
    )
    resid_all = lax.all_gather(resid.astype(jnp.bfloat16), "chan", axis=1, tiled=True)
    point_grad = lax.dot_general(
        middle, resid_all, (((0,), (0,)), ((), ())), preferred_element_type=jnp.float32
    )
    hidden_back = lax.dot_general(
        resid_all, point_low, (((1,), (1,)), ((), ())), preferred_element_type=jnp.float32
    )
    hidden_grad = jnp.where(hidden > 0.0, hidden_back.astype(jnp.bfloat16), 0)
    conv_grad = conv_weight_grad(padded, hidden_grad, rows_all)
    grad_padded = jnp.pad(hidden_grad, ((margin, margin), (0, 0)))
    slopes = jnp.logical_and(gathered > 0, valid_all)
    window = grad_padded
    back_grad = conv_input_grad(window, conv_low, rows_quarter * lax.axis_size("chan"))
    back_grad = jnp.where(slopes, back_grad, 0.0)
    own_back = lax.dynamic_slice_in_dim(back_grad, first_column, chan_width, 1)
    input_grad = lax.psum_scatter(
        lax.dynamic_update_slice_in_dim(back_grad, own_back + resid, first_column, 1),
        "chan",
        scatter_dimension=0,
        tiled=True,
    ).astype(jnp.bfloat16)
    conv_reduced, point_reduced = (
        lax.psum_scatter(conv_grad, "dp", scatter_dimension=1, tiled=True),
        lax.psum_scatter(point_grad, "dp", scatter_dimension=1, tiled=True),
    )
    proj_reduced, book_reduced, dec_reduced = (
        lax.psum_scatter(proj_grad, ("dp", "chan"), scatter_dimension=0, tiled=True),
        lax.psum_scatter(book_grad, ("dp", "chan"), scatter_dimension=0, tiled=True),
        lax.psum_scatter(decoder_grad, ("dp", "chan"), scatter_dimension=0, tiled=True),
    )
    loss_total, count_total = lax.psum((loss_part, count_part), ("dp", "chan"))
    losses = jnp.stack([loss_total, 0.25 * loss_total]) / (count_total * LAT)
    conv_out = adamw(conv_reduced, conv_weight, conv_first, conv_second, 0.01)
    point_out = adamw(point_reduced, point_weight, point_first, point_second, 0.03)
    proj_out = adamw(proj_reduced, proj_weight, proj_first, proj_second, 0.03)
    code_out = adamw(book_reduced, code_book, code_first, code_second, 0.5)
    dec_out = adamw(dec_reduced, dec_weight, dec_first, dec_second, 0.06)
    return (
        output,
        input_grad,
        losses,
        conv_out[0],
        conv_out[1],
        conv_out[2],
        conv_out[3],
        point_out[0],
        point_out[1],
        point_out[2],
        point_out[3],
        proj_out[0],
        proj_out[1],
        proj_out[2],
        proj_out[3],
        code_out[0],
        code_out[1],
        code_out[2],
        code_out[3],
        dec_out[0],
        dec_out[1],
        dec_out[2],
        dec_out[3],
    )


def solution(mesh):
    pixel = P(("dp", "chan"), None)
    conv, point = P(None, "dp", "chan"), P("chan", "dp")
    in_specs = (pixel, P("dp"), P(("dp", "chan")), pixel)
    in_specs += (conv,) * 3 + (point,) * 3 + (pixel,) * 9
    out_specs = (pixel, pixel, P()) + (conv,) * 4 + (point,) * 4 + (pixel,) * 12
    fits = mesh.shape["dp"] == 8 and mesh.shape["chan"] == 4
    body = on_device if fits else general
    return jax.shard_map(body, mesh=mesh, in_specs=in_specs, out_specs=out_specs, check_vma=False)
```

```python
import functools

import jax
import jax.numpy as jnp
from jax import lax
from jax.experimental import pallas as pl
from jax.experimental.pallas import tpu as pltpu
from jax.sharding import PartitionSpec as P

LAT = 64
BAND = 128
BANDS = 2
STEP = 5
PITCH = BANDS * BAND
CHUNK_ROWS = 8
CHUNK = CHUNK_ROWS * PITCH
BACK_ROWS = 4
BACK = BACK_ROWS * PITCH
MESH = pl.DeviceIdType.MESH
F32 = jnp.float32
BF16 = jnp.bfloat16

beta_first = 0.5
beta_second = 0.5
epsilon = 1e-08
decay_rate = 0.01


def adamw(grad, weight, first, second, rate):
    first_new = beta_first * first + (1.0 - beta_first) * grad
    second_new = beta_second * second + (1.0 - beta_second) * grad * grad
    first_hat = first_new / (1.0 - beta_first**STEP)
    second_hat = second_new / (1.0 - beta_second**STEP)
    weight_new = weight - rate * (
        first_hat / (jnp.sqrt(second_hat) + epsilon) + decay_rate * weight
    )
    return (weight_new, first_new, second_new, weight_new.astype(BF16))


def dot(a, b):
    return jnp.dot(a, b, preferred_element_type=F32)


def dot_rows(a, b):
    return lax.dot_general(a, b, (((0,), (0,)), ((), ())), preferred_element_type=F32)


def aligned(value, unit):
    return pl.multiple_of(value, unit)


def block_kernel(
    rows,
    x_hbm,
    cot_hbm,
    ids_hbm,
    mask_hbm,
    conv_hbm,
    point_hbm,
    proj_hbm,
    book_hbm,
    dec_hbm,
    ub_hbm,
    ig_hbm,
    g_ref,
    q_ref,
    dz_ref,
    ids_ref,
    mask_ref,
    conv_ref,
    point_ref,
    proj_ref,
    book_ref,
    dec_ref,
    xv,
    xhalo,
    cotv,
    shifted,
    col_mask,
    u_rows,
    lg_rows,
    hgp,
    hgt,
    wb,
    pb,
    qb,
    wfull,
    wback,
    point_t,
    point_n,
    qf,
    bookf,
    decz,
    projz,
    proj_t,
    book_t,
    dec_acc,
    proj_acc,
    point_acc,
    book_acc,
    loss_acc,
    gp,
    gb,
    gs,
    rp0,
    rp1,
    rp2,
    rb0,
    rb1,
    rb2,
    rc0,
    rc1,
    rc2,
    small_sem,
    x_sem,
    cot_sem,
    out_sem,
    ub_sem,
    halo_s,
    halo_r,
    ag_s,
    ag_r,
    rs_s,
    rs_r,
):
    dp, chan = lax.axis_index("dp"), lax.axis_index("chan")
    core, xc = lax.rem(chan, 2), lax.div(chan, 2)
    yc, zc = lax.rem(dp, 2), lax.div(dp, 2)
    core_peer = (dp, chan + 1 - 2 * core)
    other_core = 1 - core
    xy_of = [(1 - xc if k % 2 else xc, 1 - yc if k // 2 else yc) for k in range(4)]
    xy_peer = [(2 * zc + y, 2 * x + core) for x, y in xy_of]
    z_of = [zc, zc + 1 - 2 * lax.rem(zc, 2), lax.rem(zc + 2, 4), 3 - zc]
    z_peer = [(2 * z + yc, chan) for z in z_of]
    up_peer, down_peer = (dp, chan - 1), (dp, chan + 1)
    chunks = rows // CHUNK_ROWS
    pixels = rows * PITCH
    def remote(src, dst, s_sem, r_sem, peer):
        return pltpu.make_async_remote_copy(
            src_ref=src, dst_ref=dst, send_sem=s_sem, recv_sem=r_sem, device_id=peer, device_id_type=MESH
        )

    def start(copies):
        for copy in copies:
            copy.start()

    def landed(copies):
        for copy in copies:
            copy.wait_recv()

    def sent(copies):
        for copy in copies:
            copy.wait_send()

    barrier = pltpu.get_barrier_semaphore()
    partners = [core_peer, (dp, 3 - chan)]
    partners += xy_peer[1:] + z_peer[1:]
    for partner in partners:
        pl.semaphore_signal(barrier, inc=1, device_id=partner, device_id_type=MESH)

    smalls = [
        pltpu.make_async_copy(src, dst, small_sem.at[n])
        for n, (src, dst) in enumerate(
            (
                (conv_hbm, conv_ref),
                (point_hbm, point_ref),
                (proj_hbm, proj_ref),
                (book_hbm, book_ref),
                (dec_hbm, dec_ref),
                (mask_hbm, mask_ref),
                (ids_hbm, ids_ref),
            )
        )
    ]
    for copy in smalls:
        copy.start()

    def part(k):
        return pl.ds(k * CHUNK, CHUNK)

    def x_copy(k):
        return pltpu.make_async_copy(x_hbm.at[part(k)], xv.at[part(k)], x_sem.at[k])

    def cot_copy(k):
        return pltpu.make_async_copy(cot_hbm.at[part(k)], cotv.at[part(k)], cot_sem.at[k])

    for k in range(chunks):
        x_copy(k).start()
    for k in range(chunks):
        cot_copy(k).start()

    lane = lax.broadcasted_iota(jnp.int32, (1, 128), 1)
    high = lane >= LAT

    def packed(block):
        return jnp.concatenate([block[..., 0:16, :], block[..., 16:32, :]], axis=-1).astype(BF16)

    for copy in smalls[0:5]:
        copy.wait()
    conv_own = packed(conv_ref[...])
    for i in range(3):
        wb[i, core, xc, yc, zc] = conv_own[3 * i : 3 * i + 3]
    pb[core, xc, yc, zc] = packed(point_ref[...])
    quant = jnp.concatenate(
        [
            jnp.concatenate([dec_ref[...], proj_ref[...]], axis=1),
            jnp.concatenate([book_ref[0:8, :], book_ref[8:16, :]], axis=1),
        ],
        axis=0,
    )
    qb[core, xc, yc, zc] = quant.astype(BF16)

    pl.semaphore_wait(barrier, len(partners))


    def halo_copies(up_src, up_dst, down_src, down_dst, at):
        up = remote(up_src, up_dst, halo_s.at[at], halo_r.at[at], up_peer)
        down = remote(down_src, down_dst, halo_s.at[at + 1], halo_r.at[at + 1], down_peer)
        return up, down

    def halo_start(copies):
        @pl.when(chan > 0)
        def _():
            copies[0].start()

        @pl.when(chan < 3)
        def _():
            copies[1].start()

    def halo_wait_send(copies):
        @pl.when(chan > 0)
        def _():
            copies[0].wait_send()

        @pl.when(chan < 3)
        def _():
            copies[1].wait_send()

    def halo_wait_recv(copies):
        @pl.when(chan < 3)
        def _():
            copies[0].wait_recv()

        @pl.when(chan > 0)
        def _():
            copies[1].wait_recv()

    last_row = pl.ds((rows - 1) * PITCH, PITCH)
    x_halo = halo_copies(x_hbm.at[pl.ds(0, PITCH)], xhalo.at[1], x_hbm.at[last_row], xhalo.at[0], 0)
    @pl.when(chan == 0)
    def _():
        xhalo[0] = jnp.zeros(xhalo.shape[1:], BF16)

    @pl.when(chan == 3)
    def _():
        xhalo[1] = jnp.zeros(xhalo.shape[1:], BF16)

    def gather_buffer(p):
        if isinstance(p, int) and p in (0, 4):
            return qb if p == 0 else pb
        return wb.at[p - 1]

    def gather_z(p):
        buffer = gather_buffer(p)
        block = buffer.at[core, :, :, zc] if p == 3 else buffer.at[core, xc, yc, zc]
        return [remote(block, block, ag_s.at[p, k], ag_r.at[p, k], z_peer[k]) for k in (1, 2, 3)]

    def gather_xy(p):
        buffer = gather_buffer(p)
        block = buffer.at[core, xc, yc, zc] if p == 3 else buffer.at[core, xc, yc]
        return [remote(block, block, ag_s.at[p, 3 + k], ag_r.at[p, 3 + k], xy_peer[k]) for k in (1, 2, 3)]

    def gather_core(p):
        block = gather_buffer(p).at[core]
        return [remote(block, block, ag_s.at[p, 7], ag_r.at[p, 7], core_peer)]

    start(gather_z(0))
    start(gather_xy(3))
    for p in (1, 2, 4):
        start(gather_z(p))
    halo_start(x_halo)

    for copy in smalls[5:]:
        copy.wait()

    top = mask_ref[0:8, :].astype(F32).T
    for t in range(BANDS):
        col_mask[t] = jnp.broadcast_to(top[:, t : t + 1], (BAND, 128))

    def two(block):
        return jnp.concatenate([block, block], axis=1)

    def tile_mask(flags, n):
        return col_mask[n % BANDS] * flags[n : n + 1, 0:1]

    def row_flags(first_row, row_count):
        first = aligned(first_row * BANDS, 8)
        return mask_ref[pl.ds(first, row_count * BANDS), :].astype(F32)

    def shift_tile(block, valid, at):
        base = aligned(at, 16)
        act = jnp.maximum(block.astype(F32), 0.0) * two(valid)
        shifted[pl.ds(base, BAND), 256:512] = act.astype(BF16)
        before = pltpu.roll(act, 1, 0)
        shifted[pl.ds(base, BAND), 0:256] = before.astype(BF16)
        after = pltpu.roll(act, BAND - 1, 0)
        shifted[pl.ds(base, BAND), 512:768] = after.astype(BF16)

    def shift_rows(k, carry):
        flags = row_flags(chan * rows + k * 4, 4)
        for n in range(4 * BANDS):
            at = k * 4 * PITCH + n * BAND
            shift_tile(xv[pl.ds(aligned(at, 16), BAND), :], tile_mask(flags, n), at + PITCH)
        return carry

    x_copy(0).wait()
    lax.fori_loop(0, 2, shift_rows, 0)
    for k in range(1, chunks):
        x_copy(k).wait()
    lax.fori_loop(2, 5, shift_rows, 0)
    landed(gather_z(0))
    start(gather_xy(0))
    landed(gather_xy(3))
    start(gather_z(3))
    lax.fori_loop(5, rows // 4, shift_rows, 0)
    landed(gather_z(1))
    start(gather_xy(1))
    halo_wait_recv(x_halo)

    def halo_row(side, at, global_row, present):
        group = row_flags(lax.div(jnp.maximum(global_row, 0), 4) * 4, 4)
        inside = 2 * (3 if side == 0 else 0)
        flags = group[inside : inside + 2] * present.astype(F32)
        for t in range(BANDS):
            shift_tile(xhalo[side, t * BAND : (t + 1) * BAND], tile_mask(flags, t), at + t * BAND)

    halo_row(0, 0, chan * rows - 1, chan > 0)
    halo_row(1, (rows + 1) * PITCH, jnp.minimum(chan * rows + rows, 3 * rows), chan < 3)

    landed(gather_z(2))
    start(gather_xy(2))
    landed(gather_xy(0))
    start(gather_core(0))
    landed(gather_z(4))
    start(gather_xy(4))

    point_acc[...] = jnp.zeros_like(point_acc)
    book_acc[...] = jnp.zeros_like(book_acc)
    loss_acc[...] = jnp.zeros_like(loss_acc)
    landed(gather_core(0))

    squares = [(x, y, z) for z in range(4) for y in range(2) for x in range(2)]
    blocks = [(h, x, y, z) for x, y, z in squares for h in range(2)]

    def natural(first, second):
        lower = jnp.concatenate([first[:, 0:LAT], second[:, 0:LAT]], axis=1)
        upper = jnp.concatenate([first[:, LAT:], second[:, LAT:]], axis=1)
        return jnp.concatenate([lower, upper], axis=0)

    def by_core(tile):
        lower, upper = tile[0:16], tile[16:32]
        return jnp.where(high, pltpu.roll(upper, LAT, 1), lower), jnp.where(high, upper, pltpu.roll(lower, LAT, 1))

    for h, x, y, z in blocks:
        owner = (2 * z + y) * 4 + 2 * x + h
        small = qb[h, x, y, z].astype(F32)
        qf[owner * 8 : owner * 8 + 8, :] = small[0:8]
        bookf[owner * 16 : owner * 16 + 8, :] = pltpu.roll(small[8:16], LAT, 1)
        bookf[owner * 16 + 8 : owner * 16 + 16, :] = small[8:16]
    small = qf[...]
    decz[...] = jnp.where(high, 0.0, small).astype(BF16)
    projz[...] = jnp.where(high, small, 0.0).astype(BF16)
    dz_ref[...] = jnp.where(high, pltpu.roll(small, LAT, 1), 0.0).astype(BF16)
    proj_t[...] = jnp.where(high, 0.0, pltpu.roll(small, LAT, 1)).astype(BF16).T
    book_t[...] = jnp.where(high, bookf[...], 0.0).astype(BF16).T

    def onehot_t(k):
        entries = lax.broadcasted_iota(jnp.int32, (book_t.shape[1], CHUNK), 0)
        return (entries == ids_ref[k]).astype(F32).astype(BF16)

    def rows_of(k):
        return pl.ds(aligned(k * CHUNK, CHUNK), CHUNK)

    def valid_of(k):
        flags = row_flags(chan * rows + k * CHUNK_ROWS, CHUNK_ROWS)
        return jnp.concatenate([tile_mask(flags, n) for n in range(CHUNK_ROWS * BANDS)], axis=0)

    def decoder_chunk(k):
        kept = (cotv[rows_of(k), :].astype(F32) * two(valid_of(k))).astype(BF16)
        cotv[rows_of(k), :] = kept
        chosen = dot(book_t[...], onehot_t(k)).T
        both = chosen + dot(kept, decz[...])
        u_rows[rows_of(k), :] = both
        lg_rows[rows_of(k), :] = both.astype(BF16)

    def decoder_step(k, carry):
        cot_copy(k).wait()
        decoder_chunk(k)

        @pl.when(k == 2)
        def _():
            landed(gather_xy(1))
            start(gather_core(1))

        @pl.when(k == 3)
        def _():
            landed(gather_z(3))
            start(gather_core(3))

        return carry

    lax.fori_loop(0, chunks, decoder_step, 0)
    ub_copy = pltpu.make_async_copy(lg_rows, ub_hbm, ub_sem)
    ub_copy.start()
    dec_acc[...] = dot_rows(lg_rows[...], cotv[...]).T

    def unpack_taps(i):
        landed(gather_core(1 + i))
        for x, y, z in squares:
            for j in range(3):
                first = j * 256 + z * 64 + y * 32
                wfull[i, first : first + 32, x * 128 : x * 128 + 128] = natural(wb[i, 0, x, y, z, j], wb[i, 1, x, y, z, j])
        for j in range(3):
            wback[i, :, j * 256 : j * 256 + 256] = wfull[i, j * 256 : j * 256 + 256, :].T

    def taps(k, i):
        window = shifted[pl.ds(aligned((k * CHUNK_ROWS + i) * PITCH, PITCH), CHUNK), :]
        return dot(window, wfull[i])

    def middle_chunk(k, carry):
        hidden = taps(k, 0) + (taps(k, 1) + taps(k, 2))
        cotv[rows_of(k), :] = jnp.maximum(hidden, 0.0).astype(BF16)

        @pl.when(k == 0)
        def _():
            landed(gather_xy(4))
            start(gather_core(4))

        return carry

    def latent_chunk(k, carry):
        middle = cotv[rows_of(k), :]
        branch = dot(middle, point_n[...])
        summed = (xv[rows_of(k), :].astype(F32) + branch).astype(BF16)
        xv[rows_of(k), :] = summed
        valid = valid_of(k)
        gap = u_rows[rows_of(k), :] - dot(summed, projz[...])
        weighted = gap * valid
        loss_acc[...] += jnp.sum((weighted * gap).reshape(CHUNK // 8, 8, 128), axis=0)
        latent_grad = (gap - 0.5 * pltpu.roll(weighted, LAT, 1)).astype(BF16)
        lg_rows[rows_of(k), :] = latent_grad
        term = 2.0 * weighted
        coarse = term.astype(BF16).astype(F32)
        u_rows[rows_of(k), :] = jnp.where(high, coarse, pltpu.roll(term - coarse, LAT, 1))
        resid_low = dot(latent_grad, proj_t[...]).astype(BF16)
        point_acc[...] += dot_rows(resid_low, middle)
        back = dot(resid_low, point_t[...])
        hidden_grad = jnp.where(middle.astype(F32) > 0.0, back, 0.0).astype(BF16)
        hgp[pl.ds(aligned((k * CHUNK_ROWS + 1) * PITCH, PITCH), CHUNK), :] = hidden_grad
        hgt[:, pl.ds(aligned(k * CHUNK, CHUNK), CHUNK)] = hidden_grad.T
        return carry

    def book_chunk(k, carry):
        book_acc[...] += dot(onehot_t(k), u_rows[rows_of(k), :].astype(BF16))
        return carry

    landed(gather_xy(2))
    start(gather_core(2))
    for i in (0, 2, 1):
        unpack_taps(i)
    lax.fori_loop(0, chunks, middle_chunk, 0)
    landed(gather_core(4))
    for x, y, z in squares:
        first = z * 64 + y * 32
        point_t[first : first + 32, x * 128 : x * 128 + 128] = natural(pb[0, x, y, z], pb[1, x, y, z])
    point_n[...] = point_t[...].T
    ub_copy.wait()
    lax.fori_loop(0, chunks, latent_chunk, 0)

    zero_row = jnp.zeros((PITCH, 256), BF16)

    @pl.when(chan == 0)
    def _():
        hgp[0:PITCH, :] = zero_row

    @pl.when(chan == 3)
    def _():
        hgp[(rows + 1) * PITCH : (rows + 2) * PITCH, :] = zero_row

    def grad_row(r):
        return hgp.at[pl.ds(r * PITCH, PITCH), :]

    hg_halo = halo_copies(grad_row(1), grad_row(rows + 1), grad_row(rows), grad_row(0), 2)
    halo_start(hg_halo)

    def reduce_buffers(p):
        if isinstance(p, int) and p == 0:
            return gp, rp0, rp1, rp2
        if isinstance(p, int) and p == 4:
            return gb, rb0, rb1, rb2
        return gs.at[p - 1], rc0.at[p - 1], rc1.at[p - 1], rc2.at[p - 1]

    def reduce_core(p):
        buffer, first, _, _ = reduce_buffers(p)
        return [remote(buffer.at[other_core], first, rs_s.at[p, 0], rs_r.at[p, 0], core_peer)]

    def reduce_xy(p):
        buffer, _, second, _ = reduce_buffers(p)
        return [
            remote(buffer.at[core, *xy_of[k]], second.at[k - 1], rs_s.at[p, k], rs_r.at[p, k], xy_peer[k])
            for k in (1, 2, 3)
        ]

    def reduce_z(p):
        buffer, _, _, third = reduce_buffers(p)
        return [
            remote(
                buffer.at[core, xc, yc, z_of[k]], third.at[k - 1], rs_s.at[p, 3 + k], rs_r.at[p, 3 + k], z_peer[k]
            )
            for k in (1, 2, 3)
        ]

    def core_to_xy(p):
        landed(reduce_core(p))
        buffer, first, _, _ = reduce_buffers(p)
        buffer[core] = buffer[core] + first[...]
        start(reduce_xy(p))

    def xy_to_z(p):
        landed(reduce_xy(p))
        buffer, _, second, _ = reduce_buffers(p)
        buffer[core, xc, yc] = (buffer[core, xc, yc] + second[0]) + (second[1] + second[2])
        start(reduce_z(p))

    def reduce_end(p):
        landed(reduce_z(p))
        buffer, _, _, third = reduce_buffers(p)
        total = (buffer[core, xc, yc, zc] + third[0]) + (third[1] + third[2])
        if p == 0:
            q_ref[0:8] = total[16:24]
            q_ref[16:24] = total[24:32]
            g_ref[9] = total[0:16]
        elif p == 4:
            q_ref[8:16] = total
        else:
            for j in range(3):
                g_ref[3 * (p - 1) + j] = total[j * 16 : j * 16 + 16]

    def conv_grad(i):
        window = shifted[pl.ds(aligned(i * PITCH, PITCH), pixels), :]
        product = dot(hgt[...], window)
        for j in range(3):
            turned = product[:, j * 256 : j * 256 + 256].T
            for x, y, z in squares:
                first = z * 64 + y * 32
                halves = by_core(turned[first : first + 32, x * 128 : x * 128 + 128])
                for h in range(2):
                    gs[i, h, x, y, z, j * 16 : j * 16 + 16] = halves[h]

    def pack_small():
        counts = mask_ref[pl.ds(aligned(chan * rows * BANDS, 8), rows * BANDS), :].astype(F32)
        counts = jnp.sum(counts.reshape(rows * BANDS // 8, 8, 128), axis=0)
        tallies = jnp.where(high, loss_acc[...], counts + pltpu.roll(counts, LAT, 1))
        heads = jnp.where(high, dec_acc[...], proj_acc[...])
        for x, y, z in squares:
            first = z * 64 + y * 32
            halves = by_core(point_acc[first : first + 32, x * 128 : x * 128 + 128])
            for h in range(2):
                gp[h, x, y, z, 0:16] = halves[h]
        for h, x, y, z in blocks:
            owner = (2 * z + y) * 4 + 2 * x + h
            gp[h, x, y, z, 16:24] = heads[owner * 8 : owner * 8 + 8]
            gp[h, x, y, z, 24:32] = tallies

    def pack_book():
        book_sum = book_acc[...] + pltpu.roll(book_acc[...], LAT, 1)
        for h, x, y, z in blocks:
            first = ((2 * z + y) * 4 + 2 * x + h) * 16
            gb[h, x, y, z] = jnp.where(high, book_sum[first + 8 : first + 16], book_sum[first : first + 8])

    def grad_step(i, carry):
        conv_grad(i)
        start(reduce_core(i + 1))

        @pl.when(i == 0)
        def _():
            core_to_xy(0)

        @pl.when(i < 2)
        def _():
            lax.fori_loop(2 * i, 2 * i + 2, book_chunk, 0)
            core_to_xy(i + 1)

        return carry

    proj_acc[...] = dot_rows(lg_rows[...], xv[...]).T
    pack_small()
    start(reduce_core(0))
    lax.fori_loop(0, 3, grad_step, 0)
    pack_book()
    start(reduce_core(4))
    xy_to_z(0)
    xy_to_z(1)
    halo_wait_recv(hg_halo)

    def back_rows(k):
        return pl.ds(aligned(k * BACK, BACK), BACK)

    def out_copy(k):
        return pltpu.make_async_copy(cotv.at[back_rows(k)], ig_hbm.at[back_rows(k)], out_sem.at[k])

    def back_chunk(k):
        back_grad = None
        for j in (1, 0, 2):
            total = None
            for i in range(3):
                window = hgp[pl.ds(aligned((k * BACK_ROWS + 2 - i) * PITCH, PITCH), BACK), :]
                term = dot(window, wback[i, :, j * 256 : j * 256 + 256])
                total = term if total is None else total + term
            if j != 1:
                total = pltpu.roll(total, BACK - 1 if j == 0 else 1, 0)
            back_grad = total if back_grad is None else back_grad + total
        centre = pl.ds(aligned((k * BACK_ROWS + 1) * PITCH, PITCH), BACK)
        slope = shifted[centre, 256:512].astype(F32) > 0.0
        resid = dot(lg_rows[back_rows(k), :], proj_t[...])
        grad = resid + jnp.where(slope, back_grad, 0.0)
        cotv[back_rows(k), :] = grad.astype(BF16)

    steps = {
        0: [(core_to_xy, 3), (core_to_xy, 4)],
        1: [(reduce_end, 0)],
        2: [(xy_to_z, 2), (reduce_end, 1)],
        5: [(xy_to_z, 3), (xy_to_z, 4)],
        6: [(reduce_end, 2)],
    }

    def back_step(k, carry):
        back_chunk(k)
        out_copy(k).start()
        for at, todo in steps.items():

            @pl.when(k == at)
            def _():
                for act, p in todo:
                    act(p)

        return carry

    lax.fori_loop(0, rows // BACK_ROWS, back_step, 0)
    reduce_end(4)
    reduce_end(3)

    for k in range(rows // BACK_ROWS):
        out_copy(k).wait()
    halo_wait_send(x_halo)
    halo_wait_send(hg_halo)
    for p in range(5):
        sent(gather_z(p) + gather_xy(p) + gather_core(p))
        sent(reduce_core(p) + reduce_xy(p) + reduce_z(p))


def finish_kernel(tile, ig_hbm, ub_hbm, *refs):
    smalls, (out_hbm, grad_hbm, loss_ref), updates = refs[0:19], refs[19:22], refs[22:42]
    ub_rows, out_rows, ig_rows = refs[42:45]
    held, results = refs[45:64], refs[64:79]
    ub_sem, out_sem, ig_sem, grad_sem, in_sem, end_sem = refs[79:]
    tiles = ub_rows.shape[0] // tile

    def part(k):
        return pl.ds(k * tile, tile)

    def ub_copy(k):
        return pltpu.make_async_copy(ub_hbm.at[part(k)], ub_rows.at[part(k)], ub_sem.at[k])

    def ig_copy(k):
        return pltpu.make_async_copy(ig_hbm.at[part(k)], ig_rows.at[part(k)], ig_sem.at[k])

    def grad_copy(k):
        return pltpu.make_async_copy(ig_rows.at[part(k)], grad_hbm.at[part(k)], grad_sem.at[k])

    def out_copy(k):
        return pltpu.make_async_copy(out_rows.at[part(k)], out_hbm.at[part(k)], out_sem.at[k])

    arrive = [pltpu.make_async_copy(src, dst, in_sem.at[n]) for n, (src, dst) in enumerate(zip(smalls, held))]
    wide_updates = [ref for n, ref in enumerate(updates) if n % 4 < 3]
    leave = [pltpu.make_async_copy(src, dst, end_sem.at[n]) for n, (src, dst) in enumerate(zip(results, wide_updates))]
    for n in range(2):
        arrive[n].start()
    for k in range(tiles):
        ub_copy(k).start()
    for copy in arrive[2:]:
        copy.start()
    for k in range(tiles):
        ig_copy(k).start()
    mask_ref, dec_ref, g_ref, q_ref = held[0:4]
    arrive[0].wait()
    arrive[1].wait()
    chan = lax.axis_index("chan")
    top = mask_ref[0:8, :].astype(F32).T
    columns = [jnp.broadcast_to(top[:, t : t + 1], (BAND, 256)) for t in range(BANDS)]
    inner = tile // BAND

    def out_tile(k, carry):
        ub_copy(k).wait()
        here = pl.ds(aligned(k * tile, tile), tile)
        first = aligned((chan * tiles + k) * inner, 8)
        flags = mask_ref[pl.ds(first, inner), :].astype(F32)
        decoded = lax.dot_general(
            ub_rows[here, :], dec_ref[...], (((1,), (1,)), ((), ())), preferred_element_type=F32
        )
        valid = jnp.concatenate([columns[n % BANDS] * flags[n : n + 1, 0:1] for n in range(inner)], axis=0)
        out_rows[here, :] = (decoded * valid).astype(BF16)
        out_copy(k).start()
        ig_copy(k).wait()
        grad_copy(k).start()
        return carry

    lax.fori_loop(0, tiles, out_tile, 0)
    for copy in arrive[2:]:
        copy.wait()
    q = q_ref[...]
    heads, book = q[0:8], q[8:16]
    high = lax.broadcasted_iota(jnp.int32, (8, 128), 1) >= LAT
    gap = jnp.sum(jnp.where(high, q[16:24], 0.0))
    count = jnp.sum(jnp.where(high, 0.0, q[16:24]))
    ratio = jnp.full((8, 128), gap, F32) / jnp.full((8, 128), count * LAT, F32)
    loss_ref[0] = ratio[0, 0]
    loss_ref[1] = 0.25 * ratio[0, 0]
    blocks = jnp.concatenate([g_ref[..., 0:LAT], g_ref[..., LAT:]], axis=1)
    grads = (
        blocks[0:9],
        blocks[9],
        heads[:, 0:LAT],
        jnp.concatenate([book[:, 0:LAT], book[:, LAT:]], axis=0),
        heads[:, LAT:],
    )
    for n, rate in enumerate((0.01, 0.03, 0.03, 0.5, 0.06)):
        weight, moment, square = (ref[...] for ref in held[4 + 3 * n : 7 + 3 * n])
        *values, low = adamw(grads[n], weight, moment, square, rate)
        updates[4 * n + 3][...] = low
        for m, value in enumerate(values):
            results[3 * n + m][...] = value
            leave[3 * n + m].start()
    for copy in leave:
        copy.wait()
    for k in range(tiles):
        grad_copy(k).wait()
        out_copy(k).wait()


def vmem():
    return pl.BlockSpec(memory_space=pltpu.VMEM)


def anywhere():
    return pl.BlockSpec(memory_space=pl.ANY)


def on_device(
    inputs, valid_mask, code_ids, cotangent,
    conv_weight, conv_first, conv_second, point_weight, point_first, point_second,
    proj_weight, proj_first, proj_second, code_book, code_first, code_second,
    dec_weight, dec_first, dec_second,
):
    channels = inputs.shape[1]
    rows = inputs.shape[0] // PITCH
    chunks = rows // CHUNK_ROWS
    pixels = rows * PITCH
    padded = pixels + 2 * PITCH
    entries = 32 * code_book.shape[0]
    mask = valid_mask.reshape(-1, BAND)
    ids = code_ids.reshape(chunks, 1, CHUNK)
    point_weight, point_first, point_second = point_weight.T, point_first.T, point_second.T
    dma = pltpu.SemaphoreType.DMA
    ub, ig, grads, quant, decoder = pl.pallas_call(
        functools.partial(block_kernel, rows),
        out_shape=(
            jax.ShapeDtypeStruct((pixels, 128), BF16),
            jax.ShapeDtypeStruct((pixels, channels), BF16),
            jax.ShapeDtypeStruct((10, 16, 128), F32),
            jax.ShapeDtypeStruct((24, 128), F32),
            jax.ShapeDtypeStruct((channels, 128), BF16),
        ),
        in_specs=[anywhere()] * 9,
        out_specs=(anywhere(), anywhere(), vmem(), vmem(), vmem()),
        scratch_shapes=[
            pltpu.VMEM(ids.shape, jnp.int32),
            pltpu.VMEM(mask.shape, jnp.int32),
            *[pltpu.VMEM(block.shape, F32) for block in (conv_weight, point_weight, proj_weight, code_book, dec_weight)],
            pltpu.VMEM((pixels, channels), BF16),
            pltpu.VMEM((2, PITCH, channels), BF16),
            pltpu.VMEM((pixels, channels), BF16),
            pltpu.VMEM((padded, 3 * channels), BF16),
            pltpu.VMEM((BANDS, BAND, 128), F32),
            pltpu.VMEM((pixels, 128), F32),
            pltpu.VMEM((pixels, 128), BF16),
            pltpu.VMEM((padded, channels), BF16),
            pltpu.VMEM((channels, pixels), BF16),
            pltpu.VMEM((3, 2, 2, 2, 4, 3, 16, 128), BF16),
            pltpu.VMEM((2, 2, 2, 4, 16, 128), BF16),
            pltpu.VMEM((2, 2, 2, 4, 16, 128), BF16),
            pltpu.VMEM((3, 3 * channels, channels), BF16),
            pltpu.VMEM((3, channels, 3 * channels), BF16),
            pltpu.VMEM((channels, channels), BF16),
            pltpu.VMEM((channels, channels), BF16),
            pltpu.VMEM((channels, 128), F32),
            pltpu.VMEM((entries, 128), F32),
            pltpu.VMEM((channels, 128), BF16),
            pltpu.VMEM((channels, 128), BF16),
            pltpu.VMEM((128, channels), BF16),
            pltpu.VMEM((128, entries), BF16),
            pltpu.VMEM((channels, 128), F32),
            pltpu.VMEM((channels, 128), F32),
            pltpu.VMEM((channels, channels), F32),
            pltpu.VMEM((entries, 128), F32),
            pltpu.VMEM((8, 128), F32),
            pltpu.VMEM((2, 2, 2, 4, 32, 128), F32),
            pltpu.VMEM((2, 2, 2, 4, 8, 128), F32),
            pltpu.VMEM((3, 2, 2, 2, 4, 48, 128), F32),
            pltpu.VMEM((2, 2, 4, 32, 128), F32),
            pltpu.VMEM((3, 4, 32, 128), F32),
            pltpu.VMEM((3, 32, 128), F32),
            pltpu.VMEM((2, 2, 4, 8, 128), F32),
            pltpu.VMEM((3, 4, 8, 128), F32),
            pltpu.VMEM((3, 8, 128), F32),
            pltpu.VMEM((3, 2, 2, 4, 48, 128), F32),
            pltpu.VMEM((3, 3, 4, 48, 128), F32),
            pltpu.VMEM((3, 3, 48, 128), F32),
            dma((7,)),
            dma((chunks,)),
            dma((chunks,)),
            dma((rows // BACK_ROWS,)),
            dma(()),
            dma((4,)),
            dma((4,)),
            dma((5, 8)),
            dma((5, 8)),
            dma((5, 8)),
            dma((5, 8)),
        ],
        compiler_params=pltpu.CompilerParams(
            collective_id=0, has_side_effects=True, vmem_limit_bytes=62 * 2**20
        ),
        name="block",
    )(
        inputs, cotangent, ids, mask,
        conv_weight, point_weight, proj_weight, code_book, dec_weight,
    )

    states = (
        conv_weight, conv_first, conv_second, point_weight, point_first, point_second,
        proj_weight, proj_first, proj_second, code_book, code_first, code_second,
        dec_weight, dec_first, dec_second,
    )
    updates = []
    for n in range(5):
        shape = states[3 * n].shape
        updates += [jax.ShapeDtypeStruct(shape, kind) for kind in (F32, F32, F32, BF16)]
    smalls = (mask, decoder, grads, quant, *states)
    tile = CHUNK
    tiles = pixels // tile
    results = pl.pallas_call(
        functools.partial(finish_kernel, tile),
        out_shape=(
            jax.ShapeDtypeStruct(inputs.shape, BF16),
            jax.ShapeDtypeStruct(inputs.shape, BF16),
            jax.ShapeDtypeStruct((2,), F32),
            *updates,
        ),
        in_specs=[anywhere()] * (2 + len(smalls)),
        out_specs=(anywhere(), anywhere(), pl.BlockSpec(memory_space=pltpu.SMEM), *[anywhere() if n % 4 < 3 else vmem() for n in range(20)]),
        scratch_shapes=[
            pltpu.VMEM((pixels, 128), BF16),
            pltpu.VMEM((pixels, channels), BF16),
            pltpu.VMEM((pixels, channels), BF16),
            *[pltpu.VMEM(block.shape, block.dtype) for block in smalls],
            *[pltpu.VMEM(block.shape, F32) for n, block in enumerate(updates) if n % 4 < 3],
            dma((tiles,)),
            dma((tiles,)),
            dma((tiles,)),
            dma((tiles,)),
            dma((len(smalls),)),
            dma((15,)),
        ],
        compiler_params=pltpu.CompilerParams(vmem_limit_bytes=61 * 2**20),
        name="finish",
    )(ig, ub, *smalls)
    point_new = tuple(block.T for block in results[7:11])
    return (*results[:7], *point_new, *results[11:])


def row_stride():
    return BANDS * BAND


def tap_offsets():
    stride = row_stride()
    return [row_step * stride + col_step for row_step in (-1, 0, 1) for col_step in (-1, 0, 1)]


def conv_forward(padded, weights, row_count):
    margin = row_stride() + 1
    summed_terms = None
    for tap_index, offset in enumerate(tap_offsets()):
        begin = margin + offset
        window = lax.slice_in_dim(padded, begin, begin + row_count, axis=0)
        product = jnp.dot(window, weights[tap_index], preferred_element_type=jnp.float32)
        summed_terms = product if summed_terms is None else summed_terms + product
    return summed_terms


def conv_weight_grad(padded, grads, row_count):
    margin = row_stride() + 1
    products = []
    for offset in tap_offsets():
        begin = margin + offset
        window = lax.slice_in_dim(padded, begin, begin + row_count, axis=0)
        products.append(
            lax.dot_general(
                window, grads, (((0,), (0,)), ((), ())), preferred_element_type=jnp.float32
            )
        )
    return jnp.stack(products)


def conv_input_grad(padded_grads, weights, row_count):
    margin = row_stride() + 1
    summed_terms = None
    for tap_index, offset in enumerate(tap_offsets()):
        begin = margin - offset
        window = lax.slice_in_dim(padded_grads, begin, begin + row_count, axis=0)
        product = lax.dot_general(
            window, weights[tap_index], (((1,), (1,)), ((), ())), preferred_element_type=jnp.float32
        )
        summed_terms = product if summed_terms is None else summed_terms + product
    return summed_terms


def bottleneck(latent, mask_rows, code_rows, cotangent, codebook, decoder):
    weight_rows = mask_rows.astype(jnp.float32)[:, None]
    entries = jnp.arange(codebook.shape[0], dtype=jnp.int32)
    onehot = (code_rows[:, None] == entries[None, :]).astype(jnp.bfloat16)
    chosen = jnp.dot(onehot, codebook, preferred_element_type=jnp.float32)
    gap_rows = latent - chosen
    loss_part = jnp.sum(weight_rows * gap_rows * gap_rows)
    count_part = jnp.sum(weight_rows)
    decoded = chosen.astype(jnp.bfloat16)
    decoded_out = lax.dot_general(
        decoded, decoder, (((1,), (1,)), ((), ())), preferred_element_type=jnp.float32
    )
    output = (decoded_out * weight_rows).astype(jnp.bfloat16)
    kept_rows = cotangent * mask_rows.astype(jnp.bfloat16)[:, None]
    decoded_grad = jnp.dot(kept_rows, decoder, preferred_element_type=jnp.float32)
    latent_grad = (decoded_grad + 0.5 * weight_rows * gap_rows).astype(jnp.bfloat16)
    decoder_grad = lax.dot_general(
        kept_rows, decoded, (((0,), (0,)), ((), ())), preferred_element_type=jnp.float32
    )
    book_term = -2.0 * weight_rows * gap_rows
    high_part = book_term.astype(jnp.bfloat16)
    rest_term = book_term - high_part.astype(jnp.float32)
    middle_part = rest_term.astype(jnp.bfloat16)
    low_part = (rest_term - middle_part.astype(jnp.float32)).astype(jnp.bfloat16)
    stacked = jnp.concatenate([high_part, middle_part, low_part], axis=1)
    book_parts = lax.dot_general(
        onehot, stacked, (((0,), (0,)), ((), ())), preferred_element_type=jnp.float32
    )
    width = book_term.shape[1]
    book_grad = book_parts[:, :width] + (
        book_parts[:, width : 2 * width] + book_parts[:, 2 * width :]
    )
    return (output, latent_grad, decoder_grad, book_grad, loss_part, count_part)


def general(
    inputs,
    valid_mask,
    code_ids,
    cotangent,
    conv_weight,
    conv_first,
    conv_second,
    point_weight,
    point_first,
    point_second,
    proj_weight,
    proj_first,
    proj_second,
    code_book,
    code_first,
    code_second,
    dec_weight,
    dec_first,
    dec_second,
):
    chan_count = lax.axis_size("chan")
    chan_index = lax.axis_index("chan")
    rows_quarter = inputs.shape[0]
    rows_all = valid_mask.shape[0]
    channels = inputs.shape[1]
    chan_width = channels // chan_count
    margin = row_stride() + 1
    conv_low, point_low = (
        lax.all_gather(conv_weight.astype(jnp.bfloat16), "dp", axis=1, tiled=True),
        lax.all_gather(point_weight.astype(jnp.bfloat16), "dp", axis=1, tiled=True),
    )
    proj_full, book_full, dec_full = (
        lax.all_gather(proj_weight.astype(jnp.bfloat16), ("dp", "chan"), axis=0, tiled=True),
        lax.all_gather(code_book.astype(jnp.bfloat16), ("dp", "chan"), axis=0, tiled=True),
        lax.all_gather(dec_weight.astype(jnp.bfloat16), ("dp", "chan"), axis=0, tiled=True),
    )
    mask_rows = lax.dynamic_slice_in_dim(valid_mask, chan_index * rows_quarter, rows_quarter)
    first_column = chan_index * chan_width
    gathered = lax.all_gather(inputs, "chan", axis=0, tiled=True)
    valid_all = (valid_mask > 0)[:, None]
    activations = jnp.where(valid_all, jnp.maximum(gathered, 0), 0)
    padded = jnp.pad(activations, ((margin, margin), (0, 0)))
    hidden = conv_forward(padded, conv_low, rows_all)
    middle = jnp.maximum(hidden, 0.0).astype(jnp.bfloat16)
    partial_branch = jnp.dot(middle, point_low, preferred_element_type=jnp.float32)
    branch = lax.psum_scatter(partial_branch, "chan", scatter_dimension=1, tiled=True)
    own_inputs = lax.dynamic_slice_in_dim(gathered, first_column, chan_width, 1).astype(jnp.float32)
    summed = (own_inputs + branch).astype(jnp.bfloat16)
    proj_rows = lax.dynamic_slice_in_dim(proj_full, first_column, chan_width, 0)
    window = summed
    latent = lax.psum_scatter(
        jnp.dot(window, proj_rows, preferred_element_type=jnp.float32),
        "chan",
        scatter_dimension=0,
        tiled=True,
    )
    output, latent_grad, decoder_grad, book_grad, loss_part, count_part = bottleneck(
        latent, mask_rows, code_ids, cotangent, book_full, dec_full
    )
    grads_all = lax.all_gather(latent_grad, "chan", axis=0, tiled=True)
    proj_part = lax.dot_general(
        summed, grads_all, (((0,), (0,)), ((), ())), preferred_element_type=jnp.float32
    )
    proj_grad = lax.dynamic_update_slice_in_dim(
        jnp.zeros((channels, proj_part.shape[1]), jnp.float32), proj_part, first_column, 0
    )
    resid = lax.dot_general(
        grads_all, proj_rows, (((1,), (1,)), ((), ())), preferred_element_type=jnp.float32
    )
    resid_all = lax.all_gather(resid.astype(jnp.bfloat16), "chan", axis=1, tiled=True)
    point_grad = lax.dot_general(
        middle, resid_all, (((0,), (0,)), ((), ())), preferred_element_type=jnp.float32
    )
    hidden_back = lax.dot_general(
        resid_all, point_low, (((1,), (1,)), ((), ())), preferred_element_type=jnp.float32
    )
    hidden_grad = jnp.where(hidden > 0.0, hidden_back.astype(jnp.bfloat16), 0)
    conv_grad = conv_weight_grad(padded, hidden_grad, rows_all)
    grad_padded = jnp.pad(hidden_grad, ((margin, margin), (0, 0)))
    slopes = jnp.logical_and(gathered > 0, valid_all)
    window = grad_padded
    back_grad = conv_input_grad(window, conv_low, rows_quarter * lax.axis_size("chan"))
    back_grad = jnp.where(slopes, back_grad, 0.0)
    own_back = lax.dynamic_slice_in_dim(back_grad, first_column, chan_width, 1)
    input_grad = lax.psum_scatter(
        lax.dynamic_update_slice_in_dim(back_grad, own_back + resid, first_column, 1),
        "chan",
        scatter_dimension=0,
        tiled=True,
    ).astype(jnp.bfloat16)
    conv_reduced, point_reduced = (
        lax.psum_scatter(conv_grad, "dp", scatter_dimension=1, tiled=True),
        lax.psum_scatter(point_grad, "dp", scatter_dimension=1, tiled=True),
    )
    proj_reduced, book_reduced, dec_reduced = (
        lax.psum_scatter(proj_grad, ("dp", "chan"), scatter_dimension=0, tiled=True),
        lax.psum_scatter(book_grad, ("dp", "chan"), scatter_dimension=0, tiled=True),
        lax.psum_scatter(decoder_grad, ("dp", "chan"), scatter_dimension=0, tiled=True),
    )
    loss_total, count_total = lax.psum((loss_part, count_part), ("dp", "chan"))
    losses = jnp.stack([loss_total, 0.25 * loss_total]) / (count_total * LAT)
    conv_out = adamw(conv_reduced, conv_weight, conv_first, conv_second, 0.01)
    point_out = adamw(point_reduced, point_weight, point_first, point_second, 0.03)
    proj_out = adamw(proj_reduced, proj_weight, proj_first, proj_second, 0.03)
    code_out = adamw(book_reduced, code_book, code_first, code_second, 0.5)
    dec_out = adamw(dec_reduced, dec_weight, dec_first, dec_second, 0.06)
    return (
        output,
        input_grad,
        losses,
        conv_out[0],
        conv_out[1],
        conv_out[2],
        conv_out[3],
        point_out[0],
        point_out[1],
        point_out[2],
        point_out[3],
        proj_out[0],
        proj_out[1],
        proj_out[2],
        proj_out[3],
        code_out[0],
        code_out[1],
        code_out[2],
        code_out[3],
        dec_out[0],
        dec_out[1],
        dec_out[2],
        dec_out[3],
    )


def solution(mesh):
    pixel = P(("dp", "chan"), None)
    conv, point = P(None, "dp", "chan"), P("chan", "dp")
    in_specs = (pixel, P("dp"), P(("dp", "chan")), pixel)
    in_specs += (conv,) * 3 + (point,) * 3 + (pixel,) * 9
    out_specs = (pixel, pixel, P()) + (conv,) * 4 + (point,) * 4 + (pixel,) * 12
    fits = mesh.shape["dp"] == 8 and mesh.shape["chan"] == 4
    body = on_device if fits else general
    return jax.shard_map(body, mesh=mesh, in_specs=in_specs, out_specs=out_specs, check_vma=False)
```

```python
import functools

import jax
import jax.numpy as jnp
from jax import lax
from jax.experimental import pallas as pl
from jax.experimental.pallas import tpu as pltpu
from jax.sharding import PartitionSpec as P

LAT = 64
BAND = 128
BANDS = 2
STEP = 5
PITCH = BANDS * BAND
CHUNK_ROWS = 8
CHUNK = CHUNK_ROWS * PITCH
BACK_ROWS = 4
BACK = BACK_ROWS * PITCH
MESH = pl.DeviceIdType.MESH
F32 = jnp.float32
BF16 = jnp.bfloat16

beta_first = 0.5
beta_second = 0.5
epsilon = 1e-08
decay_rate = 0.01


def adamw(grad, weight, first, second, rate):
    first_new = beta_first * first + (1.0 - beta_first) * grad
    second_new = beta_second * second + (1.0 - beta_second) * grad * grad
    first_hat = first_new / (1.0 - beta_first**STEP)
    second_hat = second_new / (1.0 - beta_second**STEP)
    weight_new = weight - rate * (
        first_hat / (jnp.sqrt(second_hat) + epsilon) + decay_rate * weight
    )
    return (weight_new, first_new, second_new, weight_new.astype(BF16))


def dot(a, b):
    return jnp.dot(a, b, preferred_element_type=F32)


def dot_rows(a, b):
    return lax.dot_general(a, b, (((0,), (0,)), ((), ())), preferred_element_type=F32)


def aligned(value, unit):
    return pl.multiple_of(value, unit)


def block_kernel(
    rows,
    x_hbm,
    cot_hbm,
    ids_hbm,
    mask_hbm,
    conv_hbm,
    point_hbm,
    proj_hbm,
    book_hbm,
    dec_hbm,
    ub_hbm,
    ig_hbm,
    g_ref,
    q_ref,
    dz_ref,
    ids_ref,
    mask_ref,
    conv_ref,
    point_ref,
    proj_ref,
    book_ref,
    dec_ref,
    xv,
    xhalo,
    cotv,
    shifted,
    col_mask,
    u_rows,
    lg_rows,
    hgp,
    hgt,
    resid_rows,
    wb,
    pb,
    qb,
    wfull,
    wback,
    point_t,
    point_n,
    qf,
    bookf,
    decz,
    projz,
    proj_t,
    book_t,
    dec_acc,
    proj_acc,
    point_acc,
    book_acc,
    loss_acc,
    gp,
    gb,
    gs,
    rp0,
    rp1,
    rp2,
    rb0,
    rb1,
    rb2,
    rc0,
    rc1,
    rc2,
    small_sem,
    x_sem,
    cot_sem,
    out_sem,
    ub_sem,
    halo_s,
    halo_r,
    q_s,
    q_r,
    ag_s,
    ag_r,
    rs_s,
    rs_r,
):
    dp, chan = lax.axis_index("dp"), lax.axis_index("chan")
    core, xc = lax.rem(chan, 2), lax.div(chan, 2)
    yc, zc = lax.rem(dp, 2), lax.div(dp, 2)
    core_peer = (dp, chan + 1 - 2 * core)
    other_core = 1 - core
    xy_of = [(1 - xc if k % 2 else xc, 1 - yc if k // 2 else yc) for k in range(4)]
    xy_peer = [(2 * zc + y, 2 * x + core) for x, y in xy_of]
    z_of = [zc, zc + 1 - 2 * lax.rem(zc, 2), lax.rem(zc + 2, 4), 3 - zc]
    z_peer = [(2 * z + yc, chan) for z in z_of]
    up_peer, down_peer = (dp, chan - 1), (dp, chan + 1)
    chunks = rows // CHUNK_ROWS
    pixels = rows * PITCH
    def remote(src, dst, s_sem, r_sem, peer):
        return pltpu.make_async_remote_copy(
            src_ref=src, dst_ref=dst, send_sem=s_sem, recv_sem=r_sem, device_id=peer, device_id_type=MESH
        )

    def start(copies):
        for copy in copies:
            copy.start()

    def landed(copies):
        for copy in copies:
            copy.wait_recv()

    def sent(copies):
        for copy in copies:
            copy.wait_send()

    barrier = pltpu.get_barrier_semaphore()
    chip_peer = [(2 * z_of[k // 4] + xy_of[k % 4][1], 2 * xy_of[k % 4][0] + core) for k in range(16)]
    partners = [core_peer, (dp, 3 - chan)] + chip_peer[1:]
    for partner in partners:
        pl.semaphore_signal(barrier, inc=1, device_id=partner, device_id_type=MESH)

    smalls = [
        pltpu.make_async_copy(src, dst, small_sem.at[n])
        for n, (src, dst) in enumerate(
            (
                (conv_hbm, conv_ref),
                (point_hbm, point_ref),
                (proj_hbm, proj_ref),
                (book_hbm, book_ref),
                (dec_hbm, dec_ref),
                (mask_hbm, mask_ref),
                (ids_hbm, ids_ref),
            )
        )
    ]
    for copy in smalls:
        copy.start()

    def part(k):
        return pl.ds(k * CHUNK, CHUNK)

    def x_copy(k):
        return pltpu.make_async_copy(x_hbm.at[part(k)], xv.at[part(k)], x_sem.at[k])

    def cot_copy(k):
        return pltpu.make_async_copy(cot_hbm.at[part(k)], cotv.at[part(k)], cot_sem.at[k])

    for k in range(chunks):
        x_copy(k).start()
    for k in range(chunks):
        cot_copy(k).start()

    lane = lax.broadcasted_iota(jnp.int32, (1, 128), 1)
    high = lane >= LAT

    def packed(block):
        return jnp.concatenate([block[..., 0:16, :], block[..., 16:32, :]], axis=-1).astype(BF16)

    for copy in smalls[0:5]:
        copy.wait()
    conv_own = packed(conv_ref[...])
    for i in range(3):
        wb[i, core, xc, yc, zc] = conv_own[3 * i : 3 * i + 3]
    pb[core, xc, yc, zc] = packed(point_ref[...])
    quant = jnp.concatenate(
        [
            jnp.concatenate([dec_ref[...], proj_ref[...]], axis=1),
            jnp.concatenate([book_ref[0:8, :], book_ref[8:16, :]], axis=1),
        ],
        axis=0,
    )
    qb[core, xc, yc, zc] = quant.astype(BF16)

    pl.semaphore_wait(barrier, len(partners))


    def halo_copies(up_src, up_dst, down_src, down_dst, at):
        up = remote(up_src, up_dst, halo_s.at[at], halo_r.at[at], up_peer)
        down = remote(down_src, down_dst, halo_s.at[at + 1], halo_r.at[at + 1], down_peer)
        return up, down

    def halo_start(copies):
        @pl.when(chan > 0)
        def _():
            copies[0].start()

        @pl.when(chan < 3)
        def _():
            copies[1].start()

    def halo_wait_send(copies):
        @pl.when(chan > 0)
        def _():
            copies[0].wait_send()

        @pl.when(chan < 3)
        def _():
            copies[1].wait_send()

    def halo_wait_recv(copies):
        @pl.when(chan < 3)
        def _():
            copies[0].wait_recv()

        @pl.when(chan > 0)
        def _():
            copies[1].wait_recv()

    last_row = pl.ds((rows - 1) * PITCH, PITCH)
    x_halo = halo_copies(x_hbm.at[pl.ds(0, PITCH)], xhalo.at[1], x_hbm.at[last_row], xhalo.at[0], 0)
    @pl.when(chan == 0)
    def _():
        xhalo[0] = jnp.zeros(xhalo.shape[1:], BF16)

    @pl.when(chan == 3)
    def _():
        xhalo[1] = jnp.zeros(xhalo.shape[1:], BF16)

    def gather_buffer(p):
        if isinstance(p, int) and p in (0, 4):
            return qb if p == 0 else pb
        return wb.at[p - 1]

    def gather_z(p):
        buffer = gather_buffer(p)
        block = buffer.at[core, :, :, zc] if p == 3 else buffer.at[core, xc, yc, zc]
        return [remote(block, block, ag_s.at[p, k], ag_r.at[p, k], z_peer[k]) for k in (1, 2, 3)]

    def gather_xy(p):
        buffer = gather_buffer(p)
        block = buffer.at[core, xc, yc, zc] if p == 3 else buffer.at[core, xc, yc]
        return [remote(block, block, ag_s.at[p, 3 + k], ag_r.at[p, 3 + k], xy_peer[k]) for k in (1, 2, 3)]

    def quant_copies():
        block = qb.at[core, xc, yc, zc]
        return [remote(block, block, q_s.at[k], q_r.at[k], chip_peer[k]) for k in range(1, 16)]

    def gather_core(p):
        block = gather_buffer(p).at[core]
        return [remote(block, block, ag_s.at[p, 7], ag_r.at[p, 7], core_peer)]

    start(quant_copies())
    start(gather_xy(3))
    for p in (1, 2, 4):
        start(gather_z(p))
    halo_start(x_halo)

    for copy in smalls[5:]:
        copy.wait()

    top = mask_ref[0:8, :].astype(F32).T
    for t in range(BANDS):
        col_mask[t] = jnp.broadcast_to(top[:, t : t + 1], (BAND, 128))

    def two(block):
        return jnp.concatenate([block, block], axis=1)

    def tile_mask(flags, n):
        return col_mask[n % BANDS] * flags[n : n + 1, 0:1]

    def row_flags(first_row, row_count):
        first = aligned(first_row * BANDS, 8)
        return mask_ref[pl.ds(first, row_count * BANDS), :].astype(F32)

    def shift_tile(block, valid, at):
        base = aligned(at, 16)
        act = jnp.maximum(block.astype(F32), 0.0) * two(valid)
        shifted[pl.ds(base, BAND), 256:512] = act.astype(BF16)
        before = pltpu.roll(act, 1, 0)
        shifted[pl.ds(base, BAND), 0:256] = before.astype(BF16)
        after = pltpu.roll(act, BAND - 1, 0)
        shifted[pl.ds(base, BAND), 512:768] = after.astype(BF16)

    def shift_rows(k, carry):
        flags = row_flags(chan * rows + k * 4, 4)
        for n in range(4 * BANDS):
            at = k * 4 * PITCH + n * BAND
            shift_tile(xv[pl.ds(aligned(at, 16), BAND), :], tile_mask(flags, n), at + PITCH)
        return carry

    x_copy(0).wait()
    lax.fori_loop(0, 2, shift_rows, 0)
    for k in range(1, chunks):
        x_copy(k).wait()
    lax.fori_loop(2, 5, shift_rows, 0)
    landed(gather_xy(3))
    start(gather_z(3))
    lax.fori_loop(5, rows // 4, shift_rows, 0)
    landed(gather_z(1))
    start(gather_xy(1))
    landed(quant_copies())
    start(gather_core(0))
    halo_wait_recv(x_halo)

    def halo_row(side, at, global_row, present):
        group = row_flags(lax.div(jnp.maximum(global_row, 0), 4) * 4, 4)
        inside = 2 * (3 if side == 0 else 0)
        flags = group[inside : inside + 2] * present.astype(F32)
        for t in range(BANDS):
            shift_tile(xhalo[side, t * BAND : (t + 1) * BAND], tile_mask(flags, t), at + t * BAND)

    halo_row(0, 0, chan * rows - 1, chan > 0)
    halo_row(1, (rows + 1) * PITCH, jnp.minimum(chan * rows + rows, 3 * rows), chan < 3)


    book_acc[...] = jnp.zeros_like(book_acc)
    loss_acc[...] = jnp.zeros_like(loss_acc)
    landed(gather_z(2))
    start(gather_xy(2))
    landed(gather_core(0))

    squares = [(x, y, z) for z in range(4) for y in range(2) for x in range(2)]
    blocks = [(h, x, y, z) for x, y, z in squares for h in range(2)]

    def natural(first, second):
        lower = jnp.concatenate([first[:, 0:LAT], second[:, 0:LAT]], axis=1)
        upper = jnp.concatenate([first[:, LAT:], second[:, LAT:]], axis=1)
        return jnp.concatenate([lower, upper], axis=0)

    def by_core(tile):
        lower, upper = tile[0:16], tile[16:32]
        return jnp.where(high, pltpu.roll(upper, LAT, 1), lower), jnp.where(high, upper, pltpu.roll(lower, LAT, 1))

    for h, x, y, z in blocks:
        owner = (2 * z + y) * 4 + 2 * x + h
        small = qb[h, x, y, z].astype(F32)
        qf[owner * 8 : owner * 8 + 8, :] = small[0:8]
        bookf[owner * 16 : owner * 16 + 8, :] = pltpu.roll(small[8:16], LAT, 1)
        bookf[owner * 16 + 8 : owner * 16 + 16, :] = small[8:16]
    small = qf[...]
    decz[...] = jnp.where(high, 0.0, small).astype(BF16)
    projz[...] = jnp.where(high, small, 0.0).astype(BF16)
    dz_ref[...] = jnp.where(high, pltpu.roll(small, LAT, 1), 0.0).astype(BF16)
    proj_t[...] = jnp.where(high, 0.0, pltpu.roll(small, LAT, 1)).astype(BF16).T
    book_t[...] = jnp.where(high, bookf[...], 0.0).astype(BF16).T

    def onehot_t(k):
        entries = lax.broadcasted_iota(jnp.int32, (book_t.shape[1], CHUNK), 0)
        return (entries == ids_ref[k]).astype(F32).astype(BF16)

    def rows_of(k):
        return pl.ds(aligned(k * CHUNK, CHUNK), CHUNK)

    def valid_of(k):
        flags = row_flags(chan * rows + k * CHUNK_ROWS, CHUNK_ROWS)
        return jnp.concatenate([tile_mask(flags, n) for n in range(CHUNK_ROWS * BANDS)], axis=0)

    def decoder_chunk(k):
        kept = (cotv[rows_of(k), :].astype(F32) * two(valid_of(k))).astype(BF16)
        cotv[rows_of(k), :] = kept
        chosen = dot(book_t[...], onehot_t(k)).T
        both = chosen + dot(kept, decz[...])
        u_rows[rows_of(k), :] = both
        lg_rows[rows_of(k), :] = both.astype(BF16)

    def decoder_step(k, carry):
        cot_copy(k).wait()
        decoder_chunk(k)

        @pl.when(k == 0)
        def _():
            landed(gather_z(4))
            start(gather_xy(4))

        @pl.when(k == 2)
        def _():
            landed(gather_xy(1))
            start(gather_core(1))

        @pl.when(k == 3)
        def _():
            landed(gather_z(3))
            start(gather_core(3))

        return carry

    lax.fori_loop(0, chunks, decoder_step, 0)
    ub_copy = pltpu.make_async_copy(lg_rows, ub_hbm, ub_sem)
    ub_copy.start()
    dec_acc[...] = dot_rows(lg_rows[...], cotv[...]).T

    def unpack_taps(i):
        landed(gather_core(1 + i))
        for x, y, z in squares:
            for j in range(3):
                first = j * 256 + z * 64 + y * 32
                wfull[i, first : first + 32, x * 128 : x * 128 + 128] = natural(wb[i, 0, x, y, z, j], wb[i, 1, x, y, z, j])
        for j in range(3):
            wback[i, :, j * 256 : j * 256 + 256] = wfull[i, j * 256 : j * 256 + 256, :].T

    def taps(k, i):
        window = shifted[pl.ds(aligned((k * CHUNK_ROWS + i) * PITCH, PITCH), CHUNK), :]
        return dot(window, wfull[i])

    def middle_chunk(k, carry):
        hidden = taps(k, 0) + (taps(k, 1) + taps(k, 2))
        cotv[rows_of(k), :] = jnp.maximum(hidden, 0.0).astype(BF16)

        @pl.when(k == 0)
        def _():
            landed(gather_xy(4))
            start(gather_core(4))

        return carry

    def latent_chunk(k, carry):
        middle = cotv[rows_of(k), :]
        branch = dot(middle, point_n[...])
        summed = (xv[rows_of(k), :].astype(F32) + branch).astype(BF16)
        xv[rows_of(k), :] = summed
        valid = valid_of(k)
        gap = u_rows[rows_of(k), :] - dot(summed, projz[...])
        weighted = gap * valid
        loss_acc[...] += jnp.sum((weighted * gap).reshape(CHUNK // 8, 8, 128), axis=0)
        latent_grad = (gap - 0.5 * pltpu.roll(weighted, LAT, 1)).astype(BF16)
        lg_rows[rows_of(k), :] = latent_grad
        term = 2.0 * weighted
        coarse = term.astype(BF16).astype(F32)
        u_rows[rows_of(k), :] = jnp.where(high, coarse, pltpu.roll(term - coarse, LAT, 1))
        resid_low = dot(latent_grad, proj_t[...]).astype(BF16)
        resid_rows[rows_of(k), :] = resid_low
        back = dot(resid_low, point_t[...])
        hidden_grad = jnp.where(middle.astype(F32) > 0.0, back, 0.0).astype(BF16)
        hgp[pl.ds(aligned((k * CHUNK_ROWS + 1) * PITCH, PITCH), CHUNK), :] = hidden_grad
        hgt[:, pl.ds(aligned(k * CHUNK, CHUNK), CHUNK)] = hidden_grad.T
        return carry

    def book_chunk(k, carry):
        book_acc[...] += dot(onehot_t(k), u_rows[rows_of(k), :].astype(BF16))
        return carry

    landed(gather_xy(2))
    start(gather_core(2))
    for i in (0, 2, 1):
        unpack_taps(i)
    lax.fori_loop(0, chunks, middle_chunk, 0)
    landed(gather_core(4))
    for x, y, z in squares:
        first = z * 64 + y * 32
        point_t[first : first + 32, x * 128 : x * 128 + 128] = natural(pb[0, x, y, z], pb[1, x, y, z])
    point_n[...] = point_t[...].T
    ub_copy.wait()
    lax.fori_loop(0, chunks, latent_chunk, 0)

    zero_row = jnp.zeros((PITCH, 256), BF16)

    @pl.when(chan == 0)
    def _():
        hgp[0:PITCH, :] = zero_row

    @pl.when(chan == 3)
    def _():
        hgp[(rows + 1) * PITCH : (rows + 2) * PITCH, :] = zero_row

    def grad_row(r):
        return hgp.at[pl.ds(r * PITCH, PITCH), :]

    hg_halo = halo_copies(grad_row(1), grad_row(rows + 1), grad_row(rows), grad_row(0), 2)
    halo_start(hg_halo)

    def reduce_buffers(p):
        if isinstance(p, int) and p == 0:
            return gp, rp0, rp1, rp2
        if isinstance(p, int) and p == 4:
            return gb, rb0, rb1, rb2
        return gs.at[p - 1], rc0.at[p - 1], rc1.at[p - 1], rc2.at[p - 1]

    def reduce_core(p):
        buffer, first, _, _ = reduce_buffers(p)
        return [remote(buffer.at[other_core], first, rs_s.at[p, 0], rs_r.at[p, 0], core_peer)]

    def reduce_xy(p):
        buffer, _, second, _ = reduce_buffers(p)
        return [
            remote(buffer.at[core, *xy_of[k]], second.at[k - 1], rs_s.at[p, k], rs_r.at[p, k], xy_peer[k])
            for k in (1, 2, 3)
        ]

    def reduce_z(p):
        buffer, _, _, third = reduce_buffers(p)
        return [
            remote(
                buffer.at[core, xc, yc, z_of[k]], third.at[k - 1], rs_s.at[p, 3 + k], rs_r.at[p, 3 + k], z_peer[k]
            )
            for k in (1, 2, 3)
        ]

    def core_to_xy(p):
        landed(reduce_core(p))
        buffer, first, _, _ = reduce_buffers(p)
        buffer[core] = buffer[core] + first[...]
        start(reduce_xy(p))

    def xy_to_z(p):
        landed(reduce_xy(p))
        buffer, _, second, _ = reduce_buffers(p)
        buffer[core, xc, yc] = (buffer[core, xc, yc] + second[0]) + (second[1] + second[2])
        start(reduce_z(p))

    def reduce_end(p):
        landed(reduce_z(p))
        buffer, _, _, third = reduce_buffers(p)
        total = (buffer[core, xc, yc, zc] + third[0]) + (third[1] + third[2])
        if p == 0:
            q_ref[0:8] = total[16:24]
            q_ref[16:24] = total[24:32]
            g_ref[9] = total[0:16]
        elif p == 4:
            q_ref[8:16] = total
        else:
            for j in range(3):
                g_ref[3 * (p - 1) + j] = total[j * 16 : j * 16 + 16]

    def conv_grad(i):
        window = shifted[pl.ds(aligned(i * PITCH, PITCH), pixels), :]
        product = dot(hgt[...], window)
        for j in range(3):
            turned = product[:, j * 256 : j * 256 + 256].T
            for x, y, z in squares:
                first = z * 64 + y * 32
                halves = by_core(turned[first : first + 32, x * 128 : x * 128 + 128])
                for h in range(2):
                    gs[i, h, x, y, z, j * 16 : j * 16 + 16] = halves[h]

    def pack_small():
        counts = mask_ref[pl.ds(aligned(chan * rows * BANDS, 8), rows * BANDS), :].astype(F32)
        counts = jnp.sum(counts.reshape(rows * BANDS // 8, 8, 128), axis=0)
        tallies = jnp.where(high, loss_acc[...], counts + pltpu.roll(counts, LAT, 1))
        heads = jnp.where(high, dec_acc[...], proj_acc[...])
        for x, y, z in squares:
            first = z * 64 + y * 32
            halves = by_core(point_acc[first : first + 32, x * 128 : x * 128 + 128])
            for h in range(2):
                gp[h, x, y, z, 0:16] = halves[h]
        for h, x, y, z in blocks:
            owner = (2 * z + y) * 4 + 2 * x + h
            gp[h, x, y, z, 16:24] = heads[owner * 8 : owner * 8 + 8]
            gp[h, x, y, z, 24:32] = tallies

    def pack_book():
        book_sum = book_acc[...] + pltpu.roll(book_acc[...], LAT, 1)
        for h, x, y, z in blocks:
            first = ((2 * z + y) * 4 + 2 * x + h) * 16
            gb[h, x, y, z] = jnp.where(high, book_sum[first + 8 : first + 16], book_sum[first : first + 8])

    def grad_step(i, carry):
        conv_grad(i)
        start(reduce_core(i + 1))

        @pl.when(i == 0)
        def _():
            core_to_xy(0)

        @pl.when(i < 2)
        def _():
            lax.fori_loop(2 * i, 2 * i + 2, book_chunk, 0)
            core_to_xy(i + 1)

        return carry

    proj_acc[...] = dot_rows(lg_rows[...], xv[...]).T
    point_acc[...] = dot_rows(resid_rows[...], cotv[...])
    pack_small()
    start(reduce_core(0))
    lax.fori_loop(0, 3, grad_step, 0)
    pack_book()
    start(reduce_core(4))
    xy_to_z(0)
    xy_to_z(1)
    halo_wait_recv(hg_halo)

    def back_rows(k):
        return pl.ds(aligned(k * BACK, BACK), BACK)

    def out_copy(k):
        return pltpu.make_async_copy(cotv.at[back_rows(k)], ig_hbm.at[back_rows(k)], out_sem.at[k])

    def back_chunk(k):
        back_grad = None
        for j in (1, 0, 2):
            total = None
            for i in range(3):
                window = hgp[pl.ds(aligned((k * BACK_ROWS + 2 - i) * PITCH, PITCH), BACK), :]
                term = dot(window, wback[i, :, j * 256 : j * 256 + 256])
                total = term if total is None else total + term
            if j != 1:
                total = pltpu.roll(total, BACK - 1 if j == 0 else 1, 0)
            back_grad = total if back_grad is None else back_grad + total
        centre = pl.ds(aligned((k * BACK_ROWS + 1) * PITCH, PITCH), BACK)
        slope = shifted[centre, 256:512].astype(F32) > 0.0
        resid = dot(lg_rows[back_rows(k), :], proj_t[...])
        grad = resid + jnp.where(slope, back_grad, 0.0)
        cotv[back_rows(k), :] = grad.astype(BF16)

    steps = {
        0: [(core_to_xy, 3), (core_to_xy, 4)],
        1: [(reduce_end, 0)],
        2: [(xy_to_z, 2), (reduce_end, 1)],
        5: [(xy_to_z, 3), (xy_to_z, 4)],
        6: [(reduce_end, 2)],
    }

    def back_step(k, carry):
        back_chunk(k)
        out_copy(k).start()
        for at, todo in steps.items():

            @pl.when(k == at)
            def _():
                for act, p in todo:
                    act(p)

        return carry

    lax.fori_loop(0, rows // BACK_ROWS, back_step, 0)
    reduce_end(4)
    reduce_end(3)

    for k in range(rows // BACK_ROWS):
        out_copy(k).wait()
    halo_wait_send(x_halo)
    halo_wait_send(hg_halo)
    sent(quant_copies() + gather_core(0))
    for p in range(1, 5):
        sent(gather_z(p) + gather_xy(p) + gather_core(p))
    for p in range(5):
        sent(reduce_core(p) + reduce_xy(p) + reduce_z(p))


def finish_kernel(tile, ig_hbm, ub_hbm, *refs):
    smalls, (out_hbm, grad_hbm, loss_ref), updates = refs[0:19], refs[19:22], refs[22:42]
    ub_rows, out_rows, ig_rows = refs[42:45]
    held, results = refs[45:64], refs[64:79]
    ub_sem, out_sem, ig_sem, grad_sem, in_sem, end_sem = refs[79:]
    tiles = ub_rows.shape[0] // tile

    def part(k):
        return pl.ds(k * tile, tile)

    def ub_copy(k):
        return pltpu.make_async_copy(ub_hbm.at[part(k)], ub_rows.at[part(k)], ub_sem.at[k])

    def ig_copy(k):
        return pltpu.make_async_copy(ig_hbm.at[part(k)], ig_rows.at[part(k)], ig_sem.at[k])

    def grad_copy(k):
        return pltpu.make_async_copy(ig_rows.at[part(k)], grad_hbm.at[part(k)], grad_sem.at[k])

    def out_copy(k):
        return pltpu.make_async_copy(out_rows.at[part(k)], out_hbm.at[part(k)], out_sem.at[k])

    arrive = [pltpu.make_async_copy(src, dst, in_sem.at[n]) for n, (src, dst) in enumerate(zip(smalls, held))]
    wide_updates = [ref for n, ref in enumerate(updates) if n % 4 < 3]
    leave = [pltpu.make_async_copy(src, dst, end_sem.at[n]) for n, (src, dst) in enumerate(zip(results, wide_updates))]
    for n in range(2):
        arrive[n].start()
    for k in range(tiles):
        ub_copy(k).start()
    for copy in arrive[2:]:
        copy.start()
    for k in range(tiles):
        ig_copy(k).start()
    mask_ref, dec_ref, g_ref, q_ref = held[0:4]
    arrive[0].wait()
    arrive[1].wait()
    chan = lax.axis_index("chan")
    top = mask_ref[0:8, :].astype(F32).T
    columns = [jnp.broadcast_to(top[:, t : t + 1], (BAND, 256)) for t in range(BANDS)]
    inner = tile // BAND

    def out_tile(k, carry):
        ub_copy(k).wait()
        here = pl.ds(aligned(k * tile, tile), tile)
        first = aligned((chan * tiles + k) * inner, 8)
        flags = mask_ref[pl.ds(first, inner), :].astype(F32)
        decoded = lax.dot_general(
            ub_rows[here, :], dec_ref[...], (((1,), (1,)), ((), ())), preferred_element_type=F32
        )
        valid = jnp.concatenate([columns[n % BANDS] * flags[n : n + 1, 0:1] for n in range(inner)], axis=0)
        out_rows[here, :] = (decoded * valid).astype(BF16)
        out_copy(k).start()
        ig_copy(k).wait()
        grad_copy(k).start()
        return carry

    lax.fori_loop(0, tiles, out_tile, 0)
    for copy in arrive[2:]:
        copy.wait()
    q = q_ref[...]
    heads, book = q[0:8], q[8:16]
    high = lax.broadcasted_iota(jnp.int32, (8, 128), 1) >= LAT
    gap = jnp.sum(jnp.where(high, q[16:24], 0.0))
    count = jnp.sum(jnp.where(high, 0.0, q[16:24]))
    ratio = jnp.full((8, 128), gap, F32) / jnp.full((8, 128), count * LAT, F32)
    loss_ref[0] = ratio[0, 0]
    loss_ref[1] = 0.25 * ratio[0, 0]
    blocks = jnp.concatenate([g_ref[..., 0:LAT], g_ref[..., LAT:]], axis=1)
    grads = (
        blocks[0:9],
        blocks[9],
        heads[:, 0:LAT],
        jnp.concatenate([book[:, 0:LAT], book[:, LAT:]], axis=0),
        heads[:, LAT:],
    )
    for n, rate in enumerate((0.01, 0.03, 0.03, 0.5, 0.06)):
        weight, moment, square = (ref[...] for ref in held[4 + 3 * n : 7 + 3 * n])
        *values, low = adamw(grads[n], weight, moment, square, rate)
        updates[4 * n + 3][...] = low
        for m, value in enumerate(values):
            results[3 * n + m][...] = value
            leave[3 * n + m].start()
    for copy in leave:
        copy.wait()
    for k in range(tiles):
        grad_copy(k).wait()
        out_copy(k).wait()


def vmem():
    return pl.BlockSpec(memory_space=pltpu.VMEM)


def anywhere():
    return pl.BlockSpec(memory_space=pl.ANY)


def on_device(
    inputs, valid_mask, code_ids, cotangent,
    conv_weight, conv_first, conv_second, point_weight, point_first, point_second,
    proj_weight, proj_first, proj_second, code_book, code_first, code_second,
    dec_weight, dec_first, dec_second,
):
    channels = inputs.shape[1]
    rows = inputs.shape[0] // PITCH
    chunks = rows // CHUNK_ROWS
    pixels = rows * PITCH
    padded = pixels + 2 * PITCH
    entries = 32 * code_book.shape[0]
    mask = valid_mask.reshape(-1, BAND)
    ids = code_ids.reshape(chunks, 1, CHUNK)
    point_weight, point_first, point_second = point_weight.T, point_first.T, point_second.T
    dma = pltpu.SemaphoreType.DMA
    ub, ig, grads, quant, decoder = pl.pallas_call(
        functools.partial(block_kernel, rows),
        out_shape=(
            jax.ShapeDtypeStruct((pixels, 128), BF16),
            jax.ShapeDtypeStruct((pixels, channels), BF16),
            jax.ShapeDtypeStruct((10, 16, 128), F32),
            jax.ShapeDtypeStruct((24, 128), F32),
            jax.ShapeDtypeStruct((channels, 128), BF16),
        ),
        in_specs=[anywhere()] * 9,
        out_specs=(anywhere(), anywhere(), vmem(), vmem(), vmem()),
        scratch_shapes=[
            pltpu.VMEM(ids.shape, jnp.int32),
            pltpu.VMEM(mask.shape, jnp.int32),
            *[pltpu.VMEM(block.shape, F32) for block in (conv_weight, point_weight, proj_weight, code_book, dec_weight)],
            pltpu.VMEM((pixels, channels), BF16),
            pltpu.VMEM((2, PITCH, channels), BF16),
            pltpu.VMEM((pixels, channels), BF16),
            pltpu.VMEM((padded, 3 * channels), BF16),
            pltpu.VMEM((BANDS, BAND, 128), F32),
            pltpu.VMEM((pixels, 128), F32),
            pltpu.VMEM((pixels, 128), BF16),
            pltpu.VMEM((padded, channels), BF16),
            pltpu.VMEM((channels, pixels), BF16),
            pltpu.VMEM((pixels, channels), BF16),
            pltpu.VMEM((3, 2, 2, 2, 4, 3, 16, 128), BF16),
            pltpu.VMEM((2, 2, 2, 4, 16, 128), BF16),
            pltpu.VMEM((2, 2, 2, 4, 16, 128), BF16),
            pltpu.VMEM((3, 3 * channels, channels), BF16),
            pltpu.VMEM((3, channels, 3 * channels), BF16),
            pltpu.VMEM((channels, channels), BF16),
            pltpu.VMEM((channels, channels), BF16),
            pltpu.VMEM((channels, 128), F32),
            pltpu.VMEM((entries, 128), F32),
            pltpu.VMEM((channels, 128), BF16),
            pltpu.VMEM((channels, 128), BF16),
            pltpu.VMEM((128, channels), BF16),
            pltpu.VMEM((128, entries), BF16),
            pltpu.VMEM((channels, 128), F32),
            pltpu.VMEM((channels, 128), F32),
            pltpu.VMEM((channels, channels), F32),
            pltpu.VMEM((entries, 128), F32),
            pltpu.VMEM((8, 128), F32),
            pltpu.VMEM((2, 2, 2, 4, 32, 128), F32),
            pltpu.VMEM((2, 2, 2, 4, 8, 128), F32),
            pltpu.VMEM((3, 2, 2, 2, 4, 48, 128), F32),
            pltpu.VMEM((2, 2, 4, 32, 128), F32),
            pltpu.VMEM((3, 4, 32, 128), F32),
            pltpu.VMEM((3, 32, 128), F32),
            pltpu.VMEM((2, 2, 4, 8, 128), F32),
            pltpu.VMEM((3, 4, 8, 128), F32),
            pltpu.VMEM((3, 8, 128), F32),
            pltpu.VMEM((3, 2, 2, 4, 48, 128), F32),
            pltpu.VMEM((3, 3, 4, 48, 128), F32),
            pltpu.VMEM((3, 3, 48, 128), F32),
            dma((7,)),
            dma((chunks,)),
            dma((chunks,)),
            dma((rows // BACK_ROWS,)),
            dma(()),
            dma((4,)),
            dma((4,)),
            dma((16,)),
            dma((16,)),
            dma((5, 8)),
            dma((5, 8)),
            dma((5, 8)),
            dma((5, 8)),
        ],
        compiler_params=pltpu.CompilerParams(
            collective_id=0, has_side_effects=True, vmem_limit_bytes=62 * 2**20
        ),
        name="block",
    )(
        inputs, cotangent, ids, mask,
        conv_weight, point_weight, proj_weight, code_book, dec_weight,
    )

    states = (
        conv_weight, conv_first, conv_second, point_weight, point_first, point_second,
        proj_weight, proj_first, proj_second, code_book, code_first, code_second,
        dec_weight, dec_first, dec_second,
    )
    updates = []
    for n in range(5):
        shape = states[3 * n].shape
        updates += [jax.ShapeDtypeStruct(shape, kind) for kind in (F32, F32, F32, BF16)]
    smalls = (mask, decoder, grads, quant, *states)
    tile = CHUNK
    tiles = pixels // tile
    results = pl.pallas_call(
        functools.partial(finish_kernel, tile),
        out_shape=(
            jax.ShapeDtypeStruct(inputs.shape, BF16),
            jax.ShapeDtypeStruct(inputs.shape, BF16),
            jax.ShapeDtypeStruct((2,), F32),
            *updates,
        ),
        in_specs=[anywhere()] * (2 + len(smalls)),
        out_specs=(anywhere(), anywhere(), pl.BlockSpec(memory_space=pltpu.SMEM), *[anywhere() if n % 4 < 3 else vmem() for n in range(20)]),
        scratch_shapes=[
            pltpu.VMEM((pixels, 128), BF16),
            pltpu.VMEM((pixels, channels), BF16),
            pltpu.VMEM((pixels, channels), BF16),
            *[pltpu.VMEM(block.shape, block.dtype) for block in smalls],
            *[pltpu.VMEM(block.shape, F32) for n, block in enumerate(updates) if n % 4 < 3],
            dma((tiles,)),
            dma((tiles,)),
            dma((tiles,)),
            dma((tiles,)),
            dma((len(smalls),)),
            dma((15,)),
        ],
        compiler_params=pltpu.CompilerParams(vmem_limit_bytes=61 * 2**20),
        name="finish",
    )(ig, ub, *smalls)
    point_new = tuple(block.T for block in results[7:11])
    return (*results[:7], *point_new, *results[11:])


def row_stride():
    return BANDS * BAND


def tap_offsets():
    stride = row_stride()
    return [row_step * stride + col_step for row_step in (-1, 0, 1) for col_step in (-1, 0, 1)]


def conv_forward(padded, weights, row_count):
    margin = row_stride() + 1
    summed_terms = None
    for tap_index, offset in enumerate(tap_offsets()):
        begin = margin + offset
        window = lax.slice_in_dim(padded, begin, begin + row_count, axis=0)
        product = jnp.dot(window, weights[tap_index], preferred_element_type=jnp.float32)
        summed_terms = product if summed_terms is None else summed_terms + product
    return summed_terms


def conv_weight_grad(padded, grads, row_count):
    margin = row_stride() + 1
    products = []
    for offset in tap_offsets():
        begin = margin + offset
        window = lax.slice_in_dim(padded, begin, begin + row_count, axis=0)
        products.append(
            lax.dot_general(
                window, grads, (((0,), (0,)), ((), ())), preferred_element_type=jnp.float32
            )
        )
    return jnp.stack(products)


def conv_input_grad(padded_grads, weights, row_count):
    margin = row_stride() + 1
    summed_terms = None
    for tap_index, offset in enumerate(tap_offsets()):
        begin = margin - offset
        window = lax.slice_in_dim(padded_grads, begin, begin + row_count, axis=0)
        product = lax.dot_general(
            window, weights[tap_index], (((1,), (1,)), ((), ())), preferred_element_type=jnp.float32
        )
        summed_terms = product if summed_terms is None else summed_terms + product
    return summed_terms


def bottleneck(latent, mask_rows, code_rows, cotangent, codebook, decoder):
    weight_rows = mask_rows.astype(jnp.float32)[:, None]
    entries = jnp.arange(codebook.shape[0], dtype=jnp.int32)
    onehot = (code_rows[:, None] == entries[None, :]).astype(jnp.bfloat16)
    chosen = jnp.dot(onehot, codebook, preferred_element_type=jnp.float32)
    gap_rows = latent - chosen
    loss_part = jnp.sum(weight_rows * gap_rows * gap_rows)
    count_part = jnp.sum(weight_rows)
    decoded = chosen.astype(jnp.bfloat16)
    decoded_out = lax.dot_general(
        decoded, decoder, (((1,), (1,)), ((), ())), preferred_element_type=jnp.float32
    )
    output = (decoded_out * weight_rows).astype(jnp.bfloat16)
    kept_rows = cotangent * mask_rows.astype(jnp.bfloat16)[:, None]
    decoded_grad = jnp.dot(kept_rows, decoder, preferred_element_type=jnp.float32)
    latent_grad = (decoded_grad + 0.5 * weight_rows * gap_rows).astype(jnp.bfloat16)
    decoder_grad = lax.dot_general(
        kept_rows, decoded, (((0,), (0,)), ((), ())), preferred_element_type=jnp.float32
    )
    book_term = -2.0 * weight_rows * gap_rows
    high_part = book_term.astype(jnp.bfloat16)
    rest_term = book_term - high_part.astype(jnp.float32)
    middle_part = rest_term.astype(jnp.bfloat16)
    low_part = (rest_term - middle_part.astype(jnp.float32)).astype(jnp.bfloat16)
    stacked = jnp.concatenate([high_part, middle_part, low_part], axis=1)
    book_parts = lax.dot_general(
        onehot, stacked, (((0,), (0,)), ((), ())), preferred_element_type=jnp.float32
    )
    width = book_term.shape[1]
    book_grad = book_parts[:, :width] + (
        book_parts[:, width : 2 * width] + book_parts[:, 2 * width :]
    )
    return (output, latent_grad, decoder_grad, book_grad, loss_part, count_part)


def general(
    inputs,
    valid_mask,
    code_ids,
    cotangent,
    conv_weight,
    conv_first,
    conv_second,
    point_weight,
    point_first,
    point_second,
    proj_weight,
    proj_first,
    proj_second,
    code_book,
    code_first,
    code_second,
    dec_weight,
    dec_first,
    dec_second,
):
    chan_count = lax.axis_size("chan")
    chan_index = lax.axis_index("chan")
    rows_quarter = inputs.shape[0]
    rows_all = valid_mask.shape[0]
    channels = inputs.shape[1]
    chan_width = channels // chan_count
    margin = row_stride() + 1
    conv_low, point_low = (
        lax.all_gather(conv_weight.astype(jnp.bfloat16), "dp", axis=1, tiled=True),
        lax.all_gather(point_weight.astype(jnp.bfloat16), "dp", axis=1, tiled=True),
    )
    proj_full, book_full, dec_full = (
        lax.all_gather(proj_weight.astype(jnp.bfloat16), ("dp", "chan"), axis=0, tiled=True),
        lax.all_gather(code_book.astype(jnp.bfloat16), ("dp", "chan"), axis=0, tiled=True),
        lax.all_gather(dec_weight.astype(jnp.bfloat16), ("dp", "chan"), axis=0, tiled=True),
    )
    mask_rows = lax.dynamic_slice_in_dim(valid_mask, chan_index * rows_quarter, rows_quarter)
    first_column = chan_index * chan_width
    gathered = lax.all_gather(inputs, "chan", axis=0, tiled=True)
    valid_all = (valid_mask > 0)[:, None]
    activations = jnp.where(valid_all, jnp.maximum(gathered, 0), 0)
    padded = jnp.pad(activations, ((margin, margin), (0, 0)))
    hidden = conv_forward(padded, conv_low, rows_all)
    middle = jnp.maximum(hidden, 0.0).astype(jnp.bfloat16)
    partial_branch = jnp.dot(middle, point_low, preferred_element_type=jnp.float32)
    branch = lax.psum_scatter(partial_branch, "chan", scatter_dimension=1, tiled=True)
    own_inputs = lax.dynamic_slice_in_dim(gathered, first_column, chan_width, 1).astype(jnp.float32)
    summed = (own_inputs + branch).astype(jnp.bfloat16)
    proj_rows = lax.dynamic_slice_in_dim(proj_full, first_column, chan_width, 0)
    window = summed
    latent = lax.psum_scatter(
        jnp.dot(window, proj_rows, preferred_element_type=jnp.float32),
        "chan",
        scatter_dimension=0,
        tiled=True,
    )
    output, latent_grad, decoder_grad, book_grad, loss_part, count_part = bottleneck(
        latent, mask_rows, code_ids, cotangent, book_full, dec_full
    )
    grads_all = lax.all_gather(latent_grad, "chan", axis=0, tiled=True)
    proj_part = lax.dot_general(
        summed, grads_all, (((0,), (0,)), ((), ())), preferred_element_type=jnp.float32
    )
    proj_grad = lax.dynamic_update_slice_in_dim(
        jnp.zeros((channels, proj_part.shape[1]), jnp.float32), proj_part, first_column, 0
    )
    resid = lax.dot_general(
        grads_all, proj_rows, (((1,), (1,)), ((), ())), preferred_element_type=jnp.float32
    )
    resid_all = lax.all_gather(resid.astype(jnp.bfloat16), "chan", axis=1, tiled=True)
    point_grad = lax.dot_general(
        middle, resid_all, (((0,), (0,)), ((), ())), preferred_element_type=jnp.float32
    )
    hidden_back = lax.dot_general(
        resid_all, point_low, (((1,), (1,)), ((), ())), preferred_element_type=jnp.float32
    )
    hidden_grad = jnp.where(hidden > 0.0, hidden_back.astype(jnp.bfloat16), 0)
    conv_grad = conv_weight_grad(padded, hidden_grad, rows_all)
    grad_padded = jnp.pad(hidden_grad, ((margin, margin), (0, 0)))
    slopes = jnp.logical_and(gathered > 0, valid_all)
    window = grad_padded
    back_grad = conv_input_grad(window, conv_low, rows_quarter * lax.axis_size("chan"))
    back_grad = jnp.where(slopes, back_grad, 0.0)
    own_back = lax.dynamic_slice_in_dim(back_grad, first_column, chan_width, 1)
    input_grad = lax.psum_scatter(
        lax.dynamic_update_slice_in_dim(back_grad, own_back + resid, first_column, 1),
        "chan",
        scatter_dimension=0,
        tiled=True,
    ).astype(jnp.bfloat16)
    conv_reduced, point_reduced = (
        lax.psum_scatter(conv_grad, "dp", scatter_dimension=1, tiled=True),
        lax.psum_scatter(point_grad, "dp", scatter_dimension=1, tiled=True),
    )
    proj_reduced, book_reduced, dec_reduced = (
        lax.psum_scatter(proj_grad, ("dp", "chan"), scatter_dimension=0, tiled=True),
        lax.psum_scatter(book_grad, ("dp", "chan"), scatter_dimension=0, tiled=True),
        lax.psum_scatter(decoder_grad, ("dp", "chan"), scatter_dimension=0, tiled=True),
    )
    loss_total, count_total = lax.psum((loss_part, count_part), ("dp", "chan"))
    losses = jnp.stack([loss_total, 0.25 * loss_total]) / (count_total * LAT)
    conv_out = adamw(conv_reduced, conv_weight, conv_first, conv_second, 0.01)
    point_out = adamw(point_reduced, point_weight, point_first, point_second, 0.03)
    proj_out = adamw(proj_reduced, proj_weight, proj_first, proj_second, 0.03)
    code_out = adamw(book_reduced, code_book, code_first, code_second, 0.5)
    dec_out = adamw(dec_reduced, dec_weight, dec_first, dec_second, 0.06)
    return (
        output,
        input_grad,
        losses,
        conv_out[0],
        conv_out[1],
        conv_out[2],
        conv_out[3],
        point_out[0],
        point_out[1],
        point_out[2],
        point_out[3],
        proj_out[0],
        proj_out[1],
        proj_out[2],
        proj_out[3],
        code_out[0],
        code_out[1],
        code_out[2],
        code_out[3],
        dec_out[0],
        dec_out[1],
        dec_out[2],
        dec_out[3],
    )


def solution(mesh):
    pixel = P(("dp", "chan"), None)
    conv, point = P(None, "dp", "chan"), P("chan", "dp")
    in_specs = (pixel, P("dp"), P(("dp", "chan")), pixel)
    in_specs += (conv,) * 3 + (point,) * 3 + (pixel,) * 9
    out_specs = (pixel, pixel, P()) + (conv,) * 4 + (point,) * 4 + (pixel,) * 12
    fits = mesh.shape["dp"] == 8 and mesh.shape["chan"] == 4
    body = on_device if fits else general
    return jax.shard_map(body, mesh=mesh, in_specs=in_specs, out_specs=out_specs, check_vma=False)
```
